32 devices in a mesh: rep: 2 (over y), tp: 4 (over x, core), cp: 4 (over z).
Axes of the slice: x: 2, y: 2, z: 4, core: 2. Of those that a mesh axis runs over, the one named last changes fastest.
Arguments:
- tokens: bfloat16 [2, 3072, 1280], P('rep', 'cp', 'tp'), may hold values from -6 to 6
- qkv_weight: float32 [1280, 3, 1280], P(('rep', 'cp'), None, 'tp'), may hold values from -0.3 to 0.3
- out_weight: float32 [1280, 1280], P('tp', ('rep', 'cp')), may hold values from -0.3 to 0.3
- gate_up_weight: float32 [1280, 2, 5120], P(('rep', 'cp'), None, 'tp'), may hold values from -0.3 to 0.3
- down_weight: float32 [5120, 1280], P('tp', ('rep', 'cp')), may hold values from -0.15 to 0.15
- qk_scale: float32 [1280], P('tp'), may hold values from 0.9 to 6.6, as said below
- attn_rate: float32 [1280], replicated, may hold values from 0.05 to 0.6
- mlp_rate: float32 [1280], replicated, may hold values from 0.05 to 0.6
- up_scale: float32 [5120], P('tp'), may hold values from 0.5 to 2
- gate_scale: float32 [5120], P('tp'), may hold values from 0.5 to 2
- segment_ids: int32 [2, 3072], P('rep'), may hold values from 0 to 23, never falling along the last dimension, each value on 1 to 512 neighbouring positions
Outputs:
- next_state: bfloat16 [2, 3072, 1280], P('rep', 'cp', 'tp')
The draws below stay inside these ranges and needn't reach their ends.
Inputs may be any that keep to these rules, and one draw needn't show every extreme that they name: `segment_ids`: along each replica's row the ids never fall, and each prompt covers 1 to 512 positions; some prompt covers exactly 512. `qk_scale`: positive channel scales.
All inputs are finite; a program needn't handle non-finite values.
Results may differ from the reference program's by a relative error of at most 0.015.
Values may be sent and summed in bfloat16 or wider, within the bound.
A program may use at most 128 MiB of HBM per device.

```python
import math
import jax
import jax.numpy as jnp
import numpy as np
from jax import lax

D = 1280
H = 20
HD = 64
FF = 5120
MAXLEN = 512
N_REPLICAS = 2
STREAM = 3072
PROMPTS = 24


def level_line(count):
    return jnp.arange(count, dtype=jnp.float32) / max(count - 1, 1)


def drawn_ramp(count):
    return 0.5 + level_line(count)


def draw_qkv_weight(key, part):
    first, second, third = jax.random.split(jax.random.fold_in(key, 11), 3)
    ramp_rows = drawn_ramp(D)[:, None]
    query_part = 0.03 * jax.random.normal(first, (D, D), jnp.float32)
    key_part = 0.03 * jax.random.normal(second, (D, D), jnp.float32)
    value_part = 0.03 * jax.random.normal(third, (D, D), jnp.float32)
    stacked = jnp.stack([query_part * ramp_rows, key_part * ramp_rows, value_part * ramp_rows], axis=1)
    return jnp.clip(stacked, -0.3, 0.3)


def draw_out_weight(key, part):
    noise_key = jax.random.fold_in(key, 31)
    values = jax.random.normal(noise_key, (D, D), jnp.float32)
    ramp_cols = drawn_ramp(D)[None, :]
    return jnp.clip(values * ramp_cols / math.sqrt(D), -0.3, 0.3)


def draw_gate_up_weight(key, part):
    noise_key = jax.random.fold_in(key, 37)
    values = jax.random.normal(noise_key, (D, 2, FF), jnp.float32)
    ramp_rows = drawn_ramp(D)[:, None, None]
    return jnp.clip(values * ramp_rows / math.sqrt(D), -0.3, 0.3)


def draw_down_weight(key, part):
    noise_key = jax.random.fold_in(key, 41)
    values = jax.random.normal(noise_key, (FF, D), jnp.float32)
    ramp_cols = drawn_ramp(D)[None, :]
    return jnp.clip(values * ramp_cols / math.sqrt(FF), -0.15, 0.15)


def draw_qk_scale(key, part):
    first, second = jax.random.split(jax.random.fold_in(key, 23), 2)
    levels = jax.random.uniform(first, (H,), jnp.float32, 0.0, 1.0)
    head_level = jnp.exp(levels * math.log(2.5))
    gains = jax.random.uniform(second, (H, HD), jnp.float32, 0.9, 1.1)
    return (head_level[:, None] * gains).reshape(H * HD)


def block_scale(key, dims, cuts, smallest, largest):
    loudness, own = 1.0, jax.random.fold_in(key, 6)
    for dim, shards_of in cuts:
        steps = jnp.exp(jax.random.uniform(jax.random.fold_in(own, dim), (shards_of,), jnp.float32, smallest / len(cuts), largest / len(cuts)))
        loudness = loudness * jnp.repeat(steps, dims[dim] // shards_of).reshape([-1 if axis == dim else 1 for axis in range(len(dims))])
    return loudness


def length_profile(count, total, most, lean):
    loads = [(1 << 20) // math.isqrt(standing ** lean) + 1 for standing in range(2, count + 1)]
    rest, holding = total - most - (count - 1), [1] * (count - 1)
    while rest > 0:
        free = [i for i in range(count - 1) if holding[i] < most]
        mass, budget = sum([loads[i] for i in free]), rest
        for i in free:
            more = min(most - holding[i], max(1, budget * loads[i] // mass), rest)
            holding[i] = holding[i] + more
            rest = rest - more
    return np.array([most] + holding)


def ragged_sizes(own_key, number_of, total, most, lean):
    if number_of == 2:
        one = jax.random.randint(own_key, (), max(1, total - most), min(most, total - 1) + 1)
        return jnp.stack([one, total - one])
    lengths = jnp.asarray(length_profile(number_of, total, most, lean), jnp.int32)
    couples = (number_of - 1) // 2
    giver, taker = lengths[1:1 + 2 * couples:2], lengths[2:2 + 2 * couples:2]
    room = jnp.minimum(giver - 1, most - taker)
    passed = jax.random.randint(jax.random.fold_in(own_key, 1), (couples,), 0, 1 << 20) % (room + 1)
    lengths = lengths.at[1:1 + 2 * couples:2].set(giver - passed).at[2:2 + 2 * couples:2].set(taker + passed)
    return lengths[jax.random.permutation(jax.random.fold_in(own_key, 2), number_of)]


def scatter_about(own_key, shape, spread, most, cuts=(), held_as=jnp.bfloat16):
    factor_of = block_scale(own_key, shape, cuts, -0.22, 0.18) if cuts else 1.0
    result = jax.random.normal(own_key, shape, jnp.float32) * spread * factor_of
    return jnp.minimum(jnp.maximum(result, -most), most).astype(held_as)


def setup_inputs(seed: int = 0) -> dict:
    arg_keys = jax.random.split(jax.random.key(seed), 12)
    return {
        "tokens": scatter_about(arg_keys[0], (N_REPLICAS, STREAM, D), 1.0, 6.0, ((0, 2), (1, 4), (2, 4))),
        "qkv_weight": draw_qkv_weight(jax.random.fold_in(arg_keys[11], 71), 0),
        "out_weight": draw_out_weight(jax.random.fold_in(arg_keys[11], 71), 0),
        "gate_up_weight": draw_gate_up_weight(jax.random.fold_in(arg_keys[11], 71), 0),
        "down_weight": draw_down_weight(jax.random.fold_in(arg_keys[11], 71), 0),
        "qk_scale": draw_qk_scale(jax.random.fold_in(arg_keys[11], 71), 0),
        "attn_rate": jnp.clip(jnp.exp(jax.random.uniform(arg_keys[6], (D,), jnp.float32, math.log(0.05), math.log(0.6))), 0.05, 0.6),
        "mlp_rate": jnp.clip(jnp.exp(jax.random.uniform(arg_keys[7], (D,), jnp.float32, math.log(0.05), math.log(0.6))), 0.05, 0.6),
        "up_scale": jnp.clip(jnp.exp(math.log(2.0) - 1.3862944 * jax.random.uniform(arg_keys[8], (FF,), jnp.float32) ** block_scale(arg_keys[8], (FF,), ((0, 4),), -0.2, 0.2)), 0.5, 2.0),
        "gate_scale": jnp.clip(jnp.exp(math.log(2.0) - 1.3862944 * jax.random.uniform(arg_keys[9], (FF,), jnp.float32) ** block_scale(arg_keys[9], (FF,), ((0, 4),), -0.2, 0.2)), 0.5, 2.0),
        "segment_ids": jax.vmap(lambda own: jnp.searchsorted(jnp.cumsum(ragged_sizes(own, PROMPTS, STREAM, MAXLEN, 2)), jnp.arange(STREAM), side="right"))(jax.random.split(arg_keys[10], N_REPLICAS)).reshape((N_REPLICAS, STREAM)).astype(jnp.int32),
    }


def unit_rows(array):
    return array * lax.rsqrt(lax.optimization_barrier(jnp.sum(array * array, axis=-1, keepdims=True)) + 1e-06)

def rotate(array, position):
    half_dim = array.shape[-1] // 2
    frequency = jnp.exp(-math.log(10000.0) * jnp.arange(half_dim, dtype=jnp.float32) * 2.0 / array.shape[-1])
    angles = position.astype(jnp.float32)[:, None] * frequency[None, :]
    cosine = jnp.cos(angles)[:, None, :]
    sine_part = jnp.sin(angles)[:, None, :]
    first_half = array[..., :half_dim]
    second_half = array[..., half_dim:]
    return jnp.concatenate([first_half * cosine - second_half * sine_part, first_half * sine_part + second_half * cosine], axis=-1)

def stream_positions(segment):
    order_index = jnp.arange(segment.shape[0], dtype=jnp.int32)
    earlier = jnp.concatenate([segment[:1], segment[:-1]])
    boundary = jnp.where(segment != earlier, order_index, jnp.zeros_like(order_index))
    return order_index - lax.cummax(boundary)

def reference(tokens, qkv_weight, out_weight, gate_up_weight, down_weight, qk_scale, attn_rate, mlp_rate, up_scale, gate_scale, segment_ids):
    qkv_norm = (qkv_weight * lax.rsqrt(lax.optimization_barrier(jnp.sum(qkv_weight * qkv_weight, axis=0, keepdims=True)) + 1e-06)).astype(jnp.bfloat16).reshape(D, 3 * D)
    out_norm = (out_weight * lax.rsqrt(lax.optimization_barrier(jnp.sum(out_weight * out_weight, axis=1, keepdims=True)) + 1e-06)).astype(jnp.bfloat16)
    gate_up_norm = (gate_up_weight * lax.rsqrt(lax.optimization_barrier(jnp.sum(gate_up_weight * gate_up_weight, axis=0, keepdims=True)) + 1e-06)).astype(jnp.bfloat16).reshape(D, 2 * FF)
    down_norm = (down_weight * lax.rsqrt(lax.optimization_barrier(jnp.sum(down_weight * down_weight, axis=1, keepdims=True)) + 1e-06)).astype(jnp.bfloat16)
    scale_table = qk_scale.reshape(H, HD)

    def replica(inputs):
        stream_tokens, segment = inputs
        length = segment.shape[0]
        state = unit_rows(stream_tokens.astype(jnp.float32))
        projected = jnp.dot(state.astype(jnp.bfloat16), qkv_norm, preferred_element_type=jnp.float32).reshape(length, 3, H, HD)
        query = (scale_table * unit_rows(projected[:, 0])).astype(jnp.bfloat16)
        keys = (scale_table * unit_rows(projected[:, 1])).astype(jnp.bfloat16)
        values = projected[:, 2].astype(jnp.bfloat16)
        position = stream_positions(segment)
        query_rot = rotate(query.astype(jnp.float32), position).astype(jnp.bfloat16)
        keys_rot = rotate(keys.astype(jnp.float32), position).astype(jnp.bfloat16)
        order_index = jnp.arange(length, dtype=jnp.int32)
        allowed = (segment[:, None] == segment[None, :]) & (order_index[:, None] >= order_index[None, :])

        def one_head(head_inputs):
            head_query, head_keys, head_values = head_inputs
            scores = jnp.dot(head_query, head_keys.T, preferred_element_type=jnp.float32) * math.sqrt(HD)
            scores = jnp.where(allowed, scores, -1e+30)
            exponent = jnp.exp(scores - lax.optimization_barrier(jnp.max(scores, axis=-1, keepdims=True)))
            probs = (exponent / lax.optimization_barrier(jnp.sum(exponent, axis=-1, keepdims=True))).astype(jnp.bfloat16)
            return jnp.dot(probs, head_values, preferred_element_type=jnp.float32).astype(jnp.bfloat16)
        heads_out = lax.map(one_head, (query_rot.transpose(1, 0, 2), keys_rot.transpose(1, 0, 2), values.transpose(1, 0, 2)))
        attended = heads_out.transpose(1, 0, 2).reshape(length, D)
        attn_part = jnp.dot(attended, out_norm, preferred_element_type=jnp.float32)
        mixed = unit_rows(state + attn_rate * (unit_rows(attn_part) - state))
        gate_up = jnp.dot(mixed.astype(jnp.bfloat16), gate_up_norm, preferred_element_type=jnp.float32)
        up_branch = gate_up[:, :FF] * up_scale
        gate_branch = gate_up[:, FF:] * gate_scale * math.sqrt(D)
        inner = (up_branch * jax.nn.silu(gate_branch)).astype(jnp.bfloat16)
        mlp_part = jnp.dot(inner, down_norm, preferred_element_type=jnp.float32)
        return (math.sqrt(D) * unit_rows(mixed + mlp_rate * (unit_rows(mlp_part) - mixed))).astype(jnp.bfloat16)
    return lax.map(replica, (tokens, segment_ids))
```

```python
import math

import jax
import jax.numpy as jnp
from jax import lax
from jax.experimental import pallas as pl
from jax.experimental.pallas import tpu as pltpu
from jax.sharding import PartitionSpec as P

D = 1280
HD = 64


EPS = 1e-06


def shifted(block, axis, distance):
    devices = range(lax.axis_size(axis))
    route = [(i - distance, i) for i in devices if i - distance in devices]
    return lax.ppermute(block, axis, route)


def unit_rows(array):
    return array * lax.rsqrt(jnp.sum(array * array, axis=-1, keepdims=True) + EPS)


def share_unit(array):
    totals = lax.psum(jnp.sum(array * array, axis=-1), "tp")
    return array * lax.rsqrt(totals + EPS)[:, None]


def rotate(array, position):
    half_dim = array.shape[-1] // 2
    frequency = jnp.exp(
        -math.log(10000.0) * jnp.arange(half_dim, dtype=jnp.float32) * 2.0 / array.shape[-1]
    )
    angles = position.astype(jnp.float32)[:, None] * frequency[None, :]
    cosine = jnp.cos(angles)[:, None, :]
    sine_part = jnp.sin(angles)[:, None, :]
    first_half = array[..., :half_dim]
    second_half = array[..., half_dim:]
    return jnp.concatenate(
        [
            first_half * cosine - second_half * sine_part,
            first_half * sine_part + second_half * cosine,
        ],
        axis=-1,
    )


def stream_positions(segment):
    order_index = jnp.arange(segment.shape[0], dtype=jnp.int32)
    earlier = jnp.concatenate([segment[:1], segment[:-1]])
    boundary = jnp.where(segment != earlier, order_index, jnp.zeros_like(order_index))
    return order_index - lax.cummax(boundary)


def fold_rows(left, piece):
    return jnp.dot(left, piece.reshape(piece.shape[0], -1), preferred_element_type=jnp.float32)


def right_product(left, piece):
    return jnp.dot(left, piece, preferred_element_type=jnp.float32)


def plain_body(
    tokens,
    qkv_weight,
    out_weight,
    gate_up_weight,
    down_weight,
    qk_scale,
    attn_rate,
    mlp_rate,
    up_scale,
    gate_scale,
    segment_ids,
):
    rows = tokens.shape[1]
    local = tokens.shape[2]
    heads = local // HD
    hidden_local = gate_up_weight.shape[2]
    tp_index = lax.axis_index("tp")
    cp_index = lax.axis_index("cp")
    whole_tokens = lax.all_gather(tokens, "tp", axis=2, tiled=True)[0]
    state = unit_rows(whole_tokens.astype(jnp.float32))
    state_in = state.astype(jnp.bfloat16)
    sums = lax.psum(
        (
            jnp.sum(qkv_weight * qkv_weight, axis=0),
            jnp.sum(out_weight * out_weight, axis=1),
            jnp.sum(gate_up_weight * gate_up_weight, axis=0),
            jnp.sum(down_weight * down_weight, axis=1),
        ),
        ("rep", "cp"),
    )
    qkv_norm = (qkv_weight * lax.rsqrt(sums[0] + EPS)[None]).astype(jnp.bfloat16)
    out_norm = (out_weight * lax.rsqrt(sums[1] + EPS)[:, None]).astype(jnp.bfloat16)
    gate_up_norm = (gate_up_weight * lax.rsqrt(sums[2] + EPS)[None]).astype(jnp.bfloat16)
    down_norm = (down_weight * lax.rsqrt(sums[3] + EPS)[:, None]).astype(jnp.bfloat16)
    projected = fold_rows(state_in, lax.all_gather(qkv_norm, ("rep", "cp"), axis=0, tiled=True))
    projected = projected.reshape(rows, 3, heads, HD)
    scale_table = qk_scale.reshape(heads, HD)
    query = (scale_table * unit_rows(projected[:, 0])).astype(jnp.bfloat16)
    keys = (scale_table * unit_rows(projected[:, 1])).astype(jnp.bfloat16)
    values = projected[:, 2].astype(jnp.bfloat16)
    prev_keys, prev_values = shifted((keys, values), "cp", 1)
    segment = segment_ids[0]
    position = stream_positions(segment)
    own_start = cp_index * rows
    prev_start = jnp.maximum(own_start - rows, 0)
    own_pos = lax.dynamic_slice_in_dim(position, own_start, rows)
    prev_pos = lax.dynamic_slice_in_dim(position, prev_start, rows)
    own_seg = lax.dynamic_slice_in_dim(segment, own_start, rows)
    prev_seg = lax.dynamic_slice_in_dim(segment, prev_start, rows)
    query_rot = rotate(query.astype(jnp.float32), own_pos).astype(jnp.bfloat16)
    keys_rot = jnp.concatenate(
        [
            rotate(prev_keys.astype(jnp.float32), prev_pos),
            rotate(keys.astype(jnp.float32), own_pos),
        ],
        axis=0,
    ).astype(jnp.bfloat16)
    key_values = jnp.concatenate([prev_values, values], axis=0)
    key_seg = jnp.concatenate([prev_seg, own_seg])
    key_order = jnp.arange(2 * rows, dtype=jnp.int32)
    query_order = jnp.arange(rows, dtype=jnp.int32) + rows
    allowed = (
        (own_seg[:, None] == key_seg[None, :])
        & (query_order[:, None] >= key_order[None, :])
        & ((key_order[None, :] >= rows) | (cp_index > 0))
    )
    scores = jnp.einsum(
        "qhd,khd->hqk", query_rot, keys_rot, preferred_element_type=jnp.float32
    ) * math.sqrt(HD)
    scores = jnp.where(allowed[None], scores, -1e30)
    exponent = jnp.exp(scores - jnp.max(scores, axis=-1, keepdims=True))
    probs = (exponent / jnp.sum(exponent, axis=-1, keepdims=True)).astype(jnp.bfloat16)
    attended = (
        jnp.einsum("hqk,khd->qhd", probs, key_values, preferred_element_type=jnp.float32)
        .astype(jnp.bfloat16)
        .reshape(rows, local)
    )
    attn_part = right_product(attended, lax.all_gather(out_norm, ("rep", "cp"), axis=1, tiled=True))
    attn_block = lax.psum_scatter(attn_part, "tp", scatter_dimension=1, tiled=True)
    state_block = lax.dynamic_slice_in_dim(state, tp_index * local, local, 1)
    rate_block = lax.dynamic_slice_in_dim(attn_rate, tp_index * local, local, 0)
    mixed = share_unit(state_block + rate_block * (share_unit(attn_block) - state_block))
    mixed_in = lax.all_gather(mixed.astype(jnp.bfloat16), "tp", axis=1, tiled=True)
    gate_up = fold_rows(mixed_in, lax.all_gather(gate_up_norm, ("rep", "cp"), axis=0, tiled=True))
    up_branch = gate_up[:, :hidden_local] * up_scale
    gate_branch = gate_up[:, hidden_local:] * gate_scale * math.sqrt(D)
    inner = (up_branch * jax.nn.silu(gate_branch)).astype(jnp.bfloat16)
    mlp_part = right_product(inner, lax.all_gather(down_norm, ("rep", "cp"), axis=1, tiled=True))
    mlp_block = lax.psum_scatter(mlp_part, "tp", scatter_dimension=1, tiled=True)
    mlp_rate_block = lax.dynamic_slice_in_dim(mlp_rate, tp_index * local, local, 0)
    result = math.sqrt(D) * share_unit(mixed + mlp_rate_block * (share_unit(mlp_block) - mixed))
    return result.astype(jnp.bfloat16)[None]

MESH = pl.DeviceIdType.MESH
PARTS = 5
BACK = 512
NT = (((1,), (1,)), ((), ()))


def column_scale(block_ref, shards):
    def add(i, total):
        piece = block_ref[i].astype(jnp.float32)
        return total + jnp.sum(piece * piece, axis=0, keepdims=True)

    zero = jnp.zeros((1, block_ref.shape[-1]), jnp.float32)
    return lax.rsqrt(lax.fori_loop(0, shards, add, zero) + EPS)


def fused_kernel(
    reps, tps, cps,
    tok_ref, wa_ref, wb_ref, cos_ref, sin_ref, start_ref, qks_ref, arate_ref, mrate_ref, ups_ref, gates_ref,
    out_ref,
    tok, xt, wa, wb, wo, csa, q_s, kv, sbuf, rbuf, xm, mix, macc, sbuf2, rbuf2, obuf, fin,
    tok_send, tok_recv, w_send_z, w_send_y, w_recv, kv_send, kv_recv,
    a_send, a_recv, m_send, m_recv, b_send, b_recv, o_send, o_recv,
):
    r, t, c = lax.axis_index("rep"), lax.axis_index("tp"), lax.axis_index("cp")
    shards = reps * cps
    tile = xt.shape[1]
    width = xt.shape[2]
    local = tok.shape[2]
    heads = local // HD
    depth = wa.shape[1]
    hid = wb.shape[3] // 3
    mine = r * cps + c

    def tp_peer(d):
        return lax.rem(t + d, tps)

    def cp_peer(d):
        return lax.rem(c + d, cps)

    def rep_peer(d):
        return lax.rem(r + d, reps)

    barrier = pltpu.get_barrier_semaphore()
    for d in range(1, tps):
        pl.semaphore_signal(barrier, inc=1, device_id=(r, tp_peer(d), c), device_id_type=MESH)
    for d in range(1, cps):
        pl.semaphore_signal(barrier, inc=1, device_id=(r, t, cp_peer(d)), device_id_type=MESH)
    for d in range(1, reps):
        pl.semaphore_signal(barrier, inc=1, device_id=(rep_peer(d), t, c), device_id_type=MESH)
    pl.semaphore_wait(barrier, tps + cps + reps - 3)

    def remote(src, dst, send, recv, device):
        return pltpu.make_async_remote_copy(
            src_ref=src, dst_ref=dst, send_sem=send, recv_sem=recv, device_id=device, device_id_type=MESH
        )

    def slot(j, s):
        return wa.at[s] if j is None else wb.at[j, s]

    def own(j):
        return wa_ref if j is None else wb_ref.at[j]

    def row(j):
        return 0 if j is None else j + 1

    def z_copy(j, d):
        return remote(own(j), slot(j, mine), w_send_z.at[row(j), d], w_recv.at[row(j), mine], (r, t, cp_peer(d)))

    def y_copy(j, k, d):
        s = r * cps + cp_peer(k)
        source = own(j) if k == 0 else slot(j, s)
        return remote(source, slot(j, s), w_send_y.at[row(j), k, d], w_recv.at[row(j), s], (rep_peer(d), t, c))

    def arrive(j, s):
        remote(own(j), slot(j, s), w_send_z.at[row(j), 0], w_recv.at[row(j), s], (r, t, cp_peer(1))).wait_recv()

    def send_own(j):
        for d in range(1, reps):
            y_copy(j, 0, d).start()
        for d in range(1, cps):
            z_copy(j, d).start()

    def comm_step(j, k):
        arrive(j, r * cps + cp_peer(k))
        for d in range(1, reps):
            y_copy(j, k, d).start()

    def comm_part(j):
        @pl.when(j + 1 < PARTS)
        def _():
            send_own(j + 1)

        for k in range(1, cps):
            comm_step(j, k)

    def finish_part(j):
        for d in range(1, reps):
            for k in range(cps):
                arrive(j, rep_peer(d) * cps + cp_peer(k))

    def drain(j):
        for d in range(1, cps):
            z_copy(j, d).wait_send()
        for d in range(1, reps):
            for k in range(cps):
                y_copy(j, k, d).wait_send()

    def tok_copy(d):
        return remote(tok_ref, tok.at[t], tok_send.at[d], tok_recv.at[t], (r, tp_peer(d), c))

    for d in range(1, tps):
        tok_copy(d).start()
    send_own(None)
    tok[t] = tok_ref[...]
    wa[mine] = wa_ref[...]

    @pl.loop(0, PARTS)
    def _(j):
        wb[j, mine] = wb_ref[j]

    for d in range(1, tps):
        s = tp_peer(d)
        remote(tok_ref, tok.at[s], tok_send.at[d], tok_recv.at[s], (r, s, c)).wait_recv()
    send_own(0)
    for k in range(1, cps):
        comm_step(None, k)
    finish_part(None)
    csa[...] = column_scale(wa, shards)
    wo[...] = wa[:, :, 3 * local :].reshape(width, local)

    def project(i, carry):
        rows = pl.ds(pl.multiple_of(i * tile, 64), tile)
        x = jnp.concatenate([tok[s, rows, :] for s in range(tps)], axis=1)
        xt[i] = x
        xf = x.astype(jnp.float32)
        inv = lax.rsqrt(jnp.sum(xf * xf, axis=1, keepdims=True) + EPS)
        weights = wa[:, :, : 3 * local].reshape(width, 3 * local)
        pr = jnp.dot(x, weights, preferred_element_type=jnp.float32) * inv * csa[:, : 3 * local]
        cosine, sine = cos_ref[i], sin_ref[i]

        def rope(base, factor):
            pieces = []
            for h in range(heads):
                v = pr[:, base + HD * h : base + HD * (h + 1)]
                v = v * lax.rsqrt(jnp.sum(v * v, axis=1, keepdims=True) + EPS)
                v = v * (qks_ref[:, HD * h : HD * (h + 1)] * factor)
                swapped = jnp.concatenate([v[:, HD // 2 :], v[:, : HD // 2]], axis=1)
                pieces.append(v * cosine + swapped * sine)
            return jnp.concatenate(pieces, axis=1)

        q_s[i] = rope(0, math.sqrt(HD)).astype(jnp.bfloat16)
        kv[pl.ds(pl.multiple_of(BACK + i * tile, 64), tile), :] = jnp.concatenate(
            [rope(local, 1.0), pr[:, 2 * local :]], axis=1
        ).astype(jnp.bfloat16)
        return carry

    lax.fori_loop(0, tps, project, 0)

    rows_all = kv.shape[0]

    def kv_copy():
        return remote(
            kv.at[pl.ds(rows_all - BACK, BACK)], kv.at[pl.ds(0, BACK)], kv_send, kv_recv, (r, t, cp_peer(1))
        )

    @pl.when(c < cps - 1)
    def _():
        kv_copy().start()

    @pl.when(c == 0)
    def _():
        kv[pl.ds(0, BACK), :] = jnp.zeros((BACK, kv.shape[1]), kv.dtype)

    window = BACK + tile

    def part_copy(sent, got, p, send, recv):
        return remote(sent.at[p], got.at[t], send.at[p], recv.at[t], (r, p, c))

    def attend(step, carry):
        i = tps - 1 - step

        @pl.when((step == 1) & (c > 0))
        def _():
            kv_copy().wait_recv()

        first = pl.ds(pl.multiple_of(i * tile, 64), window)
        column = lax.broadcasted_iota(jnp.int32, (tile, window), 1)
        line = lax.broadcasted_iota(jnp.int32, (tile, window), 0) + BACK
        allowed = (column <= line) & (column >= start_ref[i] - i * tile)
        qt = q_s[i]
        outs = []
        for h in range(heads):
            keys = kv[first, HD * h : HD * (h + 1)]
            values = kv[first, local + HD * h : local + HD * (h + 1)]
            scores = lax.dot_general(
                qt[:, HD * h : HD * (h + 1)], keys, NT, preferred_element_type=jnp.float32
            )
            scores = jnp.where(allowed, scores, -1e30)
            exponent = jnp.exp(scores - jnp.max(scores, axis=1, keepdims=True))
            total = jnp.sum(exponent, axis=1, keepdims=True)
            got = jnp.dot(exponent.astype(jnp.bfloat16), values, preferred_element_type=jnp.float32)
            outs.append(got / total)
        att = (jnp.concatenate(outs, axis=1) * csa[:, 3 * local :]).astype(jnp.bfloat16)
        sbuf[i] = lax.dot_general(att, wo[...], NT, preferred_element_type=jnp.float32).astype(jnp.bfloat16)

        @pl.when(i != t)
        def _():
            part_copy(sbuf, rbuf, i, a_send, a_recv).start()

        @pl.when(i == t)
        def _():
            rbuf[t] = sbuf[t]

        @pl.when(step < 3)
        def _():
            comm_part(step)

        return carry

    lax.fori_loop(0, tps, attend, 0)

    def gather_parts(sent, got, send, recv):
        for d in range(1, tps):
            s = tp_peer(d)
            remote(sent.at[t], got.at[s], send.at[t], recv.at[s], (r, s, c)).wait_recv()
        total = got[0].astype(jnp.float32)
        for s in range(1, tps):
            total = total + got[s].astype(jnp.float32)
        return total

    def unit(v):
        return v * lax.rsqrt(jnp.sum(v * v, axis=1, keepdims=True) + EPS)

    attn = unit(gather_parts(sbuf, rbuf, a_send, a_recv))
    state = unit(xt[t].astype(jnp.float32))
    mixed = unit(state + arate_ref[...] * (attn - state))
    mix[...] = mixed
    xm[t] = mixed.astype(jnp.bfloat16)

    def mix_copy(d):
        return remote(xm.at[t], xm.at[t], m_send.at[d], m_recv.at[t], (r, tp_peer(d), c))

    for d in range(1, tps):
        mix_copy(d).start()
    comm_part(3)
    for d in range(1, tps):
        s = tp_peer(d)
        remote(xm.at[s], xm.at[s], m_send.at[d], m_recv.at[s], (r, s, c)).wait_recv()

    def feed(j, carry):
        finish_part(j)
        cs = column_scale(wb.at[j], shards)
        up_by = cs[:, :hid] * ups_ref[j]
        gate_by = cs[:, hid : 2 * hid] * gates_ref[j] * math.sqrt(width)
        down_by = cs[:, 2 * hid :]

        def one(step, inner_carry):
            p = tp_peer(step + 1)
            gu = jnp.dot(
                xm[p], wb[j, :, :, : 2 * hid].reshape(width, 2 * hid), preferred_element_type=jnp.float32
            )
            up = gu[:, :hid] * up_by
            gate = gu[:, hid:] * gate_by
            inner = (up * (gate / (1.0 + jnp.exp(-gate))) * down_by).astype(jnp.bfloat16)
            part = lax.dot_general(
                inner, wb[j, :, :, 2 * hid :].reshape(width, hid), NT, preferred_element_type=jnp.float32
            )

            @pl.when(j == 0)
            def _():
                macc[p] = part

            @pl.when((j > 0) & (j < PARTS - 1))
            def _():
                macc[p] = macc[p] + part

            @pl.when(j == PARTS - 1)
            def _():
                sbuf2[p] = (macc[p] + part).astype(jnp.bfloat16)

            @pl.when((j == PARTS - 1) & (p != t))
            def _():
                part_copy(sbuf2, rbuf2, p, b_send, b_recv).start()

            return inner_carry

        lax.fori_loop(0, tps, one, 0)

        @pl.when(j == 0)
        def _():
            comm_part(4)

        return carry

    lax.fori_loop(0, PARTS, feed, 0)
    rbuf2[t] = sbuf2[t]
    mlp = unit(gather_parts(sbuf2, rbuf2, b_send, b_recv))
    kept = mix[...]
    final = (math.sqrt(width) * unit(kept + mrate_ref[...] * (mlp - kept))).astype(jnp.bfloat16)
    for p in range(tps):
        obuf[p] = final[:, local * p : local * (p + 1)]

    def out_copy(p):
        return remote(obuf.at[p], fin.at[t], o_send.at[p], o_recv.at[t], (r, p, c))

    for d in range(1, tps):
        out_copy(tp_peer(d)).start()
    fin[t] = obuf[t]
    for d in range(1, tps):
        s = tp_peer(d)
        remote(obuf.at[t], fin.at[s], o_send.at[t], o_recv.at[s], (r, s, c)).wait_recv()
    for s in range(tps):
        out_ref[pl.ds(s * tile, tile), :] = fin[s]

    drain(None)

    @pl.loop(0, PARTS)
    def _(j):
        drain(j)

    for d in range(1, tps):
        p = tp_peer(d)
        tok_copy(d).wait_send()
        part_copy(sbuf, rbuf, p, a_send, a_recv).wait_send()
        mix_copy(d).wait_send()
        part_copy(sbuf2, rbuf2, p, b_send, b_recv).wait_send()
        out_copy(p).wait_send()

    @pl.when(c < cps - 1)
    def _():
        kv_copy().wait_send()


def fused_body(
    tokens, qkv_weight, out_weight, gate_up_weight, down_weight, qk_scale,
    attn_rate, mlp_rate, up_scale, gate_scale, segment_ids,
):
    reps, tps, cps = lax.axis_size("rep"), lax.axis_size("tp"), lax.axis_size("cp")
    rows, local = tokens.shape[1], tokens.shape[2]
    depth = qkv_weight.shape[0]
    hidden = gate_up_weight.shape[2]
    hid = hidden // PARTS
    shards = reps * cps
    width = depth * shards
    tile = rows // tps
    bf16 = jnp.bfloat16
    wa = jnp.concatenate(
        [qkv_weight.reshape(depth, 3 * local).astype(bf16), out_weight.astype(bf16).T], axis=1
    )
    gu = gate_up_weight.astype(bf16).reshape(depth, 2, PARTS, hid).transpose(2, 0, 1, 3)
    down = down_weight.astype(bf16).reshape(PARTS, hid, depth).transpose(0, 2, 1)
    wb = jnp.concatenate([gu.reshape(PARTS, depth, 2 * hid), down], axis=2)
    position = stream_positions(segment_ids[0])
    own_pos = lax.dynamic_slice_in_dim(position, lax.axis_index("cp") * rows, rows)
    half = HD // 2
    frequency = jnp.exp(-math.log(10000.0) * jnp.arange(half, dtype=jnp.float32) * 2.0 / HD)
    angles = own_pos.astype(jnp.float32)[:, None] * frequency[None, :]
    cosine, sine = jnp.cos(angles), jnp.sin(angles)
    cos_table = jnp.concatenate([cosine, cosine], axis=1).reshape(tps, tile, HD)
    sin_table = jnp.concatenate([-sine, sine], axis=1).reshape(tps, tile, HD)
    starts = (BACK + jnp.arange(rows, dtype=jnp.int32) - own_pos).reshape(tps, tile, 1)
    vmem = pl.BlockSpec(memory_space=pltpu.VMEM)
    dma = pltpu.SemaphoreType.DMA
    f32 = jnp.float32
    flops = 2 * rows * width * (4 * local + 3 * hidden) + 4 * rows * (BACK + tile) * local
    out = pl.pallas_call(
        lambda *refs: fused_kernel(reps, tps, cps, *refs),
        out_shape=jax.ShapeDtypeStruct((rows, local), bf16),
        in_specs=[vmem] * 11,
        out_specs=vmem,
        scratch_shapes=[
            pltpu.VMEM((tps, rows, local), bf16),
            pltpu.VMEM((tps, tile, width), bf16),
            pltpu.VMEM((shards, depth, 4 * local), bf16),
            pltpu.VMEM((PARTS, shards, depth, 3 * hid), bf16),
            pltpu.VMEM((width, local), bf16),
            pltpu.VMEM((1, 4 * local), f32),
            pltpu.VMEM((tps, tile, local), bf16),
            pltpu.VMEM((BACK + rows, 2 * local), bf16),
            pltpu.VMEM((tps, tile, width), bf16),
            pltpu.VMEM((tps, tile, width), bf16),
            pltpu.VMEM((tps, tile, width), bf16),
            pltpu.VMEM((tile, width), f32),
            pltpu.VMEM((tps, tile, width), f32),
            pltpu.VMEM((tps, tile, width), bf16),
            pltpu.VMEM((tps, tile, width), bf16),
            pltpu.VMEM((tps, tile, local), bf16),
            pltpu.VMEM((tps, tile, local), bf16),
            dma((tps,)), dma((tps,)),
            dma((PARTS + 1, cps)), dma((PARTS + 1, cps, reps)), dma((PARTS + 1, shards)),
            dma, dma,
            dma((tps,)), dma((tps,)), dma((tps,)), dma((tps,)),
            dma((tps,)), dma((tps,)), dma((tps,)), dma((tps,)),
        ],
        compiler_params=pltpu.CompilerParams(
            collective_id=0, has_side_effects=True, vmem_limit_bytes=58 * 1024 * 1024
        ),
        cost_estimate=pl.CostEstimate(flops=flops, bytes_accessed=2 * width * 5120, transcendentals=0),
    )(
        tokens[0], wa, wb, cos_table, sin_table, starts, qk_scale[None], attn_rate[None], mlp_rate[None],
        up_scale.reshape(PARTS, 1, hid), gate_scale.reshape(PARTS, 1, hid),
    )
    return out[None]


def body(*arrays):
    depth, tile = arrays[1].shape[0], arrays[0].shape[1] // lax.axis_size("tp")
    aligned = depth % 16 == 0 and tile % 64 == 0 and arrays[3].shape[2] % (128 * PARTS) == 0
    return fused_body(*arrays) if aligned else plain_body(*arrays)


def solution(mesh):
    in_specs = (
        P("rep", "cp", "tp"),
        P(("rep", "cp"), None, "tp"),
        P("tp", ("rep", "cp")),
        P(("rep", "cp"), None, "tp"),
        P("tp", ("rep", "cp")),
        P("tp"),
        P(),
        P(),
        P("tp"),
        P("tp"),
        P("rep", None),
    )
    out_specs = P("rep", "cp", "tp")
    return jax.shard_map(body, mesh=mesh, in_specs=in_specs, out_specs=out_specs, check_vma=False)
```

```python
import math

import jax
import jax.numpy as jnp
from jax import lax
from jax.experimental import pallas as pl
from jax.experimental.pallas import tpu as pltpu
from jax.sharding import PartitionSpec as P

D = 1280
HD = 64


EPS = 1e-06


def shifted(block, axis, distance):
    devices = range(lax.axis_size(axis))
    route = [(i - distance, i) for i in devices if i - distance in devices]
    return lax.ppermute(block, axis, route)


def unit_rows(array):
    return array * lax.rsqrt(jnp.sum(array * array, axis=-1, keepdims=True) + EPS)


def share_unit(array):
    totals = lax.psum(jnp.sum(array * array, axis=-1), "tp")
    return array * lax.rsqrt(totals + EPS)[:, None]


def rotate(array, position):
    half_dim = array.shape[-1] // 2
    frequency = jnp.exp(
        -math.log(10000.0) * jnp.arange(half_dim, dtype=jnp.float32) * 2.0 / array.shape[-1]
    )
    angles = position.astype(jnp.float32)[:, None] * frequency[None, :]
    cosine = jnp.cos(angles)[:, None, :]
    sine_part = jnp.sin(angles)[:, None, :]
    first_half = array[..., :half_dim]
    second_half = array[..., half_dim:]
    return jnp.concatenate(
        [
            first_half * cosine - second_half * sine_part,
            first_half * sine_part + second_half * cosine,
        ],
        axis=-1,
    )


def stream_positions(segment):
    order_index = jnp.arange(segment.shape[0], dtype=jnp.int32)
    earlier = jnp.concatenate([segment[:1], segment[:-1]])
    boundary = jnp.where(segment != earlier, order_index, jnp.zeros_like(order_index))
    return order_index - lax.cummax(boundary)


def fold_rows(left, piece):
    return jnp.dot(left, piece.reshape(piece.shape[0], -1), preferred_element_type=jnp.float32)


def right_product(left, piece):
    return jnp.dot(left, piece, preferred_element_type=jnp.float32)


def plain_body(
    tokens,
    qkv_weight,
    out_weight,
    gate_up_weight,
    down_weight,
    qk_scale,
    attn_rate,
    mlp_rate,
    up_scale,
    gate_scale,
    segment_ids,
):
    rows = tokens.shape[1]
    local = tokens.shape[2]
    heads = local // HD
    hidden_local = gate_up_weight.shape[2]
    tp_index = lax.axis_index("tp")
    cp_index = lax.axis_index("cp")
    whole_tokens = lax.all_gather(tokens, "tp", axis=2, tiled=True)[0]
    state = unit_rows(whole_tokens.astype(jnp.float32))
    state_in = state.astype(jnp.bfloat16)
    sums = lax.psum(
        (
            jnp.sum(qkv_weight * qkv_weight, axis=0),
            jnp.sum(out_weight * out_weight, axis=1),
            jnp.sum(gate_up_weight * gate_up_weight, axis=0),
            jnp.sum(down_weight * down_weight, axis=1),
        ),
        ("rep", "cp"),
    )
    qkv_norm = (qkv_weight * lax.rsqrt(sums[0] + EPS)[None]).astype(jnp.bfloat16)
    out_norm = (out_weight * lax.rsqrt(sums[1] + EPS)[:, None]).astype(jnp.bfloat16)
    gate_up_norm = (gate_up_weight * lax.rsqrt(sums[2] + EPS)[None]).astype(jnp.bfloat16)
    down_norm = (down_weight * lax.rsqrt(sums[3] + EPS)[:, None]).astype(jnp.bfloat16)
    projected = fold_rows(state_in, lax.all_gather(qkv_norm, ("rep", "cp"), axis=0, tiled=True))
    projected = projected.reshape(rows, 3, heads, HD)
    scale_table = qk_scale.reshape(heads, HD)
    query = (scale_table * unit_rows(projected[:, 0])).astype(jnp.bfloat16)
    keys = (scale_table * unit_rows(projected[:, 1])).astype(jnp.bfloat16)
    values = projected[:, 2].astype(jnp.bfloat16)
    prev_keys, prev_values = shifted((keys, values), "cp", 1)
    segment = segment_ids[0]
    position = stream_positions(segment)
    own_start = cp_index * rows
    prev_start = jnp.maximum(own_start - rows, 0)
    own_pos = lax.dynamic_slice_in_dim(position, own_start, rows)
    prev_pos = lax.dynamic_slice_in_dim(position, prev_start, rows)
    own_seg = lax.dynamic_slice_in_dim(segment, own_start, rows)
    prev_seg = lax.dynamic_slice_in_dim(segment, prev_start, rows)
    query_rot = rotate(query.astype(jnp.float32), own_pos).astype(jnp.bfloat16)
    keys_rot = jnp.concatenate(
        [
            rotate(prev_keys.astype(jnp.float32), prev_pos),
            rotate(keys.astype(jnp.float32), own_pos),
        ],
        axis=0,
    ).astype(jnp.bfloat16)
    key_values = jnp.concatenate([prev_values, values], axis=0)
    key_seg = jnp.concatenate([prev_seg, own_seg])
    key_order = jnp.arange(2 * rows, dtype=jnp.int32)
    query_order = jnp.arange(rows, dtype=jnp.int32) + rows
    allowed = (
        (own_seg[:, None] == key_seg[None, :])
        & (query_order[:, None] >= key_order[None, :])
        & ((key_order[None, :] >= rows) | (cp_index > 0))
    )
    scores = jnp.einsum(
        "qhd,khd->hqk", query_rot, keys_rot, preferred_element_type=jnp.float32
    ) * math.sqrt(HD)
    scores = jnp.where(allowed[None], scores, -1e30)
    exponent = jnp.exp(scores - jnp.max(scores, axis=-1, keepdims=True))
    probs = (exponent / jnp.sum(exponent, axis=-1, keepdims=True)).astype(jnp.bfloat16)
    attended = (
        jnp.einsum("hqk,khd->qhd", probs, key_values, preferred_element_type=jnp.float32)
        .astype(jnp.bfloat16)
        .reshape(rows, local)
    )
    attn_part = right_product(attended, lax.all_gather(out_norm, ("rep", "cp"), axis=1, tiled=True))
    attn_block = lax.psum_scatter(attn_part, "tp", scatter_dimension=1, tiled=True)
    state_block = lax.dynamic_slice_in_dim(state, tp_index * local, local, 1)
    rate_block = lax.dynamic_slice_in_dim(attn_rate, tp_index * local, local, 0)
    mixed = share_unit(state_block + rate_block * (share_unit(attn_block) - state_block))
    mixed_in = lax.all_gather(mixed.astype(jnp.bfloat16), "tp", axis=1, tiled=True)
    gate_up = fold_rows(mixed_in, lax.all_gather(gate_up_norm, ("rep", "cp"), axis=0, tiled=True))
    up_branch = gate_up[:, :hidden_local] * up_scale
    gate_branch = gate_up[:, hidden_local:] * gate_scale * math.sqrt(D)
    inner = (up_branch * jax.nn.silu(gate_branch)).astype(jnp.bfloat16)
    mlp_part = right_product(inner, lax.all_gather(down_norm, ("rep", "cp"), axis=1, tiled=True))
    mlp_block = lax.psum_scatter(mlp_part, "tp", scatter_dimension=1, tiled=True)
    mlp_rate_block = lax.dynamic_slice_in_dim(mlp_rate, tp_index * local, local, 0)
    result = math.sqrt(D) * share_unit(mixed + mlp_rate_block * (share_unit(mlp_block) - mixed))
    return result.astype(jnp.bfloat16)[None]

MESH = pl.DeviceIdType.MESH
PARTS = 5
BACK = 512
NT = (((1,), (1,)), ((), ()))


def column_scale(block_ref, shards):
    def add(i, total):
        piece = block_ref[i].astype(jnp.float32)
        return total + jnp.sum(piece * piece, axis=0, keepdims=True)

    zero = jnp.zeros((1, block_ref.shape[-1]), jnp.float32)
    return lax.rsqrt(lax.fori_loop(0, shards, add, zero) + EPS)


def fused_kernel(
    reps, tps, cps,
    tok_all, wa_ref, wb_ref, table_ref, vec_ref,
    out_all,
    tok, xt, wa, wb, wo, csa, q_s, kv, near, far, xm, mix, macc, kept_part, near2, far2, obuf, fin,
    tok_send, tok_recv, w_send_z, w_send_y, w_recv, kv_send, kv_recv,
    a_send, a_recv, m_send, m_recv, b_send, b_recv, o_send, o_recv,
):
    r, t, c = lax.axis_index("rep"), lax.axis_index("tp"), lax.axis_index("cp")
    shards = reps * cps
    tile = xt.shape[1]
    width = xt.shape[2]
    local = tok.shape[2]
    heads = local // HD
    depth = wa.shape[1]
    hid = wb.shape[3] // 3
    mine = r * cps + c
    hidden = PARTS * hid
    tok_ref, out_ref = tok_all.at[0], out_all.at[0]
    beside = t + 1 - 2 * lax.rem(t, 2)
    across = lax.rem(t + 2, tps)
    diagonal = lax.rem(beside + 2, tps)

    def tp_peer(d):
        return lax.rem(t + d, tps)

    def cp_peer(d):
        return lax.rem(c + d, cps)

    def rep_peer(d):
        return lax.rem(r + d, reps)

    barrier = pltpu.get_barrier_semaphore()
    for d in range(1, tps):
        pl.semaphore_signal(barrier, inc=1, device_id=(r, tp_peer(d), c), device_id_type=MESH)
    for d in range(1, cps):
        pl.semaphore_signal(barrier, inc=1, device_id=(r, t, cp_peer(d)), device_id_type=MESH)
    for d in range(1, reps):
        pl.semaphore_signal(barrier, inc=1, device_id=(rep_peer(d), t, c), device_id_type=MESH)
    pl.semaphore_wait(barrier, tps + cps + reps - 3)

    def remote(src, dst, send, recv, device):
        return pltpu.make_async_remote_copy(
            src_ref=src, dst_ref=dst, send_sem=send, recv_sem=recv, device_id=device, device_id_type=MESH
        )

    def slot(j, s):
        return wa.at[s] if j is None else wb.at[j, s]

    def own(j):
        return wa_ref if j is None else wb_ref.at[j]

    def row(j):
        return 0 if j is None else j + 1

    def z_copy(j, d):
        return remote(own(j), slot(j, mine), w_send_z.at[row(j), d], w_recv.at[row(j), mine], (r, t, cp_peer(d)))

    def y_copy(j, k, d):
        s = r * cps + cp_peer(k)
        source = own(j) if k == 0 else slot(j, s)
        return remote(source, slot(j, s), w_send_y.at[row(j), k, d], w_recv.at[row(j), s], (rep_peer(d), t, c))

    def arrive(j, s):
        remote(own(j), slot(j, s), w_send_z.at[row(j), 0], w_recv.at[row(j), s], (r, t, cp_peer(1))).wait_recv()

    def send_own(j):
        for d in range(1, reps):
            y_copy(j, 0, d).start()
        for d in range(1, cps):
            z_copy(j, d).start()

    def comm_step(j, k):
        arrive(j, r * cps + cp_peer(k))
        for d in range(1, reps):
            y_copy(j, k, d).start()

    def comm_part(j):
        @pl.when(j + 2 < PARTS)
        def _():
            send_own(j + 2)

        for k in range(1, cps):
            comm_step(j, k)

    def finish_part(j):
        for d in range(1, reps):
            for k in range(cps):
                arrive(j, rep_peer(d) * cps + cp_peer(k))

    def drain(j):
        for d in range(1, cps):
            z_copy(j, d).wait_send()
        for d in range(1, reps):
            for k in range(cps):
                y_copy(j, k, d).wait_send()

    def tok_copy(d):
        return remote(tok_ref, tok.at[t], tok_send.at[d], tok_recv.at[t], (r, tp_peer(d), c))

    for d in range(1, tps):
        tok_copy(d).start()
    send_own(None)
    tok[t] = tok_ref[...]
    wa[mine] = wa_ref[...]

    @pl.loop(0, PARTS)
    def _(j):
        wb[j, mine] = wb_ref[j]

    for d in range(1, tps):
        s = tp_peer(d)
        remote(tok_ref, tok.at[s], tok_send.at[d], tok_recv.at[s], (r, s, c)).wait_recv()
    for k in range(1, cps):
        comm_step(None, k)
    send_own(0)
    finish_part(None)
    send_own(1)
    csa[...] = column_scale(wa, shards)
    wo[...] = wa[:, :, 3 * local :].reshape(width, local)

    qks_at = 2 * width + 2 * hidden
    rows_all = kv.shape[0]

    def kv_copy():
        return remote(
            kv.at[pl.ds(rows_all - BACK, BACK)], kv.at[pl.ds(0, BACK)], kv_send, kv_recv, (r, t, cp_peer(1))
        )

    def project(step, carry):
        i = tps - 1 - step
        rows = pl.ds(pl.multiple_of(i * tile, 64), tile)
        x = jnp.concatenate([tok[s, rows, :] for s in range(tps)], axis=1)
        xt[i] = x
        xf = x.astype(jnp.float32)
        inv = lax.rsqrt(jnp.sum(xf * xf, axis=1, keepdims=True) + EPS)
        weights = wa[:, :, : 3 * local].reshape(width, 3 * local)
        pr = jnp.dot(x, weights, preferred_element_type=jnp.float32) * inv * csa[:, : 3 * local]
        cosine, sine = table_ref[i, :, :HD], table_ref[i, :, HD : 2 * HD]

        def rope(base, factor):
            pieces = []
            for h in range(heads):
                v = pr[:, base + HD * h : base + HD * (h + 1)]
                v = v * lax.rsqrt(jnp.sum(v * v, axis=1, keepdims=True) + EPS)
                v = v * (vec_ref[:, qks_at + HD * h : qks_at + HD * (h + 1)] * factor)
                swapped = jnp.concatenate([v[:, HD // 2 :], v[:, : HD // 2]], axis=1)
                pieces.append(v * cosine + swapped * sine)
            return jnp.concatenate(pieces, axis=1)

        q_s[i] = rope(0, math.sqrt(HD)).astype(jnp.bfloat16)
        kv[pl.ds(pl.multiple_of(BACK + i * tile, 64), tile), :] = jnp.concatenate(
            [rope(local, 1.0), pr[:, 2 * local :]], axis=1
        ).astype(jnp.bfloat16)

        @pl.when((step == (BACK - 1) // tile) & (c < cps - 1))
        def _():
            kv_copy().start()

        return carry

    @pl.when(c == 0)
    def _():
        kv[pl.ds(0, BACK), :] = jnp.zeros((BACK, kv.shape[1]), kv.dtype)

    lax.fori_loop(0, tps, project, 0)

    @pl.when(c > 0)
    def _():
        kv_copy().wait_recv()

    window = BACK + tile

    def near_copy(buf, k, send, recv):
        return remote(buf.at[k], buf.at[2 + k], send.at[k], recv.at[k], (r, beside, c))

    def far_copy(buf, send, recv):
        return remote(buf.at[0], buf.at[1], send.at[2], recv.at[2], (r, across, c))

    def scatter_step(step, part, kept, buf_near, buf_far, send, recv):
        @pl.when(step == 0)
        def _():
            buf_near[0] = part.astype(jnp.bfloat16)
            near_copy(buf_near, 0, send, recv).start()

        @pl.when(step == 1)
        def _():
            near_copy(buf_near, 0, send, recv).wait_recv()
            buf_far[0] = (part + buf_near[2].astype(jnp.float32)).astype(jnp.bfloat16)
            far_copy(buf_far, send, recv).start()

        @pl.when(step == 2)
        def _():
            buf_near[1] = part.astype(jnp.bfloat16)
            near_copy(buf_near, 1, send, recv).start()

        @pl.when(step == 3)
        def _():
            kept[...] = part

    def scatter_total(kept, buf_near, buf_far, send, recv):
        near_copy(buf_near, 1, send, recv).wait_recv()
        far_copy(buf_far, send, recv).wait_recv()
        return kept[...] + buf_near[3].astype(jnp.float32) + buf_far[1].astype(jnp.float32)

    def scatter_drain(buf_near, buf_far, send, recv):
        near_copy(buf_near, 0, send, recv).wait_send()
        near_copy(buf_near, 1, send, recv).wait_send()
        far_copy(buf_far, send, recv).wait_send()

    def target(step):
        late = jnp.where(step == 2, beside, t)
        return jnp.where(step == 0, diagonal, jnp.where(step == 1, across, late))

    def attend(step, carry):
        i = target(step)
        first = pl.ds(pl.multiple_of(i * tile, 64), window)
        column = lax.broadcasted_iota(jnp.int32, (tile, window), 1)
        line = lax.broadcasted_iota(jnp.int32, (tile, window), 0) + BACK
        allowed = (column <= line) & (column >= table_ref[i, :, 2 * HD : 2 * HD + 1].astype(jnp.int32) - i * tile)
        qt = q_s[i]
        outs = []
        for h in range(heads):
            keys = kv[first, HD * h : HD * (h + 1)]
            values = kv[first, local + HD * h : local + HD * (h + 1)]
            scores = lax.dot_general(
                qt[:, HD * h : HD * (h + 1)], keys, NT, preferred_element_type=jnp.float32
            )
            scores = jnp.where(allowed, scores, -1e30)
            exponent = jnp.exp(scores - jnp.max(scores, axis=1, keepdims=True))
            total = jnp.sum(exponent, axis=1, keepdims=True)
            got = jnp.dot(exponent.astype(jnp.bfloat16), values, preferred_element_type=jnp.float32)
            outs.append(got / total)
        att = (jnp.concatenate(outs, axis=1) * csa[:, 3 * local :]).astype(jnp.bfloat16)
        part = lax.dot_general(att, wo[...], NT, preferred_element_type=jnp.float32)
        scatter_step(step, part, mix, near, far, a_send, a_recv)

        @pl.when(lax.rem(step, 2) == 0)
        def _():
            comm_part(step // 2)

        return carry

    lax.fori_loop(0, tps, attend, 0)

    def unit(v):
        return v * lax.rsqrt(jnp.sum(v * v, axis=1, keepdims=True) + EPS)

    attn = unit(scatter_total(mix, near, far, a_send, a_recv))
    state = unit(xt[t].astype(jnp.float32))
    mixed = unit(state + vec_ref[:, :width] * (attn - state))
    mix[...] = mixed
    xm[t] = mixed.astype(jnp.bfloat16)

    def mix_copy(k, s, device):
        return remote(xm.at[s], xm.at[s], m_send.at[k], m_recv.at[s], (r, device, c))

    mix_copy(0, t, across).start()
    mix_copy(1, t, beside).start()
    macc[...] = jnp.zeros_like(macc)
    comm_part(2)
    mix_copy(0, across, across).wait_recv()
    mix_copy(2, across, beside).start()
    mix_copy(1, beside, beside).wait_recv()
    mix_copy(2, diagonal, beside).wait_recv()
    comm_part(3)

    def scales(j):
        cs = column_scale(wb.at[j], shards)
        mine_up = pl.ds(pl.multiple_of(2 * width + j * hid, 128), hid)
        mine_gate = pl.ds(pl.multiple_of(2 * width + hidden + j * hid, 128), hid)
        up_by = cs[:, :hid] * vec_ref[:, mine_up]
        gate_by = cs[:, hid : 2 * hid] * vec_ref[:, mine_gate] * math.sqrt(width)
        return up_by, gate_by, cs[:, 2 * hid :]

    def feed(x, j, by):
        gu = jnp.dot(x, wb[j, :, :, : 2 * hid].reshape(width, 2 * hid), preferred_element_type=jnp.float32)
        up = gu[:, :hid] * by[0]
        gate = gu[:, hid:] * by[1]
        inner = (up * (gate / (1.0 + jnp.exp(-gate))) * by[2]).astype(jnp.bfloat16)
        return lax.dot_general(
            inner, wb[j, :, :, 2 * hid :].reshape(width, hid), NT, preferred_element_type=jnp.float32
        )

    def feed_part(j, carry):
        finish_part(j)
        by = scales(j)

        def pair(i, inner_carry):
            both = pl.ds(2 * i, 2)
            part = feed(xm[both].reshape(2 * tile, width), j, by)
            macc[both] = macc[both] + part.reshape(2, tile, width)
            return inner_carry

        lax.fori_loop(0, tps // 2, pair, 0)

        @pl.when(j == 0)
        def _():
            comm_part(4)

        return carry

    lax.fori_loop(0, PARTS - 1, feed_part, 0)
    finish_part(PARTS - 1)
    last_by = scales(PARTS - 1)

    def feed_last(step, carry):
        p = target(step)
        part = macc[p] + feed(xm[p], PARTS - 1, last_by)
        scatter_step(step, part, kept_part, near2, far2, b_send, b_recv)
        return carry

    lax.fori_loop(0, tps, feed_last, 0)
    mlp = unit(scatter_total(kept_part, near2, far2, b_send, b_recv))
    kept = mix[...]
    final = (math.sqrt(width) * unit(kept + vec_ref[:, width : 2 * width] * (mlp - kept))).astype(jnp.bfloat16)
    for p in range(tps):
        obuf[p] = final[:, local * p : local * (p + 1)]

    def out_copy(p):
        return remote(obuf.at[p], fin.at[t], o_send.at[p], o_recv.at[t], (r, p, c))

    for d in range(1, tps):
        out_copy(tp_peer(d)).start()
    fin[t] = obuf[t]
    for d in range(1, tps):
        s = tp_peer(d)
        remote(obuf.at[t], fin.at[s], o_send.at[t], o_recv.at[s], (r, s, c)).wait_recv()
    for s in range(tps):
        out_ref[pl.ds(s * tile, tile), :] = fin[s]

    drain(None)

    @pl.loop(0, PARTS)
    def _(j):
        drain(j)

    for d in range(1, tps):
        p = tp_peer(d)
        tok_copy(d).wait_send()
        out_copy(p).wait_send()

    scatter_drain(near, far, a_send, a_recv)
    scatter_drain(near2, far2, b_send, b_recv)
    mix_copy(0, t, across).wait_send()
    mix_copy(1, t, beside).wait_send()
    mix_copy(2, across, beside).wait_send()

    @pl.when(c < cps - 1)
    def _():
        kv_copy().wait_send()


def fused_body(
    tokens, qkv_weight, out_weight, gate_up_weight, down_weight, qk_scale,
    attn_rate, mlp_rate, up_scale, gate_scale, segment_ids,
):
    reps, tps, cps = lax.axis_size("rep"), lax.axis_size("tp"), lax.axis_size("cp")
    rows, local = tokens.shape[1], tokens.shape[2]
    depth = qkv_weight.shape[0]
    hidden = gate_up_weight.shape[2]
    hid = hidden // PARTS
    shards = reps * cps
    width = depth * shards
    tile = rows // tps
    bf16 = jnp.bfloat16
    wa = jnp.concatenate(
        [qkv_weight.reshape(depth, 3 * local).astype(bf16), out_weight.astype(bf16).T], axis=1
    )
    gu = gate_up_weight.astype(bf16).reshape(depth, 2, PARTS, hid).transpose(2, 0, 1, 3)
    down = down_weight.astype(bf16).reshape(PARTS, hid, depth).transpose(0, 2, 1)
    wb = jnp.concatenate([gu.reshape(PARTS, depth, 2 * hid), down], axis=2)
    position = stream_positions(segment_ids[0])
    own_pos = lax.dynamic_slice_in_dim(position, lax.axis_index("cp") * rows, rows)
    half = HD // 2
    frequency = jnp.exp(-math.log(10000.0) * jnp.arange(half, dtype=jnp.float32) * 2.0 / HD)
    angles = own_pos.astype(jnp.float32)[:, None] * frequency[None, :]
    cosine, sine = jnp.cos(angles), jnp.sin(angles)
    first = (BACK + jnp.arange(rows, dtype=jnp.int32) - own_pos).astype(jnp.float32)[:, None]
    table = jnp.concatenate(
        [cosine, cosine, -sine, sine, jnp.broadcast_to(first, (rows, 2 * HD))], axis=1
    ).reshape(tps, tile, 4 * HD)
    vectors = jnp.concatenate([attn_rate, mlp_rate, up_scale, gate_scale, qk_scale])[None]
    vmem = pl.BlockSpec(memory_space=pltpu.VMEM)
    dma = pltpu.SemaphoreType.DMA
    f32 = jnp.float32
    flops = 2 * rows * width * (4 * local + 3 * hidden) + 4 * rows * (BACK + tile) * local
    out = pl.pallas_call(
        lambda *refs: fused_kernel(reps, tps, cps, *refs),
        out_shape=jax.ShapeDtypeStruct((1, rows, local), bf16),
        in_specs=[vmem] * 5,
        out_specs=vmem,
        scratch_shapes=[
            pltpu.VMEM((tps, rows, local), bf16),
            pltpu.VMEM((tps, tile, width), bf16),
            pltpu.VMEM((shards, depth, 4 * local), bf16),
            pltpu.VMEM((PARTS, shards, depth, 3 * hid), bf16),
            pltpu.VMEM((width, local), bf16),
            pltpu.VMEM((1, 4 * local), f32),
            pltpu.VMEM((tps, tile, local), bf16),
            pltpu.VMEM((BACK + rows, 2 * local), bf16),
            pltpu.VMEM((4, tile, width), bf16),
            pltpu.VMEM((2, tile, width), bf16),
            pltpu.VMEM((tps, tile, width), bf16),
            pltpu.VMEM((tile, width), f32),
            pltpu.VMEM((tps, tile, width), f32),
            pltpu.VMEM((tile, width), f32),
            pltpu.VMEM((4, tile, width), bf16),
            pltpu.VMEM((2, tile, width), bf16),
            pltpu.VMEM((tps, tile, local), bf16),
            pltpu.VMEM((tps, tile, local), bf16),
            dma((tps,)), dma((tps,)),
            dma((PARTS + 1, cps)), dma((PARTS + 1, cps, reps)), dma((PARTS + 1, shards)),
            dma, dma,
            dma((tps,)), dma((tps,)), dma((tps,)), dma((tps,)),
            dma((tps,)), dma((tps,)), dma((tps,)), dma((tps,)),
        ],
        compiler_params=pltpu.CompilerParams(
            collective_id=0, has_side_effects=True, vmem_limit_bytes=58 * 1024 * 1024
        ),
        cost_estimate=pl.CostEstimate(flops=flops, bytes_accessed=2 * width * 5120, transcendentals=0),
    )(
        tokens, wa, wb, table, vectors
    )
    return out


def body(*arrays):
    depth, tile = arrays[1].shape[0], arrays[0].shape[1] // lax.axis_size("tp")
    aligned = lax.axis_size("tp") == 4 and depth % 16 == 0 and tile % 64 == 0 and arrays[3].shape[2] % (128 * PARTS) == 0
    return fused_body(*arrays) if aligned else plain_body(*arrays)


def solution(mesh):
    in_specs = (
        P("rep", "cp", "tp"),
        P(("rep", "cp"), None, "tp"),
        P("tp", ("rep", "cp")),
        P(("rep", "cp"), None, "tp"),
        P("tp", ("rep", "cp")),
        P("tp"),
        P(),
        P(),
        P("tp"),
        P("tp"),
        P("rep", None),
    )
    out_specs = P("rep", "cp", "tp")
    return jax.shard_map(body, mesh=mesh, in_specs=in_specs, out_specs=out_specs, check_vma=False)
```

```python
import math

import jax
import jax.numpy as jnp
from jax import lax
from jax.experimental import pallas as pl
from jax.experimental.pallas import tpu as pltpu
from jax.sharding import PartitionSpec as P

D = 1280
HD = 64


EPS = 1e-06


def shifted(block, axis, distance):
    devices = range(lax.axis_size(axis))
    route = [(i - distance, i) for i in devices if i - distance in devices]
    return lax.ppermute(block, axis, route)


def unit_rows(array):
    return array * lax.rsqrt(jnp.sum(array * array, axis=-1, keepdims=True) + EPS)


def share_unit(array):
    totals = lax.psum(jnp.sum(array * array, axis=-1), "tp")
    return array * lax.rsqrt(totals + EPS)[:, None]


def rotate(array, position):
    half_dim = array.shape[-1] // 2
    frequency = jnp.exp(
        -math.log(10000.0) * jnp.arange(half_dim, dtype=jnp.float32) * 2.0 / array.shape[-1]
    )
    angles = position.astype(jnp.float32)[:, None] * frequency[None, :]
    cosine = jnp.cos(angles)[:, None, :]
    sine_part = jnp.sin(angles)[:, None, :]
    first_half = array[..., :half_dim]
    second_half = array[..., half_dim:]
    return jnp.concatenate(
        [
            first_half * cosine - second_half * sine_part,
            first_half * sine_part + second_half * cosine,
        ],
        axis=-1,
    )


def stream_positions(segment):
    order_index = jnp.arange(segment.shape[0], dtype=jnp.int32)
    earlier = jnp.concatenate([segment[:1], segment[:-1]])
    boundary = jnp.where(segment != earlier, order_index, jnp.zeros_like(order_index))
    return order_index - lax.cummax(boundary)


def fold_rows(left, piece):
    return jnp.dot(left, piece.reshape(piece.shape[0], -1), preferred_element_type=jnp.float32)


def right_product(left, piece):
    return jnp.dot(left, piece, preferred_element_type=jnp.float32)


def plain_body(
    tokens,
    qkv_weight,
    out_weight,
    gate_up_weight,
    down_weight,
    qk_scale,
    attn_rate,
    mlp_rate,
    up_scale,
    gate_scale,
    segment_ids,
):
    rows = tokens.shape[1]
    local = tokens.shape[2]
    heads = local // HD
    hidden_local = gate_up_weight.shape[2]
    tp_index = lax.axis_index("tp")
    cp_index = lax.axis_index("cp")
    whole_tokens = lax.all_gather(tokens, "tp", axis=2, tiled=True)[0]
    state = unit_rows(whole_tokens.astype(jnp.float32))
    state_in = state.astype(jnp.bfloat16)
    sums = lax.psum(
        (
            jnp.sum(qkv_weight * qkv_weight, axis=0),
            jnp.sum(out_weight * out_weight, axis=1),
            jnp.sum(gate_up_weight * gate_up_weight, axis=0),
            jnp.sum(down_weight * down_weight, axis=1),
        ),
        ("rep", "cp"),
    )
    qkv_norm = (qkv_weight * lax.rsqrt(sums[0] + EPS)[None]).astype(jnp.bfloat16)
    out_norm = (out_weight * lax.rsqrt(sums[1] + EPS)[:, None]).astype(jnp.bfloat16)
    gate_up_norm = (gate_up_weight * lax.rsqrt(sums[2] + EPS)[None]).astype(jnp.bfloat16)
    down_norm = (down_weight * lax.rsqrt(sums[3] + EPS)[:, None]).astype(jnp.bfloat16)
    projected = fold_rows(state_in, lax.all_gather(qkv_norm, ("rep", "cp"), axis=0, tiled=True))
    projected = projected.reshape(rows, 3, heads, HD)
    scale_table = qk_scale.reshape(heads, HD)
    query = (scale_table * unit_rows(projected[:, 0])).astype(jnp.bfloat16)
    keys = (scale_table * unit_rows(projected[:, 1])).astype(jnp.bfloat16)
    values = projected[:, 2].astype(jnp.bfloat16)
    prev_keys, prev_values = shifted((keys, values), "cp", 1)
    segment = segment_ids[0]
    position = stream_positions(segment)
    own_start = cp_index * rows
    prev_start = jnp.maximum(own_start - rows, 0)
    own_pos = lax.dynamic_slice_in_dim(position, own_start, rows)
    prev_pos = lax.dynamic_slice_in_dim(position, prev_start, rows)
    own_seg = lax.dynamic_slice_in_dim(segment, own_start, rows)
    prev_seg = lax.dynamic_slice_in_dim(segment, prev_start, rows)
    query_rot = rotate(query.astype(jnp.float32), own_pos).astype(jnp.bfloat16)
    keys_rot = jnp.concatenate(
        [
            rotate(prev_keys.astype(jnp.float32), prev_pos),
            rotate(keys.astype(jnp.float32), own_pos),
        ],
        axis=0,
    ).astype(jnp.bfloat16)
    key_values = jnp.concatenate([prev_values, values], axis=0)
    key_seg = jnp.concatenate([prev_seg, own_seg])
    key_order = jnp.arange(2 * rows, dtype=jnp.int32)
    query_order = jnp.arange(rows, dtype=jnp.int32) + rows
    allowed = (
        (own_seg[:, None] == key_seg[None, :])
        & (query_order[:, None] >= key_order[None, :])
        & ((key_order[None, :] >= rows) | (cp_index > 0))
    )
    scores = jnp.einsum(
        "qhd,khd->hqk", query_rot, keys_rot, preferred_element_type=jnp.float32
    ) * math.sqrt(HD)
    scores = jnp.where(allowed[None], scores, -1e30)
    exponent = jnp.exp(scores - jnp.max(scores, axis=-1, keepdims=True))
    probs = (exponent / jnp.sum(exponent, axis=-1, keepdims=True)).astype(jnp.bfloat16)
    attended = (
        jnp.einsum("hqk,khd->qhd", probs, key_values, preferred_element_type=jnp.float32)
        .astype(jnp.bfloat16)
        .reshape(rows, local)
    )
    attn_part = right_product(attended, lax.all_gather(out_norm, ("rep", "cp"), axis=1, tiled=True))
    attn_block = lax.psum_scatter(attn_part, "tp", scatter_dimension=1, tiled=True)
    state_block = lax.dynamic_slice_in_dim(state, tp_index * local, local, 1)
    rate_block = lax.dynamic_slice_in_dim(attn_rate, tp_index * local, local, 0)
    mixed = share_unit(state_block + rate_block * (share_unit(attn_block) - state_block))
    mixed_in = lax.all_gather(mixed.astype(jnp.bfloat16), "tp", axis=1, tiled=True)
    gate_up = fold_rows(mixed_in, lax.all_gather(gate_up_norm, ("rep", "cp"), axis=0, tiled=True))
    up_branch = gate_up[:, :hidden_local] * up_scale
    gate_branch = gate_up[:, hidden_local:] * gate_scale * math.sqrt(D)
    inner = (up_branch * jax.nn.silu(gate_branch)).astype(jnp.bfloat16)
    mlp_part = right_product(inner, lax.all_gather(down_norm, ("rep", "cp"), axis=1, tiled=True))
    mlp_block = lax.psum_scatter(mlp_part, "tp", scatter_dimension=1, tiled=True)
    mlp_rate_block = lax.dynamic_slice_in_dim(mlp_rate, tp_index * local, local, 0)
    result = math.sqrt(D) * share_unit(mixed + mlp_rate_block * (share_unit(mlp_block) - mixed))
    return result.astype(jnp.bfloat16)[None]

MESH = pl.DeviceIdType.MESH
PARTS = 5
BACK = 512
NT = (((1,), (1,)), ((), ()))


def column_scale(block_ref, shards):
    def add(i, total):
        piece = block_ref[i].astype(jnp.float32)
        return total + jnp.sum(piece * piece, axis=0, keepdims=True)

    zero = jnp.zeros((1, block_ref.shape[-1]), jnp.float32)
    return lax.rsqrt(lax.fori_loop(0, shards, add, zero) + EPS)


def fused_kernel(
    reps, tps, cps,
    tok_all, qkv_ref, outs_ref, gu_ref, down_ref, vec_ref,
    out_all,
    table_ref, tok, xt, wa, wb, wo, csa, q_s, kv, near, far, xm, mix, macc, kept_part, near2, far2, obuf, fin,
    tok_send, tok_recv, w_send_z, w_send_y, w_recv, kv_send, kv_recv,
    a_send, a_recv, m_send, m_recv, b_send, b_recv, o_send, o_recv,
):
    r, t, c = lax.axis_index("rep"), lax.axis_index("tp"), lax.axis_index("cp")
    shards = reps * cps
    tile = xt.shape[1]
    width = xt.shape[2]
    local = tok.shape[2]
    heads = local // HD
    depth = wa.shape[1]
    hid = wb.shape[3] // 3
    mine = r * cps + c
    hidden = PARTS * hid
    tok_ref, out_ref = tok_all.at[0], out_all.at[0]
    beside = t + 1 - 2 * lax.rem(t, 2)
    across = lax.rem(t + 2, tps)
    diagonal = lax.rem(beside + 2, tps)

    def tp_peer(d):
        return lax.rem(t + d, tps)

    def cp_peer(d):
        return lax.rem(c + d, cps)

    def rep_peer(d):
        return lax.rem(r + d, reps)

    barrier = pltpu.get_barrier_semaphore()
    for d in range(1, tps):
        pl.semaphore_signal(barrier, inc=1, device_id=(r, tp_peer(d), c), device_id_type=MESH)
    for d in range(1, cps):
        pl.semaphore_signal(barrier, inc=1, device_id=(r, t, cp_peer(d)), device_id_type=MESH)
    for d in range(1, reps):
        pl.semaphore_signal(barrier, inc=1, device_id=(rep_peer(d), t, c), device_id_type=MESH)
    pl.semaphore_wait(barrier, tps + cps + reps - 3)

    def remote(src, dst, send, recv, device):
        return pltpu.make_async_remote_copy(
            src_ref=src, dst_ref=dst, send_sem=send, recv_sem=recv, device_id=device, device_id_type=MESH
        )

    def slot(j, s):
        return wa.at[s] if j is None else wb.at[j, s]

    def near_cp(k):
        if k == 1:
            return c + 1 - 2 * lax.rem(c, 2)
        return jnp.where(c < 2, k, 3 - k)

    inner_cp = (c == 1) | (c == 2)

    def row(j):
        return 0 if j is None else j + 1

    def z_copy(j, k):
        part = slot(j, mine)
        return remote(part, part, w_send_z.at[row(j), k], w_recv.at[row(j), mine], (r, t, near_cp(k)))

    def z_relay(j):
        s = r * cps + near_cp(3)
        part = slot(j, s)
        return remote(part, part, w_send_z.at[row(j), 0], w_recv.at[row(j), s], (r, t, near_cp(1)))

    def y_copy(j, k, d):
        s = mine if k == 0 else r * cps + near_cp(k)
        part = slot(j, s)
        return remote(part, part, w_send_y.at[row(j), k, d], w_recv.at[row(j), s], (rep_peer(d), t, c))

    def arrive(j, s):
        part = slot(j, s)
        remote(part, part, w_send_z.at[row(j), 0], w_recv.at[row(j), s], (r, t, near_cp(1))).wait_recv()

    def send_own(j):
        for d in range(1, reps):
            y_copy(j, 0, d).start()
        z_copy(j, 1).start()
        z_copy(j, 2).start()

        @pl.when(inner_cp)
        def _():
            z_copy(j, 3).start()

    def comm_part(j):
        for k in range(1, cps):
            arrive(j, r * cps + near_cp(k))
            if k == 3:

                @pl.when(inner_cp)
                def _():
                    z_relay(j).start()

            for d in range(1, reps):
                y_copy(j, k, d).start()

    def finish_part(j):
        for d in range(1, reps):
            for k in range(cps):
                arrive(j, rep_peer(d) * cps + cp_peer(k))

    def drain(j):
        z_copy(j, 1).wait_send()
        z_copy(j, 2).wait_send()

        @pl.when(inner_cp)
        def _():
            z_copy(j, 3).wait_send()
            z_relay(j).wait_send()

        for d in range(1, reps):
            for k in range(cps):
                y_copy(j, k, d).wait_send()

    def tok_copy(d):
        return remote(tok_ref, tok.at[t], tok_send.at[d], tok_recv.at[t], (r, tp_peer(d), c))

    wa[mine, :, : 3 * local] = qkv_ref[...]
    wa[mine, :, 3 * local :] = outs_ref[...]
    send_own(None)
    for d in range(1, tps):
        tok_copy(d).start()
    tok[t] = tok_ref[...]
    for j in range(PARTS):
        wb[j, mine, :, :hid] = gu_ref[:, j * hid : (j + 1) * hid]
        wb[j, mine, :, hid : 2 * hid] = gu_ref[:, hidden + j * hid : hidden + (j + 1) * hid]
        wb[j, mine, :, 2 * hid :] = down_ref[:, j * hid : (j + 1) * hid]

    segments_at = 2 * width + 2 * hidden
    rates_at = segments_at + kv.shape[0]
    qks_at = rates_at + 2 * HD
    window = BACK + tile
    for i in range(tps):
        begin = segments_at + i * tile
        key_ids = vec_ref[:, begin : begin + window]
        square = (tile, tile)
        diagonal_only = lax.broadcasted_iota(jnp.int32, square, 0) == lax.broadcasted_iota(jnp.int32, square, 1)
        own_ids = jnp.sum(jnp.where(diagonal_only, key_ids[:, BACK:], 0.0), axis=1, keepdims=True)
        column = lax.broadcasted_iota(jnp.int32, (tile, window), 1)
        line = lax.broadcasted_iota(jnp.int32, (tile, window), 0) + BACK
        earlier = (key_ids == own_ids) & (column < line)
        position = jnp.sum(jnp.where(earlier, 1.0, 0.0), axis=1, keepdims=True)
        angles = position * vec_ref[:, rates_at : rates_at + HD]
        left = lax.broadcasted_iota(jnp.int32, (tile, HD), 1) < HD // 2
        sine = jnp.sin(angles)
        begins = lax.broadcasted_iota(jnp.int32, (tile, 2 * HD), 0).astype(jnp.float32) + BACK - position
        table_ref[i] = jnp.concatenate([jnp.cos(angles), jnp.where(left, -sine, sine), begins], axis=1)

    comm_part(None)
    send_own(0)
    for d in range(1, tps):
        s = tp_peer(d)
        remote(tok_ref, tok.at[s], tok_send.at[d], tok_recv.at[s], (r, s, c)).wait_recv()
    finish_part(None)
    csa[...] = column_scale(wa, shards)
    wo[...] = wa[:, :, 3 * local :].reshape(width, local)

    rows_all = kv.shape[0]

    def kv_copy():
        return remote(
            kv.at[pl.ds(rows_all - BACK, BACK)], kv.at[pl.ds(0, BACK)], kv_send, kv_recv, (r, t, cp_peer(1))
        )

    def project(step, carry):
        i = tps - 1 - step
        rows = pl.ds(pl.multiple_of(i * tile, 64), tile)
        x = jnp.concatenate([tok[s, rows, :] for s in range(tps)], axis=1)
        xt[i] = x
        xf = x.astype(jnp.float32)
        inv = lax.rsqrt(jnp.sum(xf * xf, axis=1, keepdims=True) + EPS)
        weights = wa[:, :, : 3 * local].reshape(width, 3 * local)
        pr = jnp.dot(x, weights, preferred_element_type=jnp.float32) * inv * csa[:, : 3 * local]
        cosine, sine = table_ref[i, :, :HD], table_ref[i, :, HD : 2 * HD]

        def rope(base, factor):
            pieces = []
            for h in range(heads):
                v = pr[:, base + HD * h : base + HD * (h + 1)]
                v = v * lax.rsqrt(jnp.sum(v * v, axis=1, keepdims=True) + EPS)
                v = v * (vec_ref[:, qks_at + HD * h : qks_at + HD * (h + 1)] * factor)
                swapped = jnp.concatenate([v[:, HD // 2 :], v[:, : HD // 2]], axis=1)
                pieces.append(v * cosine + swapped * sine)
            return jnp.concatenate(pieces, axis=1)

        q_s[i] = rope(0, math.sqrt(HD)).astype(jnp.bfloat16)
        kv[pl.ds(pl.multiple_of(BACK + i * tile, 64), tile), :] = jnp.concatenate(
            [rope(local, 1.0), pr[:, 2 * local :]], axis=1
        ).astype(jnp.bfloat16)

        @pl.when((step == (BACK - 1) // tile) & (c < cps - 1))
        def _():
            kv_copy().start()

        @pl.when(step == (BACK - 1) // tile)
        def _():
            comm_part(0)

        return carry

    @pl.when(c == 0)
    def _():
        kv[pl.ds(0, BACK), :] = jnp.zeros((BACK, kv.shape[1]), kv.dtype)

    lax.fori_loop(0, tps, project, 0)

    @pl.when(c > 0)
    def _():
        kv_copy().wait_recv()

    send_own(1)

    def near_copy(buf, k, send, recv):
        return remote(buf.at[k], buf.at[2 + k], send.at[k], recv.at[k], (r, beside, c))

    def far_copy(buf, send, recv):
        return remote(buf.at[0], buf.at[1], send.at[2], recv.at[2], (r, across, c))

    def scatter_step(step, part, kept, buf_near, buf_far, send, recv):
        @pl.when(step == 0)
        def _():
            buf_near[0] = part.astype(jnp.bfloat16)
            near_copy(buf_near, 0, send, recv).start()

        @pl.when(step == 1)
        def _():
            near_copy(buf_near, 0, send, recv).wait_recv()
            buf_far[0] = (part + buf_near[2].astype(jnp.float32)).astype(jnp.bfloat16)
            far_copy(buf_far, send, recv).start()

        @pl.when(step == 2)
        def _():
            buf_near[1] = part.astype(jnp.bfloat16)
            near_copy(buf_near, 1, send, recv).start()

        @pl.when(step == 3)
        def _():
            kept[...] = part

    def scatter_total(kept, buf_near, buf_far, send, recv):
        near_copy(buf_near, 1, send, recv).wait_recv()
        far_copy(buf_far, send, recv).wait_recv()
        return kept[...] + buf_near[3].astype(jnp.float32) + buf_far[1].astype(jnp.float32)

    def scatter_drain(buf_near, buf_far, send, recv):
        near_copy(buf_near, 0, send, recv).wait_send()
        near_copy(buf_near, 1, send, recv).wait_send()
        far_copy(buf_far, send, recv).wait_send()

    def target(step):
        late = jnp.where(step == 2, beside, t)
        return jnp.where(step == 0, diagonal, jnp.where(step == 1, across, late))

    def attend(step, carry):
        i = target(step)
        first = pl.ds(pl.multiple_of(i * tile, 64), window)
        column = lax.broadcasted_iota(jnp.int32, (tile, window), 1)
        line = lax.broadcasted_iota(jnp.int32, (tile, window), 0) + BACK
        allowed = (column <= line) & (column >= table_ref[i, :, 2 * HD : 2 * HD + 1].astype(jnp.int32))
        qt = q_s[i]
        outs = []
        for h in range(heads):
            keys = kv[first, HD * h : HD * (h + 1)]
            values = kv[first, local + HD * h : local + HD * (h + 1)]
            scores = lax.dot_general(
                qt[:, HD * h : HD * (h + 1)], keys, NT, preferred_element_type=jnp.float32
            )
            scores = jnp.where(allowed, scores, -1e30)
            exponent = jnp.exp(scores - jnp.max(scores, axis=1, keepdims=True))
            total = jnp.sum(exponent, axis=1, keepdims=True)
            got = jnp.dot(exponent.astype(jnp.bfloat16), values, preferred_element_type=jnp.float32)
            outs.append(got / total)
        att = (jnp.concatenate(outs, axis=1) * csa[:, 3 * local :]).astype(jnp.bfloat16)
        part = lax.dot_general(att, wo[...], NT, preferred_element_type=jnp.float32)
        scatter_step(step, part, mix, near, far, a_send, a_recv)

        @pl.when(lax.rem(step, 2) == 1)
        def _():
            comm_part(1 + step // 2)

        @pl.when(step < PARTS - 2)
        def _():
            send_own(step + 2)

        return carry

    lax.fori_loop(0, tps, attend, 0)

    def unit(v):
        return v * lax.rsqrt(jnp.sum(v * v, axis=1, keepdims=True) + EPS)

    attn = unit(scatter_total(mix, near, far, a_send, a_recv))
    state = unit(xt[t].astype(jnp.float32))
    mixed = unit(state + vec_ref[:, :width] * (attn - state))
    mix[...] = mixed
    xm[t] = mixed.astype(jnp.bfloat16)

    def mix_copy(k, s, device):
        return remote(xm.at[s], xm.at[s], m_send.at[k], m_recv.at[s], (r, device, c))

    mix_copy(0, t, across).start()
    mix_copy(1, t, beside).start()
    macc[...] = jnp.zeros_like(macc)
    mix_copy(0, across, across).wait_recv()
    mix_copy(2, across, beside).start()
    mix_copy(1, beside, beside).wait_recv()
    mix_copy(2, diagonal, beside).wait_recv()
    comm_part(3)

    def scales(j):
        cs = column_scale(wb.at[j], shards)
        mine_up = pl.ds(pl.multiple_of(2 * width + j * hid, 128), hid)
        mine_gate = pl.ds(pl.multiple_of(2 * width + hidden + j * hid, 128), hid)
        up_by = cs[:, :hid] * vec_ref[:, mine_up]
        gate_by = cs[:, hid : 2 * hid] * vec_ref[:, mine_gate] * math.sqrt(width)
        return up_by, gate_by, cs[:, 2 * hid :]

    def feed(x, j, by):
        gu = jnp.dot(x, wb[j, :, :, : 2 * hid].reshape(width, 2 * hid), preferred_element_type=jnp.float32)
        up = gu[:, :hid] * by[0]
        gate = gu[:, hid:] * by[1]
        inner = (up * (gate / (1.0 + jnp.exp(-gate))) * by[2]).astype(jnp.bfloat16)
        return lax.dot_general(
            inner, wb[j, :, :, 2 * hid :].reshape(width, hid), NT, preferred_element_type=jnp.float32
        )

    def feed_part(j, carry):
        finish_part(j)
        by = scales(j)

        def pair(i, inner_carry):
            both = pl.ds(2 * i, 2)
            part = feed(xm[both].reshape(2 * tile, width), j, by)
            macc[both] = macc[both] + part.reshape(2, tile, width)
            return inner_carry

        lax.fori_loop(0, tps // 2, pair, 0)

        @pl.when(j == 0)
        def _():
            comm_part(4)

        return carry

    lax.fori_loop(0, PARTS - 1, feed_part, 0)
    finish_part(PARTS - 1)
    last_by = scales(PARTS - 1)

    def feed_last(step, carry):
        p = target(step)
        part = macc[p] + feed(xm[p], PARTS - 1, last_by)
        scatter_step(step, part, kept_part, near2, far2, b_send, b_recv)
        return carry

    lax.fori_loop(0, tps, feed_last, 0)
    mlp = unit(scatter_total(kept_part, near2, far2, b_send, b_recv))
    kept = mix[...]
    final = (math.sqrt(width) * unit(kept + vec_ref[:, width : 2 * width] * (mlp - kept))).astype(jnp.bfloat16)
    for p in range(tps):
        obuf[p] = final[:, local * p : local * (p + 1)]

    def out_copy(p):
        return remote(obuf.at[p], fin.at[t], o_send.at[p], o_recv.at[t], (r, p, c))

    for d in range(1, tps):
        out_copy(tp_peer(d)).start()
    fin[t] = obuf[t]
    for d in range(1, tps):
        s = tp_peer(d)
        remote(obuf.at[t], fin.at[s], o_send.at[t], o_recv.at[s], (r, s, c)).wait_recv()
    for s in range(tps):
        out_ref[pl.ds(s * tile, tile), :] = fin[s]

    drain(None)

    @pl.loop(0, PARTS)
    def _(j):
        drain(j)

    for d in range(1, tps):
        p = tp_peer(d)
        tok_copy(d).wait_send()
        out_copy(p).wait_send()

    scatter_drain(near, far, a_send, a_recv)
    scatter_drain(near2, far2, b_send, b_recv)
    mix_copy(0, t, across).wait_send()
    mix_copy(1, t, beside).wait_send()
    mix_copy(2, across, beside).wait_send()

    @pl.when(c < cps - 1)
    def _():
        kv_copy().wait_send()


def fused_body(
    tokens, qkv_weight, out_weight, gate_up_weight, down_weight, qk_scale,
    attn_rate, mlp_rate, up_scale, gate_scale, segment_ids,
):
    reps, tps, cps = lax.axis_size("rep"), lax.axis_size("tp"), lax.axis_size("cp")
    rows, local = tokens.shape[1], tokens.shape[2]
    depth = qkv_weight.shape[0]
    hidden = gate_up_weight.shape[2]
    hid = hidden // PARTS
    shards = reps * cps
    width = depth * shards
    tile = rows // tps
    bf16 = jnp.bfloat16
    cp = lax.axis_index("cp")
    qkv = qkv_weight.reshape(depth, 3 * local).astype(bf16)
    gate_up = gate_up_weight.reshape(depth, 2 * hidden).astype(bf16)
    padded = jnp.concatenate([jnp.full((BACK,), -1.0, jnp.float32), segment_ids[0].astype(jnp.float32)])
    window = lax.dynamic_slice_in_dim(padded, cp * rows, BACK + rows)
    half = HD // 2
    frequency = jnp.exp(-math.log(10000.0) * jnp.arange(half, dtype=jnp.float32) * 2.0 / HD)
    vectors = jnp.concatenate(
        [attn_rate, mlp_rate, up_scale, gate_scale, window, frequency, frequency, frequency, frequency, qk_scale]
    )[None]
    vmem = pl.BlockSpec(memory_space=pltpu.VMEM)
    dma = pltpu.SemaphoreType.DMA
    f32 = jnp.float32
    flops = 2 * rows * width * (4 * local + 3 * hidden) + 4 * rows * (BACK + tile) * local
    out = pl.pallas_call(
        lambda *refs: fused_kernel(reps, tps, cps, *refs),
        out_shape=jax.ShapeDtypeStruct((1, rows, local), bf16),
        in_specs=[vmem] * 6,
        out_specs=vmem,
        scratch_shapes=[
            pltpu.VMEM((tps, tile, 4 * HD), f32),
            pltpu.VMEM((tps, rows, local), bf16),
            pltpu.VMEM((tps, tile, width), bf16),
            pltpu.VMEM((shards, depth, 4 * local), bf16),
            pltpu.VMEM((PARTS, shards, depth, 3 * hid), bf16),
            pltpu.VMEM((width, local), bf16),
            pltpu.VMEM((1, 4 * local), f32),
            pltpu.VMEM((tps, tile, local), bf16),
            pltpu.VMEM((BACK + rows, 2 * local), bf16),
            pltpu.VMEM((4, tile, width), bf16),
            pltpu.VMEM((2, tile, width), bf16),
            pltpu.VMEM((tps, tile, width), bf16),
            pltpu.VMEM((tile, width), f32),
            pltpu.VMEM((tps, tile, width), f32),
            pltpu.VMEM((tile, width), f32),
            pltpu.VMEM((4, tile, width), bf16),
            pltpu.VMEM((2, tile, width), bf16),
            pltpu.VMEM((tps, tile, local), bf16),
            pltpu.VMEM((tps, tile, local), bf16),
            dma((tps,)), dma((tps,)),
            dma((PARTS + 1, cps)), dma((PARTS + 1, cps, reps)), dma((PARTS + 1, shards)),
            dma, dma,
            dma((tps,)), dma((tps,)), dma((tps,)), dma((tps,)),
            dma((tps,)), dma((tps,)), dma((tps,)), dma((tps,)),
        ],
        compiler_params=pltpu.CompilerParams(
            collective_id=0, has_side_effects=True, vmem_limit_bytes=58 * 1024 * 1024
        ),
        cost_estimate=pl.CostEstimate(flops=flops, bytes_accessed=2 * width * 5120, transcendentals=0),
    )(
        tokens, qkv, out_weight.astype(bf16).T, gate_up, down_weight.astype(bf16).T, vectors
    )
    return out


def body(*arrays):
    depth, tile = arrays[1].shape[0], arrays[0].shape[1] // lax.axis_size("tp")
    aligned = lax.axis_size("tp") == 4 and lax.axis_size("cp") == 4 and depth % 16 == 0 and tile % 64 == 0 and arrays[3].shape[2] % (128 * PARTS) == 0
    return fused_body(*arrays) if aligned else plain_body(*arrays)


def solution(mesh):
    in_specs = (
        P("rep", "cp", "tp"),
        P(("rep", "cp"), None, "tp"),
        P("tp", ("rep", "cp")),
        P(("rep", "cp"), None, "tp"),
        P("tp", ("rep", "cp")),
        P("tp"),
        P(),
        P(),
        P("tp"),
        P("tp"),
        P("rep", None),
    )
    out_specs = P("rep", "cp", "tp")
    return jax.shard_map(body, mesh=mesh, in_specs=in_specs, out_specs=out_specs, check_vma=False)
```

```python
import functools
import math

import jax
import jax.numpy as jnp
from jax import lax
from jax.experimental import pallas as pl
from jax.experimental.pallas import tpu as pltpu
from jax.sharding import PartitionSpec as P

D = 1280
HD = 64


EPS = 1e-06


def shifted(block, axis, distance):
    devices = range(lax.axis_size(axis))
    route = [(i - distance, i) for i in devices if i - distance in devices]
    return lax.ppermute(block, axis, route)


def unit_rows(array):
    return array * lax.rsqrt(jnp.sum(array * array, axis=-1, keepdims=True) + EPS)


def share_unit(array):
    totals = lax.psum(jnp.sum(array * array, axis=-1), "tp")
    return array * lax.rsqrt(totals + EPS)[:, None]


def rotate(array, position):
    half_dim = array.shape[-1] // 2
    frequency = jnp.exp(
        -math.log(10000.0) * jnp.arange(half_dim, dtype=jnp.float32) * 2.0 / array.shape[-1]
    )
    angles = position.astype(jnp.float32)[:, None] * frequency[None, :]
    cosine = jnp.cos(angles)[:, None, :]
    sine_part = jnp.sin(angles)[:, None, :]
    first_half = array[..., :half_dim]
    second_half = array[..., half_dim:]
    return jnp.concatenate(
        [
            first_half * cosine - second_half * sine_part,
            first_half * sine_part + second_half * cosine,
        ],
        axis=-1,
    )


def stream_positions(segment):
    order_index = jnp.arange(segment.shape[0], dtype=jnp.int32)
    earlier = jnp.concatenate([segment[:1], segment[:-1]])
    boundary = jnp.where(segment != earlier, order_index, jnp.zeros_like(order_index))
    return order_index - lax.cummax(boundary)


def fold_rows(left, piece):
    return jnp.dot(left, piece.reshape(piece.shape[0], -1), preferred_element_type=jnp.float32)


def right_product(left, piece):
    return jnp.dot(left, piece, preferred_element_type=jnp.float32)


def plain_body(
    tokens,
    qkv_weight,
    out_weight,
    gate_up_weight,
    down_weight,
    qk_scale,
    attn_rate,
    mlp_rate,
    up_scale,
    gate_scale,
    segment_ids,
):
    rows = tokens.shape[1]
    local = tokens.shape[2]
    heads = local // HD
    hidden_local = gate_up_weight.shape[2]
    tp_index = lax.axis_index("tp")
    cp_index = lax.axis_index("cp")
    whole_tokens = lax.all_gather(tokens, "tp", axis=2, tiled=True)[0]
    state = unit_rows(whole_tokens.astype(jnp.float32))
    state_in = state.astype(jnp.bfloat16)
    sums = lax.psum(
        (
            jnp.sum(qkv_weight * qkv_weight, axis=0),
            jnp.sum(out_weight * out_weight, axis=1),
            jnp.sum(gate_up_weight * gate_up_weight, axis=0),
            jnp.sum(down_weight * down_weight, axis=1),
        ),
        ("rep", "cp"),
    )
    qkv_norm = (qkv_weight * lax.rsqrt(sums[0] + EPS)[None]).astype(jnp.bfloat16)
    out_norm = (out_weight * lax.rsqrt(sums[1] + EPS)[:, None]).astype(jnp.bfloat16)
    gate_up_norm = (gate_up_weight * lax.rsqrt(sums[2] + EPS)[None]).astype(jnp.bfloat16)
    down_norm = (down_weight * lax.rsqrt(sums[3] + EPS)[:, None]).astype(jnp.bfloat16)
    projected = fold_rows(state_in, lax.all_gather(qkv_norm, ("rep", "cp"), axis=0, tiled=True))
    projected = projected.reshape(rows, 3, heads, HD)
    scale_table = qk_scale.reshape(heads, HD)
    query = (scale_table * unit_rows(projected[:, 0])).astype(jnp.bfloat16)
    keys = (scale_table * unit_rows(projected[:, 1])).astype(jnp.bfloat16)
    values = projected[:, 2].astype(jnp.bfloat16)
    prev_keys, prev_values = shifted((keys, values), "cp", 1)
    segment = segment_ids[0]
    position = stream_positions(segment)
    own_start = cp_index * rows
    prev_start = jnp.maximum(own_start - rows, 0)
    own_pos = lax.dynamic_slice_in_dim(position, own_start, rows)
    prev_pos = lax.dynamic_slice_in_dim(position, prev_start, rows)
    own_seg = lax.dynamic_slice_in_dim(segment, own_start, rows)
    prev_seg = lax.dynamic_slice_in_dim(segment, prev_start, rows)
    query_rot = rotate(query.astype(jnp.float32), own_pos).astype(jnp.bfloat16)
    keys_rot = jnp.concatenate(
        [
            rotate(prev_keys.astype(jnp.float32), prev_pos),
            rotate(keys.astype(jnp.float32), own_pos),
        ],
        axis=0,
    ).astype(jnp.bfloat16)
    key_values = jnp.concatenate([prev_values, values], axis=0)
    key_seg = jnp.concatenate([prev_seg, own_seg])
    key_order = jnp.arange(2 * rows, dtype=jnp.int32)
    query_order = jnp.arange(rows, dtype=jnp.int32) + rows
    allowed = (
        (own_seg[:, None] == key_seg[None, :])
        & (query_order[:, None] >= key_order[None, :])
        & ((key_order[None, :] >= rows) | (cp_index > 0))
    )
    scores = jnp.einsum(
        "qhd,khd->hqk", query_rot, keys_rot, preferred_element_type=jnp.float32
    ) * math.sqrt(HD)
    scores = jnp.where(allowed[None], scores, -1e30)
    exponent = jnp.exp(scores - jnp.max(scores, axis=-1, keepdims=True))
    probs = (exponent / jnp.sum(exponent, axis=-1, keepdims=True)).astype(jnp.bfloat16)
    attended = (
        jnp.einsum("hqk,khd->qhd", probs, key_values, preferred_element_type=jnp.float32)
        .astype(jnp.bfloat16)
        .reshape(rows, local)
    )
    attn_part = right_product(attended, lax.all_gather(out_norm, ("rep", "cp"), axis=1, tiled=True))
    attn_block = lax.psum_scatter(attn_part, "tp", scatter_dimension=1, tiled=True)
    state_block = lax.dynamic_slice_in_dim(state, tp_index * local, local, 1)
    rate_block = lax.dynamic_slice_in_dim(attn_rate, tp_index * local, local, 0)
    mixed = share_unit(state_block + rate_block * (share_unit(attn_block) - state_block))
    mixed_in = lax.all_gather(mixed.astype(jnp.bfloat16), "tp", axis=1, tiled=True)
    gate_up = fold_rows(mixed_in, lax.all_gather(gate_up_norm, ("rep", "cp"), axis=0, tiled=True))
    up_branch = gate_up[:, :hidden_local] * up_scale
    gate_branch = gate_up[:, hidden_local:] * gate_scale * math.sqrt(D)
    inner = (up_branch * jax.nn.silu(gate_branch)).astype(jnp.bfloat16)
    mlp_part = right_product(inner, lax.all_gather(down_norm, ("rep", "cp"), axis=1, tiled=True))
    mlp_block = lax.psum_scatter(mlp_part, "tp", scatter_dimension=1, tiled=True)
    mlp_rate_block = lax.dynamic_slice_in_dim(mlp_rate, tp_index * local, local, 0)
    result = math.sqrt(D) * share_unit(mixed + mlp_rate_block * (share_unit(mlp_block) - mixed))
    return result.astype(jnp.bfloat16)[None]

MESH = pl.DeviceIdType.MESH
PARTS = 5
SWAPPED = (2, 4)
BACK = 512
NT = (((1,), (1,)), ((), ()))


def column_scale(block_ref, shards):
    def add(i, total):
        piece = block_ref[i].astype(jnp.float32)
        return total + jnp.sum(piece * piece, axis=0, keepdims=True)

    zero = jnp.zeros((1, block_ref.shape[-1]), jnp.float32)
    return lax.rsqrt(lax.fori_loop(0, shards, add, zero) + EPS)


def fused_kernel(
    reps, tps, cps,
    tok_all, qkv_ref, outs_ref, gu_ref, down_ref, vec_ref,
    out_all,
    table_ref, tok, xt, wa, wb, wo, csa, q_s, kv, near, far, xm, mix, macc, kept_part, near2, far2, obuf, fin,
    tok_send, tok_recv, w_send_z, w_send_y, w_recv, kv_send, kv_recv,
    a_send, a_recv, m_send, m_recv, b_send, b_recv, o_send, o_recv,
):
    r, t, c = lax.axis_index("rep"), lax.axis_index("tp"), lax.axis_index("cp")
    shards = reps * cps
    tile = xt.shape[1]
    width = xt.shape[2]
    local = tok.shape[2]
    heads = local // HD
    depth = wa.shape[1]
    hid = wb.shape[3] // 3
    mine = r * cps + c
    hidden = PARTS * hid
    tok_ref, out_ref = tok_all.at[0], out_all.at[0]
    beside = t + 1 - 2 * lax.rem(t, 2)
    across = lax.rem(t + 2, tps)
    diagonal = lax.rem(beside + 2, tps)

    def tp_peer(d):
        return lax.rem(t + d, tps)

    def cp_peer(d):
        return lax.rem(c + d, cps)

    def rep_peer(d):
        return lax.rem(r + d, reps)

    barrier = pltpu.get_barrier_semaphore()
    for d in range(1, tps):
        pl.semaphore_signal(barrier, inc=1, device_id=(r, tp_peer(d), c), device_id_type=MESH)
    for d in range(1, cps):
        pl.semaphore_signal(barrier, inc=1, device_id=(r, t, cp_peer(d)), device_id_type=MESH)
    for d in range(1, reps):
        pl.semaphore_signal(barrier, inc=1, device_id=(rep_peer(d), t, c), device_id_type=MESH)
    pl.semaphore_wait(barrier, tps + cps + reps - 3)

    def remote(src, dst, send, recv, device):
        return pltpu.make_async_remote_copy(
            src_ref=src, dst_ref=dst, send_sem=send, recv_sem=recv, device_id=device, device_id_type=MESH
        )

    def slot(j, s):
        return wa.at[s] if j is None else wb.at[j, s]

    def near_cp(k):
        if k == 1:
            return c + 1 - 2 * lax.rem(c, 2)
        return jnp.where(c < 2, k, 3 - k)

    inner_cp = (c == 1) | (c == 2)

    def row(j):
        return 0 if j is None else j + 1

    def z_copy(j, k):
        part = slot(j, mine)
        return remote(part, part, w_send_z.at[row(j), k], w_recv.at[row(j), mine], (r, t, near_cp(k)))

    def z_relay(j):
        s = r * cps + near_cp(3)
        part = slot(j, s)
        return remote(part, part, w_send_z.at[row(j), 0], w_recv.at[row(j), s], (r, t, near_cp(1)))

    def y_copy(j, k, d):
        s = mine if k == 0 else r * cps + near_cp(k)
        part = slot(j, s)
        return remote(part, part, w_send_y.at[row(j), k, d], w_recv.at[row(j), s], (rep_peer(d), t, c))

    def arrive(j, s):
        part = slot(j, s)
        remote(part, part, w_send_z.at[row(j), 0], w_recv.at[row(j), s], (r, t, near_cp(1))).wait_recv()

    def swap_copy(j):
        s = rep_peer(1) * cps + c
        part = slot(j, s)
        return remote(part, part, w_send_y.at[row(j), 1, 0], w_recv.at[row(j), s], (r, t, near_cp(1)))

    def send_y(j):
        for d in range(1, reps):
            y_copy(j, 0, d).start()

    def send_z(j):
        z_copy(j, 1).start()
        z_copy(j, 2).start()

        @pl.when(inner_cp)
        def _():
            z_copy(j, 3).start()

    def comm_part(j):
        if j in SWAPPED:
            arrive(j, rep_peer(1) * cps + c)
            swap_copy(j).start()
        for k in range(1, cps):
            arrive(j, r * cps + near_cp(k))
            if k == 3:

                @pl.when(inner_cp)
                def _():
                    z_relay(j).start()

            if k > 1 or j not in SWAPPED:
                for d in range(1, reps):
                    y_copy(j, k, d).start()

    def finish_part(j):
        for d in range(1, reps):
            for k in range(1, cps):
                arrive(j, rep_peer(d) * cps + cp_peer(k))

            if j is None:
                arrive(j, rep_peer(d) * cps + c)
            else:

                @pl.when(functools.reduce(lambda a, b: a & b, [j != q for q in SWAPPED]))
                def _():
                    arrive(j, rep_peer(d) * cps + c)

    def drain(j):
        z_copy(j, 1).wait_send()
        z_copy(j, 2).wait_send()

        @pl.when(inner_cp)
        def _():
            z_copy(j, 3).wait_send()
            z_relay(j).wait_send()

        for d in range(1, reps):
            for k in range(cps):
                if k == 1 and j in SWAPPED:
                    swap_copy(j).wait_send()
                else:
                    y_copy(j, k, d).wait_send()

    def tok_copy(d):
        return remote(tok_ref, tok.at[t], tok_send.at[d], tok_recv.at[t], (r, tp_peer(d), c))

    wa[mine, :, : 3 * local] = qkv_ref[...]
    wa[mine, :, 3 * local :] = outs_ref[...]
    send_y(None)
    send_z(None)
    for d in range(1, tps):
        tok_copy(d).start()
    tok[t] = tok_ref[...]
    for j in range(PARTS):
        wb[j, mine, :, :hid] = gu_ref[:, j * hid : (j + 1) * hid]
        wb[j, mine, :, hid : 2 * hid] = gu_ref[:, hidden + j * hid : hidden + (j + 1) * hid]
        wb[j, mine, :, 2 * hid :] = down_ref[:, j * hid : (j + 1) * hid]

    segments_at = 2 * width + 2 * hidden
    rates_at = segments_at + kv.shape[0]
    qks_at = rates_at + 2 * HD
    window = BACK + tile
    for i in range(tps):
        begin = segments_at + i * tile
        key_ids = vec_ref[:, begin : begin + window]
        square = (tile, tile)
        diagonal_only = lax.broadcasted_iota(jnp.int32, square, 0) == lax.broadcasted_iota(jnp.int32, square, 1)
        own_ids = jnp.sum(jnp.where(diagonal_only, key_ids[:, BACK:], 0.0), axis=1, keepdims=True)
        column = lax.broadcasted_iota(jnp.int32, (tile, window), 1)
        line = lax.broadcasted_iota(jnp.int32, (tile, window), 0) + BACK
        earlier = (key_ids == own_ids) & (column < line)
        position = jnp.sum(jnp.where(earlier, 1.0, 0.0), axis=1, keepdims=True)
        angles = position * vec_ref[:, rates_at : rates_at + HD]
        left = lax.broadcasted_iota(jnp.int32, (tile, HD), 1) < HD // 2
        sine = jnp.sin(angles)
        begins = lax.broadcasted_iota(jnp.int32, (tile, 2 * HD), 0).astype(jnp.float32) + BACK - position
        table_ref[i] = jnp.concatenate([jnp.cos(angles), jnp.where(left, -sine, sine), begins], axis=1)

    comm_part(None)
    send_z(0)
    for j in range(3):
        send_y(j)
    for d in range(1, tps):
        s = tp_peer(d)
        remote(tok_ref, tok.at[s], tok_send.at[d], tok_recv.at[s], (r, s, c)).wait_recv()
    finish_part(None)
    csa[...] = column_scale(wa, shards)
    wo[...] = wa[:, :, 3 * local :].reshape(width, local)
    comm_part(0)

    rows_all = kv.shape[0]

    kv_pieces = -(-BACK // tile)

    def kv_copy(piece):
        count = min(tile, BACK - piece * tile)
        taken = piece * tile + count
        return remote(
            kv.at[pl.ds(rows_all - taken, count)],
            kv.at[pl.ds(BACK - taken, count)],
            kv_send.at[piece],
            kv_recv.at[piece],
            (r, t, cp_peer(1)),
        )

    def project(step, carry):
        i = tps - 1 - step
        rows = pl.ds(pl.multiple_of(i * tile, 64), tile)
        x = jnp.concatenate([tok[s, rows, :] for s in range(tps)], axis=1)
        xt[i] = x
        xf = x.astype(jnp.float32)
        inv = lax.rsqrt(jnp.sum(xf * xf, axis=1, keepdims=True) + EPS)
        weights = wa[:, :, : 3 * local].reshape(width, 3 * local)
        pr = jnp.dot(x, weights, preferred_element_type=jnp.float32) * inv * csa[:, : 3 * local]
        cosine, sine = table_ref[i, :, :HD], table_ref[i, :, HD : 2 * HD]

        def rope(base, factor):
            pieces = []
            for h in range(heads):
                v = pr[:, base + HD * h : base + HD * (h + 1)]
                v = v * lax.rsqrt(jnp.sum(v * v, axis=1, keepdims=True) + EPS)
                v = v * (vec_ref[:, qks_at + HD * h : qks_at + HD * (h + 1)] * factor)
                swapped = jnp.concatenate([v[:, HD // 2 :], v[:, : HD // 2]], axis=1)
                pieces.append(v * cosine + swapped * sine)
            return jnp.concatenate(pieces, axis=1)

        q_s[i] = rope(0, math.sqrt(HD)).astype(jnp.bfloat16)
        kv[pl.ds(pl.multiple_of(BACK + i * tile, 64), tile), :] = jnp.concatenate(
            [rope(local, 1.0), pr[:, 2 * local :]], axis=1
        ).astype(jnp.bfloat16)

        for piece in range(kv_pieces):

            @pl.when((step == piece) & (c < cps - 1))
            def _():
                kv_copy(piece).start()

        @pl.when(step == kv_pieces - 1)
        def _():
            send_z(1)
            send_y(3)
            send_y(4)

        return carry

    @pl.when(c == 0)
    def _():
        kv[pl.ds(0, BACK), :] = jnp.zeros((BACK, kv.shape[1]), kv.dtype)

    lax.fori_loop(0, tps, project, 0)

    @pl.when(c > 0)
    def _():
        for piece in range(kv_pieces):
            kv_copy(piece).wait_recv()

    send_z(2)

    def near_copy(buf, k, send, recv):
        return remote(buf.at[k], buf.at[2 + k], send.at[k], recv.at[k], (r, beside, c))

    def far_copy(buf, send, recv):
        return remote(buf.at[0], buf.at[1], send.at[2], recv.at[2], (r, across, c))

    def scatter_step(step, part, kept, buf_near, buf_far, send, recv):
        @pl.when(step == 0)
        def _():
            buf_near[0] = part.astype(jnp.bfloat16)
            near_copy(buf_near, 0, send, recv).start()

        @pl.when(step == 1)
        def _():
            near_copy(buf_near, 0, send, recv).wait_recv()
            buf_far[0] = (part + buf_near[2].astype(jnp.float32)).astype(jnp.bfloat16)
            far_copy(buf_far, send, recv).start()

        @pl.when(step == 2)
        def _():
            buf_near[1] = part.astype(jnp.bfloat16)
            near_copy(buf_near, 1, send, recv).start()

        @pl.when(step == 3)
        def _():
            kept[...] = part

    def scatter_total(kept, buf_near, buf_far, send, recv):
        near_copy(buf_near, 1, send, recv).wait_recv()
        far_copy(buf_far, send, recv).wait_recv()
        return kept[...] + buf_near[3].astype(jnp.float32) + buf_far[1].astype(jnp.float32)

    def scatter_drain(buf_near, buf_far, send, recv):
        near_copy(buf_near, 0, send, recv).wait_send()
        near_copy(buf_near, 1, send, recv).wait_send()
        far_copy(buf_far, send, recv).wait_send()

    def target(step):
        late = jnp.where(step == 2, beside, t)
        return jnp.where(step == 0, diagonal, jnp.where(step == 1, across, late))

    def attend(step, carry):
        i = target(step)
        first = pl.ds(pl.multiple_of(i * tile, 64), window)
        column = lax.broadcasted_iota(jnp.int32, (tile, window), 1)
        line = lax.broadcasted_iota(jnp.int32, (tile, window), 0) + BACK
        allowed = (column <= line) & (column >= table_ref[i, :, 2 * HD : 2 * HD + 1].astype(jnp.int32))
        qt = q_s[i]
        outs = []
        for h in range(heads):
            keys = kv[first, HD * h : HD * (h + 1)]
            values = kv[first, local + HD * h : local + HD * (h + 1)]
            scores = lax.dot_general(
                qt[:, HD * h : HD * (h + 1)], keys, NT, preferred_element_type=jnp.float32
            )
            scores = jnp.where(allowed, scores, -1e30)
            exponent = jnp.exp(scores - jnp.max(scores, axis=1, keepdims=True))
            total = jnp.sum(exponent, axis=1, keepdims=True)
            got = jnp.dot(exponent.astype(jnp.bfloat16), values, preferred_element_type=jnp.float32)
            outs.append(got / total)
        att = (jnp.concatenate(outs, axis=1) * csa[:, 3 * local :]).astype(jnp.bfloat16)
        part = lax.dot_general(att, wo[...], NT, preferred_element_type=jnp.float32)
        scatter_step(step, part, mix, near, far, a_send, a_recv)

        @pl.when(step == 1)
        def _():
            send_z(3)

        @pl.when(step == 2)
        def _():
            comm_part(1)
            send_z(4)

        return carry

    lax.fori_loop(0, tps, attend, 0)
    comm_part(2)

    def unit(v):
        return v * lax.rsqrt(jnp.sum(v * v, axis=1, keepdims=True) + EPS)

    attn = unit(scatter_total(mix, near, far, a_send, a_recv))
    state = unit(xt[t].astype(jnp.float32))
    mixed = unit(state + vec_ref[:, :width] * (attn - state))
    mix[...] = mixed
    xm[t] = mixed.astype(jnp.bfloat16)

    def mix_copy(k, s, device):
        return remote(xm.at[s], xm.at[s], m_send.at[k], m_recv.at[s], (r, device, c))

    mix_copy(0, t, across).start()
    mix_copy(1, t, beside).start()
    macc[...] = jnp.zeros_like(macc)
    mix_copy(0, across, across).wait_recv()
    mix_copy(2, across, beside).start()
    comm_part(3)
    mix_copy(1, beside, beside).wait_recv()
    mix_copy(2, diagonal, beside).wait_recv()

    def scales(j):
        cs = column_scale(wb.at[j], shards)
        mine_up = pl.ds(pl.multiple_of(2 * width + j * hid, 128), hid)
        mine_gate = pl.ds(pl.multiple_of(2 * width + hidden + j * hid, 128), hid)
        up_by = cs[:, :hid] * vec_ref[:, mine_up]
        gate_by = cs[:, hid : 2 * hid] * vec_ref[:, mine_gate] * math.sqrt(width)
        return up_by, gate_by, cs[:, 2 * hid :]

    def feed(x, j, by):
        gu = jnp.dot(x, wb[j, :, :, : 2 * hid].reshape(width, 2 * hid), preferred_element_type=jnp.float32)
        up = gu[:, :hid] * by[0]
        gate = gu[:, hid:] * by[1]
        inner = (up * (gate / (1.0 + jnp.exp(-gate))) * by[2]).astype(jnp.bfloat16)
        return lax.dot_general(
            inner, wb[j, :, :, 2 * hid :].reshape(width, hid), NT, preferred_element_type=jnp.float32
        )

    def feed_part(j, carry):
        finish_part(j)
        by = scales(j)

        def pair(i, inner_carry):
            both = pl.ds(2 * i, 2)
            part = feed(xm[both].reshape(2 * tile, width), j, by)
            macc[both] = macc[both] + part.reshape(2, tile, width)
            return inner_carry

        lax.fori_loop(0, tps // 2, pair, 0)

        @pl.when(j == 0)
        def _():
            comm_part(4)

        return carry

    lax.fori_loop(0, PARTS - 1, feed_part, 0)
    finish_part(PARTS - 1)
    last_by = scales(PARTS - 1)

    def feed_last(step, carry):
        p = target(step)
        part = macc[p] + feed(xm[p], PARTS - 1, last_by)
        scatter_step(step, part, kept_part, near2, far2, b_send, b_recv)
        return carry

    lax.fori_loop(0, tps, feed_last, 0)
    mlp = unit(scatter_total(kept_part, near2, far2, b_send, b_recv))
    kept = mix[...]
    final = (math.sqrt(width) * unit(kept + vec_ref[:, width : 2 * width] * (mlp - kept))).astype(jnp.bfloat16)
    for p in range(tps):
        obuf[p] = final[:, local * p : local * (p + 1)]

    def out_copy(p):
        return remote(obuf.at[p], fin.at[t], o_send.at[p], o_recv.at[t], (r, p, c))

    for d in range(1, tps):
        out_copy(tp_peer(d)).start()
    fin[t] = obuf[t]
    for d in range(1, tps):
        s = tp_peer(d)
        remote(obuf.at[t], fin.at[s], o_send.at[t], o_recv.at[s], (r, s, c)).wait_recv()
    for s in range(tps):
        out_ref[pl.ds(s * tile, tile), :] = fin[s]

    drain(None)

    for j in range(PARTS):
        drain(j)

    for d in range(1, tps):
        p = tp_peer(d)
        tok_copy(d).wait_send()
        out_copy(p).wait_send()

    scatter_drain(near, far, a_send, a_recv)
    scatter_drain(near2, far2, b_send, b_recv)
    mix_copy(0, t, across).wait_send()
    mix_copy(1, t, beside).wait_send()
    mix_copy(2, across, beside).wait_send()

    @pl.when(c < cps - 1)
    def _():
        for piece in range(kv_pieces):
            kv_copy(piece).wait_send()


def fused_body(
    tokens, qkv_weight, out_weight, gate_up_weight, down_weight, qk_scale,
    attn_rate, mlp_rate, up_scale, gate_scale, segment_ids,
):
    reps, tps, cps = lax.axis_size("rep"), lax.axis_size("tp"), lax.axis_size("cp")
    rows, local = tokens.shape[1], tokens.shape[2]
    depth = qkv_weight.shape[0]
    hidden = gate_up_weight.shape[2]
    hid = hidden // PARTS
    shards = reps * cps
    width = depth * shards
    tile = rows // tps
    bf16 = jnp.bfloat16
    cp = lax.axis_index("cp")
    qkv = qkv_weight.reshape(depth, 3 * local).astype(bf16)
    gate_up = gate_up_weight.reshape(depth, 2 * hidden).astype(bf16)
    padded = jnp.concatenate([jnp.full((BACK,), -1.0, jnp.float32), segment_ids[0].astype(jnp.float32)])
    window = lax.dynamic_slice_in_dim(padded, cp * rows, BACK + rows)
    half = HD // 2
    frequency = jnp.exp(-math.log(10000.0) * jnp.arange(half, dtype=jnp.float32) * 2.0 / HD)
    vectors = jnp.concatenate(
        [attn_rate, mlp_rate, up_scale, gate_scale, window, frequency, frequency, frequency, frequency, qk_scale]
    )[None]
    vmem = pl.BlockSpec(memory_space=pltpu.VMEM)
    dma = pltpu.SemaphoreType.DMA
    f32 = jnp.float32
    flops = 2 * rows * width * (4 * local + 3 * hidden) + 4 * rows * (BACK + tile) * local
    out = pl.pallas_call(
        lambda *refs: fused_kernel(reps, tps, cps, *refs),
        out_shape=jax.ShapeDtypeStruct((1, rows, local), bf16),
        in_specs=[vmem] * 6,
        out_specs=vmem,
        scratch_shapes=[
            pltpu.VMEM((tps, tile, 4 * HD), f32),
            pltpu.VMEM((tps, rows, local), bf16),
            pltpu.VMEM((tps, tile, width), bf16),
            pltpu.VMEM((shards, depth, 4 * local), bf16),
            pltpu.VMEM((PARTS, shards, depth, 3 * hid), bf16),
            pltpu.VMEM((width, local), bf16),
            pltpu.VMEM((1, 4 * local), f32),
            pltpu.VMEM((tps, tile, local), bf16),
            pltpu.VMEM((BACK + rows, 2 * local), bf16),
            pltpu.VMEM((4, tile, width), bf16),
            pltpu.VMEM((2, tile, width), bf16),
            pltpu.VMEM((tps, tile, width), bf16),
            pltpu.VMEM((tile, width), f32),
            pltpu.VMEM((tps, tile, width), f32),
            pltpu.VMEM((tile, width), f32),
            pltpu.VMEM((4, tile, width), bf16),
            pltpu.VMEM((2, tile, width), bf16),
            pltpu.VMEM((tps, tile, local), bf16),
            pltpu.VMEM((tps, tile, local), bf16),
            dma((tps,)), dma((tps,)),
            dma((PARTS + 1, cps)), dma((PARTS + 1, cps, reps)), dma((PARTS + 1, shards)),
            dma((-(-BACK // tile),)), dma((-(-BACK // tile),)),
            dma((tps,)), dma((tps,)), dma((tps,)), dma((tps,)),
            dma((tps,)), dma((tps,)), dma((tps,)), dma((tps,)),
        ],
        compiler_params=pltpu.CompilerParams(
            collective_id=0, has_side_effects=True, vmem_limit_bytes=58 * 1024 * 1024
        ),
        cost_estimate=pl.CostEstimate(flops=flops, bytes_accessed=2 * width * 5120, transcendentals=0),
    )(
        tokens, qkv, out_weight.astype(bf16).T, gate_up, down_weight.astype(bf16).T, vectors
    )
    return out


def body(*arrays):
    depth, tile = arrays[1].shape[0], arrays[0].shape[1] // lax.axis_size("tp")
    aligned = lax.axis_size("tp") == 4 and lax.axis_size("cp") == 4 and lax.axis_size("rep") == 2 and depth % 16 == 0 and tile % 64 == 0 and arrays[3].shape[2] % (128 * PARTS) == 0
    return fused_body(*arrays) if aligned else plain_body(*arrays)


def solution(mesh):
    in_specs = (
        P("rep", "cp", "tp"),
        P(("rep", "cp"), None, "tp"),
        P("tp", ("rep", "cp")),
        P(("rep", "cp"), None, "tp"),
        P("tp", ("rep", "cp")),
        P("tp"),
        P(),
        P(),
        P("tp"),
        P("tp"),
        P("rep", None),
    )
    out_specs = P("rep", "cp", "tp")
    return jax.shard_map(body, mesh=mesh, in_specs=in_specs, out_specs=out_specs, check_vma=False)
```

```python
import functools
import math

import jax
import jax.numpy as jnp
from jax import lax
from jax.experimental import pallas as pl
from jax.experimental.pallas import tpu as pltpu
from jax.sharding import PartitionSpec as P

D = 1280
HD = 64


EPS = 1e-06


def shifted(block, axis, distance):
    devices = range(lax.axis_size(axis))
    route = [(i - distance, i) for i in devices if i - distance in devices]
    return lax.ppermute(block, axis, route)


def unit_rows(array):
    return array * lax.rsqrt(jnp.sum(array * array, axis=-1, keepdims=True) + EPS)


def share_unit(array):
    totals = lax.psum(jnp.sum(array * array, axis=-1), "tp")
    return array * lax.rsqrt(totals + EPS)[:, None]


def rotate(array, position):
    half_dim = array.shape[-1] // 2
    frequency = jnp.exp(
        -math.log(10000.0) * jnp.arange(half_dim, dtype=jnp.float32) * 2.0 / array.shape[-1]
    )
    angles = position.astype(jnp.float32)[:, None] * frequency[None, :]
    cosine = jnp.cos(angles)[:, None, :]
    sine_part = jnp.sin(angles)[:, None, :]
    first_half = array[..., :half_dim]
    second_half = array[..., half_dim:]
    return jnp.concatenate(
        [
            first_half * cosine - second_half * sine_part,
            first_half * sine_part + second_half * cosine,
        ],
        axis=-1,
    )


def stream_positions(segment):
    order_index = jnp.arange(segment.shape[0], dtype=jnp.int32)
    earlier = jnp.concatenate([segment[:1], segment[:-1]])
    boundary = jnp.where(segment != earlier, order_index, jnp.zeros_like(order_index))
    return order_index - lax.cummax(boundary)


def fold_rows(left, piece):
    return jnp.dot(left, piece.reshape(piece.shape[0], -1), preferred_element_type=jnp.float32)


def right_product(left, piece):
    return jnp.dot(left, piece, preferred_element_type=jnp.float32)


def plain_body(
    tokens,
    qkv_weight,
    out_weight,
    gate_up_weight,
    down_weight,
    qk_scale,
    attn_rate,
    mlp_rate,
    up_scale,
    gate_scale,
    segment_ids,
):
    rows = tokens.shape[1]
    local = tokens.shape[2]
    heads = local // HD
    hidden_local = gate_up_weight.shape[2]
    tp_index = lax.axis_index("tp")
    cp_index = lax.axis_index("cp")
    whole_tokens = lax.all_gather(tokens, "tp", axis=2, tiled=True)[0]
    state = unit_rows(whole_tokens.astype(jnp.float32))
    state_in = state.astype(jnp.bfloat16)
    sums = lax.psum(
        (
            jnp.sum(qkv_weight * qkv_weight, axis=0),
            jnp.sum(out_weight * out_weight, axis=1),
            jnp.sum(gate_up_weight * gate_up_weight, axis=0),
            jnp.sum(down_weight * down_weight, axis=1),
        ),
        ("rep", "cp"),
    )
    qkv_norm = (qkv_weight * lax.rsqrt(sums[0] + EPS)[None]).astype(jnp.bfloat16)
    out_norm = (out_weight * lax.rsqrt(sums[1] + EPS)[:, None]).astype(jnp.bfloat16)
    gate_up_norm = (gate_up_weight * lax.rsqrt(sums[2] + EPS)[None]).astype(jnp.bfloat16)
    down_norm = (down_weight * lax.rsqrt(sums[3] + EPS)[:, None]).astype(jnp.bfloat16)
    projected = fold_rows(state_in, lax.all_gather(qkv_norm, ("rep", "cp"), axis=0, tiled=True))
    projected = projected.reshape(rows, 3, heads, HD)
    scale_table = qk_scale.reshape(heads, HD)
    query = (scale_table * unit_rows(projected[:, 0])).astype(jnp.bfloat16)
    keys = (scale_table * unit_rows(projected[:, 1])).astype(jnp.bfloat16)
    values = projected[:, 2].astype(jnp.bfloat16)
    prev_keys, prev_values = shifted((keys, values), "cp", 1)
    segment = segment_ids[0]
    position = stream_positions(segment)
    own_start = cp_index * rows
    prev_start = jnp.maximum(own_start - rows, 0)
    own_pos = lax.dynamic_slice_in_dim(position, own_start, rows)
    prev_pos = lax.dynamic_slice_in_dim(position, prev_start, rows)
    own_seg = lax.dynamic_slice_in_dim(segment, own_start, rows)
    prev_seg = lax.dynamic_slice_in_dim(segment, prev_start, rows)
    query_rot = rotate(query.astype(jnp.float32), own_pos).astype(jnp.bfloat16)
    keys_rot = jnp.concatenate(
        [
            rotate(prev_keys.astype(jnp.float32), prev_pos),
            rotate(keys.astype(jnp.float32), own_pos),
        ],
        axis=0,
    ).astype(jnp.bfloat16)
    key_values = jnp.concatenate([prev_values, values], axis=0)
    key_seg = jnp.concatenate([prev_seg, own_seg])
    key_order = jnp.arange(2 * rows, dtype=jnp.int32)
    query_order = jnp.arange(rows, dtype=jnp.int32) + rows
    allowed = (
        (own_seg[:, None] == key_seg[None, :])
        & (query_order[:, None] >= key_order[None, :])
        & ((key_order[None, :] >= rows) | (cp_index > 0))
    )
    scores = jnp.einsum(
        "qhd,khd->hqk", query_rot, keys_rot, preferred_element_type=jnp.float32
    ) * math.sqrt(HD)
    scores = jnp.where(allowed[None], scores, -1e30)
    exponent = jnp.exp(scores - jnp.max(scores, axis=-1, keepdims=True))
    probs = (exponent / jnp.sum(exponent, axis=-1, keepdims=True)).astype(jnp.bfloat16)
    attended = (
        jnp.einsum("hqk,khd->qhd", probs, key_values, preferred_element_type=jnp.float32)
        .astype(jnp.bfloat16)
        .reshape(rows, local)
    )
    attn_part = right_product(attended, lax.all_gather(out_norm, ("rep", "cp"), axis=1, tiled=True))
    attn_block = lax.psum_scatter(attn_part, "tp", scatter_dimension=1, tiled=True)
    state_block = lax.dynamic_slice_in_dim(state, tp_index * local, local, 1)
    rate_block = lax.dynamic_slice_in_dim(attn_rate, tp_index * local, local, 0)
    mixed = share_unit(state_block + rate_block * (share_unit(attn_block) - state_block))
    mixed_in = lax.all_gather(mixed.astype(jnp.bfloat16), "tp", axis=1, tiled=True)
    gate_up = fold_rows(mixed_in, lax.all_gather(gate_up_norm, ("rep", "cp"), axis=0, tiled=True))
    up_branch = gate_up[:, :hidden_local] * up_scale
    gate_branch = gate_up[:, hidden_local:] * gate_scale * math.sqrt(D)
    inner = (up_branch * jax.nn.silu(gate_branch)).astype(jnp.bfloat16)
    mlp_part = right_product(inner, lax.all_gather(down_norm, ("rep", "cp"), axis=1, tiled=True))
    mlp_block = lax.psum_scatter(mlp_part, "tp", scatter_dimension=1, tiled=True)
    mlp_rate_block = lax.dynamic_slice_in_dim(mlp_rate, tp_index * local, local, 0)
    result = math.sqrt(D) * share_unit(mixed + mlp_rate_block * (share_unit(mlp_block) - mixed))
    return result.astype(jnp.bfloat16)[None]

MESH = pl.DeviceIdType.MESH
PARTS = 5
SWAPPED = (2, 4)
BACK = 512
NT = (((1,), (1,)), ((), ()))


def column_scale(block_ref, shards):
    def add(i, total):
        piece = block_ref[i].astype(jnp.float32)
        return total + jnp.sum(piece * piece, axis=0, keepdims=True)

    zero = jnp.zeros((1, block_ref.shape[-1]), jnp.float32)
    return lax.rsqrt(lax.fori_loop(0, shards, add, zero) + EPS)


def fused_kernel(
    reps, tps, cps,
    tok_all, qkv_all, outs_all, gu_all, down_all, vec_ref,
    out_ref,
    tok_raw, qkv_raw, outs_raw, gu_raw, down_raw, load, table_ref, tok, xt, wa, wb, wo, csa, q_s, kv, near, far, xm, mix, macc, kept_part, near2, far2, obuf, fin,
    tok_send, tok_recv, w_send_z, w_send_y, w_recv, kv_send, kv_recv,
    a_send, a_recv, m_send, m_recv, b_send, b_recv, o_send, o_recv,
):
    r, t, c = lax.axis_index("rep"), lax.axis_index("tp"), lax.axis_index("cp")
    shards = reps * cps
    tile = xt.shape[1]
    width = xt.shape[2]
    local = tok.shape[2]
    heads = local // HD
    depth = wa.shape[1]
    hid = wb.shape[3] // 3
    mine = r * cps + c
    hidden = PARTS * hid
    tok_ref = tok.at[t]
    beside = t + 1 - 2 * lax.rem(t, 2)
    across = lax.rem(t + 2, tps)
    diagonal = lax.rem(beside + 2, tps)

    def tp_peer(d):
        return lax.rem(t + d, tps)

    def cp_peer(d):
        return lax.rem(c + d, cps)

    def rep_peer(d):
        return lax.rem(r + d, reps)

    loads = [
        pltpu.make_async_copy(source, place, load.at[i])
        for i, (source, place) in enumerate(
            [(qkv_all, qkv_raw), (outs_all, outs_raw), (tok_all, tok_raw), (gu_all, gu_raw), (down_all, down_raw)]
        )
    ]
    for copy in loads:
        copy.start()
    barrier = pltpu.get_barrier_semaphore()
    for d in range(1, tps):
        pl.semaphore_signal(barrier, inc=1, device_id=(r, tp_peer(d), c), device_id_type=MESH)
    for d in range(1, cps):
        pl.semaphore_signal(barrier, inc=1, device_id=(r, t, cp_peer(d)), device_id_type=MESH)
    for d in range(1, reps):
        pl.semaphore_signal(barrier, inc=1, device_id=(rep_peer(d), t, c), device_id_type=MESH)
    pl.semaphore_wait(barrier, tps + cps + reps - 3)

    def remote(src, dst, send, recv, device):
        return pltpu.make_async_remote_copy(
            src_ref=src, dst_ref=dst, send_sem=send, recv_sem=recv, device_id=device, device_id_type=MESH
        )

    def slot(j, s):
        return wa.at[s] if j is None else wb.at[j, s]

    def near_cp(k):
        if k == 1:
            return c + 1 - 2 * lax.rem(c, 2)
        return jnp.where(c < 2, k, 3 - k)

    inner_cp = (c == 1) | (c == 2)

    def row(j):
        return 0 if j is None else j + 1

    def z_copy(j, k):
        part = slot(j, mine)
        return remote(part, part, w_send_z.at[row(j), k], w_recv.at[row(j), mine], (r, t, near_cp(k)))

    def z_relay(j):
        s = r * cps + near_cp(3)
        part = slot(j, s)
        return remote(part, part, w_send_z.at[row(j), 0], w_recv.at[row(j), s], (r, t, near_cp(1)))

    def y_copy(j, k, d):
        s = mine if k == 0 else r * cps + near_cp(k)
        part = slot(j, s)
        return remote(part, part, w_send_y.at[row(j), k, d], w_recv.at[row(j), s], (rep_peer(d), t, c))

    def arrive(j, s):
        part = slot(j, s)
        remote(part, part, w_send_z.at[row(j), 0], w_recv.at[row(j), s], (r, t, near_cp(1))).wait_recv()

    def swap_copy(j):
        s = rep_peer(1) * cps + c
        part = slot(j, s)
        return remote(part, part, w_send_y.at[row(j), 1, 0], w_recv.at[row(j), s], (r, t, near_cp(1)))

    def send_y(j):
        for d in range(1, reps):
            y_copy(j, 0, d).start()

    def send_z(j):
        z_copy(j, 1).start()
        z_copy(j, 2).start()
        if j in SWAPPED:
            z_copy(j, 3).start()
        else:

            @pl.when(inner_cp)
            def _():
                z_copy(j, 3).start()

    def comm_part(j):
        if j in SWAPPED:
            arrive(j, rep_peer(1) * cps + c)
            swap_copy(j).start()
        for k in range(1, cps):
            arrive(j, r * cps + near_cp(k))
            if k == 3 and j not in SWAPPED:

                @pl.when(inner_cp)
                def _():
                    z_relay(j).start()

            if k > 1 or j not in SWAPPED:
                for d in range(1, reps):
                    y_copy(j, k, d).start()

    def finish_part(j):
        for d in range(1, reps):
            for k in range(1, cps):
                arrive(j, rep_peer(d) * cps + cp_peer(k))

            if j is None:
                arrive(j, rep_peer(d) * cps + c)
            else:

                @pl.when(functools.reduce(lambda a, b: a & b, [j != q for q in SWAPPED]))
                def _():
                    arrive(j, rep_peer(d) * cps + c)

    def drain(j):
        z_copy(j, 1).wait_send()
        z_copy(j, 2).wait_send()

        if j in SWAPPED:
            z_copy(j, 3).wait_send()
        else:

            @pl.when(inner_cp)
            def _():
                z_copy(j, 3).wait_send()
                z_relay(j).wait_send()

        for d in range(1, reps):
            for k in range(cps):
                if k == 1 and j in SWAPPED:
                    swap_copy(j).wait_send()
                else:
                    y_copy(j, k, d).wait_send()

    def tok_copy(d):
        return remote(tok_ref, tok.at[t], tok_send.at[d], tok_recv.at[t], (r, tp_peer(d), c))

    loads[0].wait()
    loads[1].wait()
    for kind in range(3):
        wa[mine, :, kind * local : (kind + 1) * local] = qkv_raw[kind].astype(jnp.bfloat16)
    wa[mine, :, 3 * local :] = outs_raw[...].astype(jnp.bfloat16)
    send_y(None)
    send_z(None)
    loads[2].wait()
    tok[t] = tok_raw[...].astype(jnp.float32).T.astype(jnp.bfloat16)
    for d in range(1, tps):
        tok_copy(d).start()
    loads[3].wait()
    loads[4].wait()
    for j in range(PARTS):
        wb[j, mine, :, :hid] = gu_raw[:, 0, j * hid : (j + 1) * hid].astype(jnp.bfloat16)
        wb[j, mine, :, hid : 2 * hid] = gu_raw[:, 1, j * hid : (j + 1) * hid].astype(jnp.bfloat16)
        wb[j, mine, :, 2 * hid :] = down_raw[:, j * hid : (j + 1) * hid].astype(jnp.bfloat16)

    segments_at = 2 * width + 2 * hidden
    rates_at = segments_at + kv.shape[0]
    qks_at = rates_at + 2 * HD
    window = BACK + tile
    for i in range(tps):
        begin = segments_at + i * tile
        key_ids = vec_ref[:, begin : begin + window]
        square = (tile, tile)
        diagonal_only = lax.broadcasted_iota(jnp.int32, square, 0) == lax.broadcasted_iota(jnp.int32, square, 1)
        own_ids = jnp.sum(jnp.where(diagonal_only, key_ids[:, BACK:], 0.0), axis=1, keepdims=True)
        column = lax.broadcasted_iota(jnp.int32, (tile, window), 1)
        line = lax.broadcasted_iota(jnp.int32, (tile, window), 0) + BACK
        earlier = (key_ids == own_ids) & (column < line)
        position = jnp.sum(jnp.where(earlier, 1.0, 0.0), axis=1, keepdims=True)
        angles = position * vec_ref[:, rates_at : rates_at + HD]
        left = lax.broadcasted_iota(jnp.int32, (tile, HD), 1) < HD // 2
        sine = jnp.sin(angles)
        begins = lax.broadcasted_iota(jnp.int32, (tile, 2 * HD), 0).astype(jnp.float32) + BACK - position
        table_ref[i] = jnp.concatenate([jnp.cos(angles), jnp.where(left, -sine, sine), begins], axis=1)

    comm_part(None)
    send_z(0)
    for j in range(3):
        send_y(j)
    for d in range(1, tps):
        s = tp_peer(d)
        remote(tok_ref, tok.at[s], tok_send.at[d], tok_recv.at[s], (r, s, c)).wait_recv()
    finish_part(None)
    csa[...] = column_scale(wa, shards)
    wo[...] = wa[:, :, 3 * local :].reshape(width, local)
    comm_part(0)

    rows_all = kv.shape[0]

    kv_pieces = -(-BACK // tile)

    def kv_copy(piece):
        count = min(tile, BACK - piece * tile)
        taken = piece * tile + count
        return remote(
            kv.at[pl.ds(rows_all - taken, count)],
            kv.at[pl.ds(BACK - taken, count)],
            kv_send.at[piece],
            kv_recv.at[piece],
            (r, t, cp_peer(1)),
        )

    def project(step, carry):
        i = tps - 1 - step
        rows = pl.ds(pl.multiple_of(i * tile, 64), tile)
        x = jnp.concatenate([tok[s, rows, :] for s in range(tps)], axis=1)
        xt[i] = x
        xf = x.astype(jnp.float32)
        inv = lax.rsqrt(jnp.sum(xf * xf, axis=1, keepdims=True) + EPS)
        weights = wa[:, :, : 3 * local].reshape(width, 3 * local)
        pr = jnp.dot(x, weights, preferred_element_type=jnp.float32) * inv * csa[:, : 3 * local]
        cosine, sine = table_ref[i, :, :HD], table_ref[i, :, HD : 2 * HD]

        def rope(base, factor):
            pieces = []
            for h in range(heads):
                v = pr[:, base + HD * h : base + HD * (h + 1)]
                v = v * lax.rsqrt(jnp.sum(v * v, axis=1, keepdims=True) + EPS)
                v = v * (vec_ref[:, qks_at + HD * h : qks_at + HD * (h + 1)] * factor)
                swapped = jnp.concatenate([v[:, HD // 2 :], v[:, : HD // 2]], axis=1)
                pieces.append(v * cosine + swapped * sine)
            return jnp.concatenate(pieces, axis=1)

        q_s[i] = rope(0, math.sqrt(HD)).astype(jnp.bfloat16)
        kv[pl.ds(pl.multiple_of(BACK + i * tile, 64), tile), :] = jnp.concatenate(
            [rope(local, 1.0), pr[:, 2 * local :]], axis=1
        ).astype(jnp.bfloat16)

        for piece in range(kv_pieces):

            @pl.when((step == piece) & (c < cps - 1))
            def _():
                kv_copy(piece).start()

        @pl.when(step == kv_pieces - 1)
        def _():
            send_z(1)
            send_z(2)
            send_y(3)
            send_y(4)

        return carry

    @pl.when(c == 0)
    def _():
        kv[pl.ds(0, BACK), :] = jnp.zeros((BACK, kv.shape[1]), kv.dtype)

    lax.fori_loop(0, tps, project, 0)

    @pl.when(c > 0)
    def _():
        for piece in range(kv_pieces):
            kv_copy(piece).wait_recv()

    send_z(3)

    def near_copy(buf, k, send, recv):
        return remote(buf.at[k], buf.at[2 + k], send.at[k], recv.at[k], (r, beside, c))

    def far_copy(buf, send, recv):
        return remote(buf.at[0], buf.at[1], send.at[2], recv.at[2], (r, across, c))

    def scatter_step(step, part, kept, buf_near, buf_far, send, recv):
        @pl.when(step == 0)
        def _():
            buf_near[0] = part.astype(jnp.bfloat16)
            near_copy(buf_near, 0, send, recv).start()

        @pl.when(step == 1)
        def _():
            near_copy(buf_near, 0, send, recv).wait_recv()
            buf_far[0] = (part + buf_near[2].astype(jnp.float32)).astype(jnp.bfloat16)
            far_copy(buf_far, send, recv).start()

        @pl.when(step == 2)
        def _():
            buf_near[1] = part.astype(jnp.bfloat16)
            near_copy(buf_near, 1, send, recv).start()

        @pl.when(step == 3)
        def _():
            kept[...] = part

    def scatter_total(kept, buf_near, buf_far, send, recv):
        near_copy(buf_near, 1, send, recv).wait_recv()
        far_copy(buf_far, send, recv).wait_recv()
        return kept[...] + buf_near[3].astype(jnp.float32) + buf_far[1].astype(jnp.float32)

    def scatter_drain(buf_near, buf_far, send, recv):
        near_copy(buf_near, 0, send, recv).wait_send()
        near_copy(buf_near, 1, send, recv).wait_send()
        far_copy(buf_far, send, recv).wait_send()

    def target(step):
        late = jnp.where(step == 2, beside, t)
        return jnp.where(step == 0, diagonal, jnp.where(step == 1, across, late))

    def attend(step, carry):
        i = target(step)
        first = pl.ds(pl.multiple_of(i * tile, 64), window)
        column = lax.broadcasted_iota(jnp.int32, (tile, window), 1)
        line = lax.broadcasted_iota(jnp.int32, (tile, window), 0) + BACK
        allowed = (column <= line) & (column >= table_ref[i, :, 2 * HD : 2 * HD + 1].astype(jnp.int32))
        qt = q_s[i]
        outs = []
        for h in range(heads):
            keys = kv[first, HD * h : HD * (h + 1)]
            values = kv[first, local + HD * h : local + HD * (h + 1)]
            scores = lax.dot_general(
                qt[:, HD * h : HD * (h + 1)], keys, NT, preferred_element_type=jnp.float32
            )
            scores = jnp.where(allowed, scores, -1e30)
            exponent = jnp.exp(scores - jnp.max(scores, axis=1, keepdims=True))
            total = jnp.sum(exponent, axis=1, keepdims=True)
            got = jnp.dot(exponent.astype(jnp.bfloat16), values, preferred_element_type=jnp.float32)
            outs.append(got / total)
        att = (jnp.concatenate(outs, axis=1) * csa[:, 3 * local :]).astype(jnp.bfloat16)
        part = lax.dot_general(att, wo[...], NT, preferred_element_type=jnp.float32)
        scatter_step(step, part, mix, near, far, a_send, a_recv)

        @pl.when(step == 1)
        def _():
            send_z(4)

        @pl.when(step == 2)
        def _():
            comm_part(1)

        return carry

    lax.fori_loop(0, tps, attend, 0)
    comm_part(2)

    def unit(v):
        return v * lax.rsqrt(jnp.sum(v * v, axis=1, keepdims=True) + EPS)

    attn = unit(scatter_total(mix, near, far, a_send, a_recv))
    state = unit(xt[t].astype(jnp.float32))
    mixed = unit(state + vec_ref[:, :width] * (attn - state))
    mix[...] = mixed
    xm[t] = mixed.astype(jnp.bfloat16)

    def mix_copy(k, s, device):
        return remote(xm.at[s], xm.at[s], m_send.at[k], m_recv.at[s], (r, device, c))

    mix_copy(0, t, across).start()
    mix_copy(1, t, beside).start()
    macc[...] = jnp.zeros_like(macc)
    mix_copy(0, across, across).wait_recv()
    mix_copy(2, across, beside).start()
    comm_part(3)
    mix_copy(1, beside, beside).wait_recv()
    mix_copy(2, diagonal, beside).wait_recv()

    def scales(j):
        cs = column_scale(wb.at[j], shards)
        mine_up = pl.ds(pl.multiple_of(2 * width + j * hid, 128), hid)
        mine_gate = pl.ds(pl.multiple_of(2 * width + hidden + j * hid, 128), hid)
        up_by = cs[:, :hid] * vec_ref[:, mine_up]
        gate_by = cs[:, hid : 2 * hid] * vec_ref[:, mine_gate] * math.sqrt(width)
        return up_by, gate_by, cs[:, 2 * hid :]

    def feed(x, j, by):
        gu = jnp.dot(x, wb[j, :, :, : 2 * hid].reshape(width, 2 * hid), preferred_element_type=jnp.float32)
        up = gu[:, :hid] * by[0]
        gate = gu[:, hid:] * by[1]
        inner = (up * (gate / (1.0 + jnp.exp(-gate))) * by[2]).astype(jnp.bfloat16)
        return lax.dot_general(
            inner, wb[j, :, :, 2 * hid :].reshape(width, hid), NT, preferred_element_type=jnp.float32
        )

    def feed_part(j, carry):
        finish_part(j)
        by = scales(j)

        def pair(i, inner_carry):
            both = pl.ds(2 * i, 2)
            part = feed(xm[both].reshape(2 * tile, width), j, by)
            macc[both] = macc[both] + part.reshape(2, tile, width)
            return inner_carry

        lax.fori_loop(0, tps // 2, pair, 0)

        @pl.when(j == 0)
        def _():
            comm_part(4)

        return carry

    lax.fori_loop(0, PARTS - 1, feed_part, 0)
    finish_part(PARTS - 1)
    last_by = scales(PARTS - 1)

    def feed_last(step, carry):
        p = target(step)
        part = macc[p] + feed(xm[p], PARTS - 1, last_by)
        scatter_step(step, part, kept_part, near2, far2, b_send, b_recv)
        return carry

    lax.fori_loop(0, tps, feed_last, 0)
    mlp = unit(scatter_total(kept_part, near2, far2, b_send, b_recv))
    kept = mix[...]
    final = (math.sqrt(width) * unit(kept + vec_ref[:, width : 2 * width] * (mlp - kept))).astype(jnp.bfloat16)
    for p in range(tps):
        obuf[p] = final[:, local * p : local * (p + 1)]

    def out_copy(p):
        return remote(obuf.at[p], fin.at[t], o_send.at[p], o_recv.at[t], (r, p, c))

    for d in range(1, tps):
        out_copy(tp_peer(d)).start()
    fin[t] = obuf[t]
    for d in range(1, tps):
        s = tp_peer(d)
        remote(obuf.at[t], fin.at[s], o_send.at[t], o_recv.at[s], (r, s, c)).wait_recv()
    whole = jnp.concatenate([fin[s] for s in range(tps)], axis=0)
    out_ref[...] = whole.astype(jnp.float32).T.astype(jnp.bfloat16)

    drain(None)

    for j in range(PARTS):
        drain(j)

    for d in range(1, tps):
        p = tp_peer(d)
        tok_copy(d).wait_send()
        out_copy(p).wait_send()

    scatter_drain(near, far, a_send, a_recv)
    scatter_drain(near2, far2, b_send, b_recv)
    mix_copy(0, t, across).wait_send()
    mix_copy(1, t, beside).wait_send()
    mix_copy(2, across, beside).wait_send()

    @pl.when(c < cps - 1)
    def _():
        for piece in range(kv_pieces):
            kv_copy(piece).wait_send()


def fused_body(
    tokens, qkv_weight, out_weight, gate_up_weight, down_weight, qk_scale,
    attn_rate, mlp_rate, up_scale, gate_scale, segment_ids,
):
    reps, tps, cps = lax.axis_size("rep"), lax.axis_size("tp"), lax.axis_size("cp")
    rows, local = tokens.shape[1], tokens.shape[2]
    depth = qkv_weight.shape[0]
    hidden = gate_up_weight.shape[2]
    hid = hidden // PARTS
    shards = reps * cps
    width = depth * shards
    tile = rows // tps
    bf16 = jnp.bfloat16
    cp = lax.axis_index("cp")
    padded = jnp.concatenate([jnp.full((BACK,), -1.0, jnp.float32), segment_ids[0].astype(jnp.float32)])
    window = lax.dynamic_slice_in_dim(padded, cp * rows, BACK + rows)
    half = HD // 2
    frequency = jnp.exp(-math.log(10000.0) * jnp.arange(half, dtype=jnp.float32) * 2.0 / HD)
    vectors = jnp.concatenate(
        [attn_rate, mlp_rate, up_scale, gate_scale, window, frequency, frequency, frequency, frequency, qk_scale]
    )[None]
    vmem = pl.BlockSpec(memory_space=pltpu.VMEM)
    hbm = pl.BlockSpec(memory_space=pl.ANY)
    dma = pltpu.SemaphoreType.DMA
    f32 = jnp.float32
    flops = 2 * rows * width * (4 * local + 3 * hidden) + 4 * rows * (BACK + tile) * local
    out = pl.pallas_call(
        lambda *refs: fused_kernel(reps, tps, cps, *refs),
        out_shape=jax.ShapeDtypeStruct((local, rows), bf16),
        in_specs=[hbm] * 5 + [vmem],
        out_specs=vmem,
        scratch_shapes=[
            pltpu.VMEM((local, rows), bf16),
            pltpu.VMEM((3, depth, local), f32),
            pltpu.VMEM((depth, local), f32),
            pltpu.VMEM((depth, 2, hidden), f32),
            pltpu.VMEM((depth, hidden), f32),
            dma((5,)),
            pltpu.VMEM((tps, tile, 4 * HD), f32),
            pltpu.VMEM((tps, rows, local), bf16),
            pltpu.VMEM((tps, tile, width), bf16),
            pltpu.VMEM((shards, depth, 4 * local), bf16),
            pltpu.VMEM((PARTS, shards, depth, 3 * hid), bf16),
            pltpu.VMEM((width, local), bf16),
            pltpu.VMEM((1, 4 * local), f32),
            pltpu.VMEM((tps, tile, local), bf16),
            pltpu.VMEM((BACK + rows, 2 * local), bf16),
            pltpu.VMEM((4, tile, width), bf16),
            pltpu.VMEM((2, tile, width), bf16),
            pltpu.VMEM((tps, tile, width), bf16),
            pltpu.VMEM((tile, width), f32),
            pltpu.VMEM((tps, tile, width), f32),
            pltpu.VMEM((tile, width), f32),
            pltpu.VMEM((4, tile, width), bf16),
            pltpu.VMEM((2, tile, width), bf16),
            pltpu.VMEM((tps, tile, local), bf16),
            pltpu.VMEM((tps, tile, local), bf16),
            dma((tps,)), dma((tps,)),
            dma((PARTS + 1, cps)), dma((PARTS + 1, cps, reps)), dma((PARTS + 1, shards)),
            dma((-(-BACK // tile),)), dma((-(-BACK // tile),)),
            dma((tps,)), dma((tps,)), dma((tps,)), dma((tps,)),
            dma((tps,)), dma((tps,)), dma((tps,)), dma((tps,)),
        ],
        compiler_params=pltpu.CompilerParams(
            collective_id=0, has_side_effects=True, vmem_limit_bytes=58 * 1024 * 1024
        ),
        cost_estimate=pl.CostEstimate(flops=flops, bytes_accessed=2 * width * 5120, transcendentals=0),
    )(
        tokens[0].T, qkv_weight.transpose(1, 0, 2), out_weight.T, gate_up_weight, down_weight.T, vectors
    )
    return out.T[None]


def body(*arrays):
    depth, tile = arrays[1].shape[0], arrays[0].shape[1] // lax.axis_size("tp")
    aligned = lax.axis_size("tp") == 4 and lax.axis_size("cp") == 4 and lax.axis_size("rep") == 2 and depth % 16 == 0 and tile % 64 == 0 and arrays[3].shape[2] % (128 * PARTS) == 0
    return fused_body(*arrays) if aligned else plain_body(*arrays)


def solution(mesh):
    in_specs = (
        P("rep", "cp", "tp"),
        P(("rep", "cp"), None, "tp"),
        P("tp", ("rep", "cp")),
        P(("rep", "cp"), None, "tp"),
        P("tp", ("rep", "cp")),
        P("tp"),
        P(),
        P(),
        P("tp"),
        P("tp"),
        P("rep", None),
    )
    out_specs = P("rep", "cp", "tp")
    return jax.shard_map(body, mesh=mesh, in_specs=in_specs, out_specs=out_specs, check_vma=False)
```

```python
import functools
import math

import jax
import jax.numpy as jnp
from jax import lax
from jax.experimental import pallas as pl
from jax.experimental.pallas import tpu as pltpu
from jax.sharding import PartitionSpec as P

D = 1280
HD = 64


EPS = 1e-06


def shifted(block, axis, distance):
    devices = range(lax.axis_size(axis))
    route = [(i - distance, i) for i in devices if i - distance in devices]
    return lax.ppermute(block, axis, route)


def unit_rows(array):
    return array * lax.rsqrt(jnp.sum(array * array, axis=-1, keepdims=True) + EPS)


def share_unit(array):
    totals = lax.psum(jnp.sum(array * array, axis=-1), "tp")
    return array * lax.rsqrt(totals + EPS)[:, None]


def rotate(array, position):
    half_dim = array.shape[-1] // 2
    frequency = jnp.exp(
        -math.log(10000.0) * jnp.arange(half_dim, dtype=jnp.float32) * 2.0 / array.shape[-1]
    )
    angles = position.astype(jnp.float32)[:, None] * frequency[None, :]
    cosine = jnp.cos(angles)[:, None, :]
    sine_part = jnp.sin(angles)[:, None, :]
    first_half = array[..., :half_dim]
    second_half = array[..., half_dim:]
    return jnp.concatenate(
        [
            first_half * cosine - second_half * sine_part,
            first_half * sine_part + second_half * cosine,
        ],
        axis=-1,
    )


def stream_positions(segment):
    order_index = jnp.arange(segment.shape[0], dtype=jnp.int32)
    earlier = jnp.concatenate([segment[:1], segment[:-1]])
    boundary = jnp.where(segment != earlier, order_index, jnp.zeros_like(order_index))
    return order_index - lax.cummax(boundary)


def fold_rows(left, piece):
    return jnp.dot(left, piece.reshape(piece.shape[0], -1), preferred_element_type=jnp.float32)


def right_product(left, piece):
    return jnp.dot(left, piece, preferred_element_type=jnp.float32)


def plain_body(
    tokens,
    qkv_weight,
    out_weight,
    gate_up_weight,
    down_weight,
    qk_scale,
    attn_rate,
    mlp_rate,
    up_scale,
    gate_scale,
    segment_ids,
):
    rows = tokens.shape[1]
    local = tokens.shape[2]
    heads = local // HD
    hidden_local = gate_up_weight.shape[2]
    tp_index = lax.axis_index("tp")
    cp_index = lax.axis_index("cp")
    whole_tokens = lax.all_gather(tokens, "tp", axis=2, tiled=True)[0]
    state = unit_rows(whole_tokens.astype(jnp.float32))
    state_in = state.astype(jnp.bfloat16)
    sums = lax.psum(
        (
            jnp.sum(qkv_weight * qkv_weight, axis=0),
            jnp.sum(out_weight * out_weight, axis=1),
            jnp.sum(gate_up_weight * gate_up_weight, axis=0),
            jnp.sum(down_weight * down_weight, axis=1),
        ),
        ("rep", "cp"),
    )
    qkv_norm = (qkv_weight * lax.rsqrt(sums[0] + EPS)[None]).astype(jnp.bfloat16)
    out_norm = (out_weight * lax.rsqrt(sums[1] + EPS)[:, None]).astype(jnp.bfloat16)
    gate_up_norm = (gate_up_weight * lax.rsqrt(sums[2] + EPS)[None]).astype(jnp.bfloat16)
    down_norm = (down_weight * lax.rsqrt(sums[3] + EPS)[:, None]).astype(jnp.bfloat16)
    projected = fold_rows(state_in, lax.all_gather(qkv_norm, ("rep", "cp"), axis=0, tiled=True))
    projected = projected.reshape(rows, 3, heads, HD)
    scale_table = qk_scale.reshape(heads, HD)
    query = (scale_table * unit_rows(projected[:, 0])).astype(jnp.bfloat16)
    keys = (scale_table * unit_rows(projected[:, 1])).astype(jnp.bfloat16)
    values = projected[:, 2].astype(jnp.bfloat16)
    prev_keys, prev_values = shifted((keys, values), "cp", 1)
    segment = segment_ids[0]
    position = stream_positions(segment)
    own_start = cp_index * rows
    prev_start = jnp.maximum(own_start - rows, 0)
    own_pos = lax.dynamic_slice_in_dim(position, own_start, rows)
    prev_pos = lax.dynamic_slice_in_dim(position, prev_start, rows)
    own_seg = lax.dynamic_slice_in_dim(segment, own_start, rows)
    prev_seg = lax.dynamic_slice_in_dim(segment, prev_start, rows)
    query_rot = rotate(query.astype(jnp.float32), own_pos).astype(jnp.bfloat16)
    keys_rot = jnp.concatenate(
        [
            rotate(prev_keys.astype(jnp.float32), prev_pos),
            rotate(keys.astype(jnp.float32), own_pos),
        ],
        axis=0,
    ).astype(jnp.bfloat16)
    key_values = jnp.concatenate([prev_values, values], axis=0)
    key_seg = jnp.concatenate([prev_seg, own_seg])
    key_order = jnp.arange(2 * rows, dtype=jnp.int32)
    query_order = jnp.arange(rows, dtype=jnp.int32) + rows
    allowed = (
        (own_seg[:, None] == key_seg[None, :])
        & (query_order[:, None] >= key_order[None, :])
        & ((key_order[None, :] >= rows) | (cp_index > 0))
    )
    scores = jnp.einsum(
        "qhd,khd->hqk", query_rot, keys_rot, preferred_element_type=jnp.float32
    ) * math.sqrt(HD)
    scores = jnp.where(allowed[None], scores, -1e30)
    exponent = jnp.exp(scores - jnp.max(scores, axis=-1, keepdims=True))
    probs = (exponent / jnp.sum(exponent, axis=-1, keepdims=True)).astype(jnp.bfloat16)
    attended = (
        jnp.einsum("hqk,khd->qhd", probs, key_values, preferred_element_type=jnp.float32)
        .astype(jnp.bfloat16)
        .reshape(rows, local)
    )
    attn_part = right_product(attended, lax.all_gather(out_norm, ("rep", "cp"), axis=1, tiled=True))
    attn_block = lax.psum_scatter(attn_part, "tp", scatter_dimension=1, tiled=True)
    state_block = lax.dynamic_slice_in_dim(state, tp_index * local, local, 1)
    rate_block = lax.dynamic_slice_in_dim(attn_rate, tp_index * local, local, 0)
    mixed = share_unit(state_block + rate_block * (share_unit(attn_block) - state_block))
    mixed_in = lax.all_gather(mixed.astype(jnp.bfloat16), "tp", axis=1, tiled=True)
    gate_up = fold_rows(mixed_in, lax.all_gather(gate_up_norm, ("rep", "cp"), axis=0, tiled=True))
    up_branch = gate_up[:, :hidden_local] * up_scale
    gate_branch = gate_up[:, hidden_local:] * gate_scale * math.sqrt(D)
    inner = (up_branch * jax.nn.silu(gate_branch)).astype(jnp.bfloat16)
    mlp_part = right_product(inner, lax.all_gather(down_norm, ("rep", "cp"), axis=1, tiled=True))
    mlp_block = lax.psum_scatter(mlp_part, "tp", scatter_dimension=1, tiled=True)
    mlp_rate_block = lax.dynamic_slice_in_dim(mlp_rate, tp_index * local, local, 0)
    result = math.sqrt(D) * share_unit(mixed + mlp_rate_block * (share_unit(mlp_block) - mixed))
    return result.astype(jnp.bfloat16)[None]

MESH = pl.DeviceIdType.MESH
PARTS = 5
SWAPPED = (3, 4)
BACK = 512
NT = (((1,), (1,)), ((), ()))


def column_scale(block_ref, shards):
    def add(i, total):
        piece = block_ref[i].astype(jnp.float32)
        return total + jnp.sum(piece * piece, axis=0, keepdims=True)

    zero = jnp.zeros((1, block_ref.shape[-1]), jnp.float32)
    return lax.rsqrt(lax.fori_loop(0, shards, add, zero) + EPS)


def fused_kernel(
    reps, tps, cps,
    tok_all, qkv_all, outs_all, gu_all, down_all, vec_ref,
    out_ref,
    tok_raw, qkv_raw, outs_raw, gu_raw, down_raw, load, table_ref, tok, xt, wa, wb, wo, csa, q_s, kv, near, far, xm, mix, macc, kept_part, near2, far2, obuf, fin,
    tok_send, tok_recv, w_send_z, w_send_y, w_recv, kv_send, kv_recv,
    a_send, a_recv, m_send, m_recv, b_send, b_recv, o_send, o_recv,
):
    r, t, c = lax.axis_index("rep"), lax.axis_index("tp"), lax.axis_index("cp")
    shards = reps * cps
    tile = xt.shape[1]
    width = xt.shape[2]
    local = tok.shape[2]
    heads = local // HD
    depth = wa.shape[1]
    hid = wb.shape[3] // 3
    mine = r * cps + c
    hidden = PARTS * hid
    tok_ref = tok.at[t]
    beside = t + 1 - 2 * lax.rem(t, 2)
    across = lax.rem(t + 2, tps)
    diagonal = lax.rem(beside + 2, tps)

    def tp_peer(d):
        return lax.rem(t + d, tps)

    def cp_peer(d):
        return lax.rem(c + d, cps)

    def rep_peer(d):
        return lax.rem(r + d, reps)

    loads = [
        pltpu.make_async_copy(source, place, load.at[i])
        for i, (source, place) in enumerate(
            [(qkv_all, qkv_raw), (outs_all, outs_raw), (tok_all, tok_raw), (gu_all, gu_raw), (down_all, down_raw)]
        )
    ]
    for copy in loads:
        copy.start()
    barrier = pltpu.get_barrier_semaphore()
    for d in range(1, tps):
        pl.semaphore_signal(barrier, inc=1, device_id=(r, tp_peer(d), c), device_id_type=MESH)
    for d in range(1, cps):
        pl.semaphore_signal(barrier, inc=1, device_id=(r, t, cp_peer(d)), device_id_type=MESH)
    for d in range(1, reps):
        pl.semaphore_signal(barrier, inc=1, device_id=(rep_peer(d), t, c), device_id_type=MESH)
    pl.semaphore_wait(barrier, tps + cps + reps - 3)

    def remote(src, dst, send, recv, device):
        return pltpu.make_async_remote_copy(
            src_ref=src, dst_ref=dst, send_sem=send, recv_sem=recv, device_id=device, device_id_type=MESH
        )

    def slot(j, s):
        return wa.at[s] if j is None else wb.at[j, s]

    def near_cp(k):
        if k == 1:
            return c + 1 - 2 * lax.rem(c, 2)
        return jnp.where(c < 2, k, 3 - k)

    inner_cp = (c == 1) | (c == 2)

    def row(j):
        return 0 if j is None else j + 1

    def z_copy(j, k):
        part = slot(j, mine)
        return remote(part, part, w_send_z.at[row(j), k], w_recv.at[row(j), mine], (r, t, near_cp(k)))

    def z_relay(j):
        s = r * cps + near_cp(3)
        part = slot(j, s)
        return remote(part, part, w_send_z.at[row(j), 0], w_recv.at[row(j), s], (r, t, near_cp(1)))

    def y_copy(j, k, d):
        s = mine if k == 0 else r * cps + near_cp(k)
        part = slot(j, s)
        return remote(part, part, w_send_y.at[row(j), k, d], w_recv.at[row(j), s], (rep_peer(d), t, c))

    def arrive(j, s):
        part = slot(j, s)
        remote(part, part, w_send_z.at[row(j), 0], w_recv.at[row(j), s], (r, t, near_cp(1))).wait_recv()

    def swap_copy(j):
        s = rep_peer(1) * cps + c
        part = slot(j, s)
        return remote(part, part, w_send_y.at[row(j), 1, 0], w_recv.at[row(j), s], (r, t, near_cp(1)))

    def send_y(j):
        for d in range(1, reps):
            y_copy(j, 0, d).start()

    def send_z(j):
        z_copy(j, 1).start()
        z_copy(j, 2).start()
        if j in SWAPPED:
            z_copy(j, 3).start()
        else:

            @pl.when(inner_cp)
            def _():
                z_copy(j, 3).start()

    def comm_part(j):
        if j in SWAPPED:
            arrive(j, rep_peer(1) * cps + c)
            swap_copy(j).start()
        for k in range(1, cps):
            arrive(j, r * cps + near_cp(k))
            if k == 3 and j not in SWAPPED:

                @pl.when(inner_cp)
                def _():
                    z_relay(j).start()

            if k > 1 or j not in SWAPPED:
                for d in range(1, reps):
                    y_copy(j, k, d).start()

    def finish_part(j):
        for d in range(1, reps):
            for k in range(1, cps):
                arrive(j, rep_peer(d) * cps + cp_peer(k))

            if j is None:
                arrive(j, rep_peer(d) * cps + c)
            else:

                @pl.when(functools.reduce(lambda a, b: a & b, [j != q for q in SWAPPED]))
                def _():
                    arrive(j, rep_peer(d) * cps + c)

    def drain(j):
        z_copy(j, 1).wait_send()
        z_copy(j, 2).wait_send()

        if j in SWAPPED:
            z_copy(j, 3).wait_send()
        else:

            @pl.when(inner_cp)
            def _():
                z_copy(j, 3).wait_send()
                z_relay(j).wait_send()

        for d in range(1, reps):
            for k in range(cps):
                if k == 1 and j in SWAPPED:
                    swap_copy(j).wait_send()
                else:
                    y_copy(j, k, d).wait_send()

    def tok_copy(d):
        return remote(tok_ref, tok.at[t], tok_send.at[d], tok_recv.at[t], (r, tp_peer(d), c))

    loads[0].wait()
    loads[1].wait()
    for kind in range(3):
        wa[mine, :, kind * local : (kind + 1) * local] = qkv_raw[kind].astype(jnp.bfloat16)
    wa[mine, :, 3 * local :] = outs_raw[...].astype(jnp.bfloat16)
    send_y(None)
    send_z(None)
    loads[2].wait()
    tok[t] = tok_raw[...].astype(jnp.float32).T.astype(jnp.bfloat16)
    for d in range(1, tps):
        tok_copy(d).start()
    loads[3].wait()
    loads[4].wait()
    for j in range(PARTS):
        wb[j, mine, :, :hid] = gu_raw[:, 0, j * hid : (j + 1) * hid].astype(jnp.bfloat16)
        wb[j, mine, :, hid : 2 * hid] = gu_raw[:, 1, j * hid : (j + 1) * hid].astype(jnp.bfloat16)
        wb[j, mine, :, 2 * hid :] = down_raw[:, j * hid : (j + 1) * hid].astype(jnp.bfloat16)

    segments_at = 2 * width + 2 * hidden
    rates_at = segments_at + kv.shape[0]
    qks_at = rates_at + 2 * HD
    window = BACK + tile
    for i in range(tps):
        begin = segments_at + i * tile
        key_ids = vec_ref[:, begin : begin + window]
        square = (tile, tile)
        diagonal_only = lax.broadcasted_iota(jnp.int32, square, 0) == lax.broadcasted_iota(jnp.int32, square, 1)
        own_ids = jnp.sum(jnp.where(diagonal_only, key_ids[:, BACK:], 0.0), axis=1, keepdims=True)
        column = lax.broadcasted_iota(jnp.int32, (tile, window), 1)
        line = lax.broadcasted_iota(jnp.int32, (tile, window), 0) + BACK
        earlier = (key_ids == own_ids) & (column < line)
        position = jnp.sum(jnp.where(earlier, 1.0, 0.0), axis=1, keepdims=True)
        angles = position * vec_ref[:, rates_at : rates_at + HD]
        left = lax.broadcasted_iota(jnp.int32, (tile, HD), 1) < HD // 2
        sine = jnp.sin(angles)
        begins = lax.broadcasted_iota(jnp.int32, (tile, 2 * HD), 0).astype(jnp.float32) + BACK - position
        table_ref[i] = jnp.concatenate([jnp.cos(angles), jnp.where(left, -sine, sine), begins], axis=1)

    comm_part(None)
    send_z(0)
    for j in range(3):
        send_y(j)
    for d in range(1, tps):
        s = tp_peer(d)
        remote(tok_ref, tok.at[s], tok_send.at[d], tok_recv.at[s], (r, s, c)).wait_recv()
    finish_part(None)
    csa[...] = column_scale(wa, shards)
    comm_part(0)
    send_z(1)
    wo[...] = wa[:, :, 3 * local :].reshape(width, local)

    rows_all = kv.shape[0]

    kv_pieces = -(-BACK // tile)

    def kv_copy(piece):
        count = min(tile, BACK - piece * tile)
        taken = piece * tile + count
        return remote(
            kv.at[pl.ds(rows_all - taken, count)],
            kv.at[pl.ds(BACK - taken, count)],
            kv_send.at[piece],
            kv_recv.at[piece],
            (r, t, cp_peer(1)),
        )

    def project(step, carry):
        i = tps - 1 - step
        rows = pl.ds(pl.multiple_of(i * tile, 64), tile)
        x = jnp.concatenate([tok[s, rows, :] for s in range(tps)], axis=1)
        xt[i] = x
        xf = x.astype(jnp.float32)
        inv = lax.rsqrt(jnp.sum(xf * xf, axis=1, keepdims=True) + EPS)
        weights = wa[:, :, : 3 * local].reshape(width, 3 * local)
        pr = jnp.dot(x, weights, preferred_element_type=jnp.float32) * inv * csa[:, : 3 * local]
        cosine, sine = table_ref[i, :, :HD], table_ref[i, :, HD : 2 * HD]

        def rope(base, factor):
            pieces = []
            for h in range(heads):
                v = pr[:, base + HD * h : base + HD * (h + 1)]
                v = v * lax.rsqrt(jnp.sum(v * v, axis=1, keepdims=True) + EPS)
                v = v * (vec_ref[:, qks_at + HD * h : qks_at + HD * (h + 1)] * factor)
                swapped = jnp.concatenate([v[:, HD // 2 :], v[:, : HD // 2]], axis=1)
                pieces.append(v * cosine + swapped * sine)
            return jnp.concatenate(pieces, axis=1)

        q_s[i] = rope(0, math.sqrt(HD)).astype(jnp.bfloat16)
        kv[pl.ds(pl.multiple_of(BACK + i * tile, 64), tile), :] = jnp.concatenate(
            [rope(local, 1.0), pr[:, 2 * local :]], axis=1
        ).astype(jnp.bfloat16)

        for piece in range(kv_pieces):

            @pl.when((step == piece) & (c < cps - 1))
            def _():
                kv_copy(piece).start()

        @pl.when(step == kv_pieces - 1)
        def _():
            send_z(2)
            send_y(3)
            send_y(4)

        return carry

    @pl.when(c == 0)
    def _():
        kv[pl.ds(0, BACK), :] = jnp.zeros((BACK, kv.shape[1]), kv.dtype)

    lax.fori_loop(0, tps, project, 0)

    @pl.when(c > 0)
    def _():
        for piece in range(kv_pieces):
            kv_copy(piece).wait_recv()

    send_z(3)

    def near_copy(buf, k, send, recv):
        return remote(buf.at[k], buf.at[2 + k], send.at[k], recv.at[k], (r, beside, c))

    def far_copy(buf, send, recv):
        return remote(buf.at[0], buf.at[1], send.at[2], recv.at[2], (r, across, c))

    def scatter_step(step, part, kept, buf_near, buf_far, send, recv):
        @pl.when(step == 0)
        def _():
            buf_near[0] = part.astype(jnp.bfloat16)
            near_copy(buf_near, 0, send, recv).start()

        @pl.when(step == 1)
        def _():
            near_copy(buf_near, 0, send, recv).wait_recv()
            buf_far[0] = (part + buf_near[2].astype(jnp.float32)).astype(jnp.bfloat16)
            far_copy(buf_far, send, recv).start()

        @pl.when(step == 2)
        def _():
            buf_near[1] = part.astype(jnp.bfloat16)
            near_copy(buf_near, 1, send, recv).start()

        @pl.when(step == 3)
        def _():
            kept[...] = part

    def scatter_total(kept, buf_near, buf_far, send, recv):
        near_copy(buf_near, 1, send, recv).wait_recv()
        far_copy(buf_far, send, recv).wait_recv()
        return kept[...] + buf_near[3].astype(jnp.float32) + buf_far[1].astype(jnp.float32)

    def scatter_drain(buf_near, buf_far, send, recv):
        near_copy(buf_near, 0, send, recv).wait_send()
        near_copy(buf_near, 1, send, recv).wait_send()
        far_copy(buf_far, send, recv).wait_send()

    def target(step):
        late = jnp.where(step == 2, beside, t)
        return jnp.where(step == 0, diagonal, jnp.where(step == 1, across, late))

    def attend(step, carry):
        i = target(step)
        first = pl.ds(pl.multiple_of(i * tile, 64), window)
        column = lax.broadcasted_iota(jnp.int32, (tile, window), 1)
        line = lax.broadcasted_iota(jnp.int32, (tile, window), 0) + BACK
        allowed = (column <= line) & (column >= table_ref[i, :, 2 * HD : 2 * HD + 1].astype(jnp.int32))
        qt = q_s[i]
        outs = []
        for h in range(heads):
            keys = kv[first, HD * h : HD * (h + 1)]
            values = kv[first, local + HD * h : local + HD * (h + 1)]
            scores = lax.dot_general(
                qt[:, HD * h : HD * (h + 1)], keys, NT, preferred_element_type=jnp.float32
            )
            scores = jnp.where(allowed, scores, -1e30)
            exponent = jnp.exp(scores - jnp.max(scores, axis=1, keepdims=True))
            total = jnp.sum(exponent, axis=1, keepdims=True)
            got = jnp.dot(exponent.astype(jnp.bfloat16), values, preferred_element_type=jnp.float32)
            outs.append(got / total)
        att = (jnp.concatenate(outs, axis=1) * csa[:, 3 * local :]).astype(jnp.bfloat16)
        part = lax.dot_general(att, wo[...], NT, preferred_element_type=jnp.float32)
        scatter_step(step, part, mix, near, far, a_send, a_recv)

        @pl.when(step == 1)
        def _():
            send_z(4)

        @pl.when(step == 2)
        def _():
            comm_part(1)

        return carry

    lax.fori_loop(0, tps, attend, 0)
    comm_part(2)

    def unit(v):
        return v * lax.rsqrt(jnp.sum(v * v, axis=1, keepdims=True) + EPS)

    attn = unit(scatter_total(mix, near, far, a_send, a_recv))
    state = unit(xt[t].astype(jnp.float32))
    mixed = unit(state + vec_ref[:, :width] * (attn - state))
    mix[...] = mixed
    xm[t] = mixed.astype(jnp.bfloat16)

    def mix_copy(k, s, device):
        return remote(xm.at[s], xm.at[s], m_send.at[k], m_recv.at[s], (r, device, c))

    mix_copy(0, t, across).start()
    mix_copy(1, t, beside).start()
    macc[...] = jnp.zeros_like(macc)
    mix_copy(0, across, across).wait_recv()
    mix_copy(2, across, beside).start()
    comm_part(3)
    mix_copy(1, beside, beside).wait_recv()
    mix_copy(2, diagonal, beside).wait_recv()

    def scales(j):
        cs = column_scale(wb.at[j], shards)
        mine_up = pl.ds(pl.multiple_of(2 * width + j * hid, 128), hid)
        mine_gate = pl.ds(pl.multiple_of(2 * width + hidden + j * hid, 128), hid)
        up_by = cs[:, :hid] * vec_ref[:, mine_up]
        gate_by = cs[:, hid : 2 * hid] * vec_ref[:, mine_gate] * math.sqrt(width)
        return up_by, gate_by, cs[:, 2 * hid :]

    def feed(x, j, by):
        gu = jnp.dot(x, wb[j, :, :, : 2 * hid].reshape(width, 2 * hid), preferred_element_type=jnp.float32)
        up = gu[:, :hid] * by[0]
        gate = gu[:, hid:] * by[1]
        inner = (up * (gate / (1.0 + jnp.exp(-gate))) * by[2]).astype(jnp.bfloat16)
        return lax.dot_general(
            inner, wb[j, :, :, 2 * hid :].reshape(width, hid), NT, preferred_element_type=jnp.float32
        )

    def feed_part(j, carry):
        finish_part(j)
        by = scales(j)

        def pair(i, inner_carry):
            both = pl.ds(2 * i, 2)
            part = feed(xm[both].reshape(2 * tile, width), j, by)
            macc[both] = macc[both] + part.reshape(2, tile, width)
            return inner_carry

        lax.fori_loop(0, tps // 2, pair, 0)

        @pl.when(j == 0)
        def _():
            comm_part(4)

        return carry

    lax.fori_loop(0, PARTS - 1, feed_part, 0)
    finish_part(PARTS - 1)
    last_by = scales(PARTS - 1)

    def feed_last(step, carry):
        p = target(step)
        part = macc[p] + feed(xm[p], PARTS - 1, last_by)
        scatter_step(step, part, kept_part, near2, far2, b_send, b_recv)
        return carry

    lax.fori_loop(0, tps, feed_last, 0)
    mlp = unit(scatter_total(kept_part, near2, far2, b_send, b_recv))
    kept = mix[...]
    final = (math.sqrt(width) * unit(kept + vec_ref[:, width : 2 * width] * (mlp - kept))).astype(jnp.bfloat16)
    for p in range(tps):
        obuf[p] = final[:, local * p : local * (p + 1)]

    def out_copy(p):
        return remote(obuf.at[p], fin.at[t], o_send.at[p], o_recv.at[t], (r, p, c))

    for d in range(1, tps):
        out_copy(tp_peer(d)).start()
    fin[t] = obuf[t]
    for d in range(1, tps):
        s = tp_peer(d)
        remote(obuf.at[t], fin.at[s], o_send.at[t], o_recv.at[s], (r, s, c)).wait_recv()
    whole = jnp.concatenate([fin[s] for s in range(tps)], axis=0)
    out_ref[...] = whole.astype(jnp.float32).T.astype(jnp.bfloat16)

    drain(None)

    for j in range(PARTS):
        drain(j)

    for d in range(1, tps):
        p = tp_peer(d)
        tok_copy(d).wait_send()
        out_copy(p).wait_send()

    scatter_drain(near, far, a_send, a_recv)
    scatter_drain(near2, far2, b_send, b_recv)
    mix_copy(0, t, across).wait_send()
    mix_copy(1, t, beside).wait_send()
    mix_copy(2, across, beside).wait_send()

    @pl.when(c < cps - 1)
    def _():
        for piece in range(kv_pieces):
            kv_copy(piece).wait_send()


def fused_body(
    tokens, qkv_weight, out_weight, gate_up_weight, down_weight, qk_scale,
    attn_rate, mlp_rate, up_scale, gate_scale, segment_ids,
):
    reps, tps, cps = lax.axis_size("rep"), lax.axis_size("tp"), lax.axis_size("cp")
    rows, local = tokens.shape[1], tokens.shape[2]
    depth = qkv_weight.shape[0]
    hidden = gate_up_weight.shape[2]
    hid = hidden // PARTS
    shards = reps * cps
    width = depth * shards
    tile = rows // tps
    bf16 = jnp.bfloat16
    cp = lax.axis_index("cp")
    padded = jnp.concatenate([jnp.full((BACK,), -1.0, jnp.float32), segment_ids[0].astype(jnp.float32)])
    window = lax.dynamic_slice_in_dim(padded, cp * rows, BACK + rows)
    half = HD // 2
    frequency = jnp.exp(-math.log(10000.0) * jnp.arange(half, dtype=jnp.float32) * 2.0 / HD)
    vectors = jnp.concatenate(
        [attn_rate, mlp_rate, up_scale, gate_scale, window, frequency, frequency, frequency, frequency, qk_scale]
    )[None]
    vmem = pl.BlockSpec(memory_space=pltpu.VMEM)
    hbm = pl.BlockSpec(memory_space=pl.ANY)
    dma = pltpu.SemaphoreType.DMA
    f32 = jnp.float32
    flops = 2 * rows * width * (4 * local + 3 * hidden) + 4 * rows * (BACK + tile) * local
    out = pl.pallas_call(
        lambda *refs: fused_kernel(reps, tps, cps, *refs),
        out_shape=jax.ShapeDtypeStruct((local, rows), bf16),
        in_specs=[hbm] * 5 + [vmem],
        out_specs=vmem,
        scratch_shapes=[
            pltpu.VMEM((local, rows), bf16),
            pltpu.VMEM((3, depth, local), f32),
            pltpu.VMEM((depth, local), f32),
            pltpu.VMEM((depth, 2, hidden), f32),
            pltpu.VMEM((depth, hidden), f32),
            dma((5,)),
            pltpu.VMEM((tps, tile, 4 * HD), f32),
            pltpu.VMEM((tps, rows, local), bf16),
            pltpu.VMEM((tps, tile, width), bf16),
            pltpu.VMEM((shards, depth, 4 * local), bf16),
            pltpu.VMEM((PARTS, shards, depth, 3 * hid), bf16),
            pltpu.VMEM((width, local), bf16),
            pltpu.VMEM((1, 4 * local), f32),
            pltpu.VMEM((tps, tile, local), bf16),
            pltpu.VMEM((BACK + rows, 2 * local), bf16),
            pltpu.VMEM((4, tile, width), bf16),
            pltpu.VMEM((2, tile, width), bf16),
            pltpu.VMEM((tps, tile, width), bf16),
            pltpu.VMEM((tile, width), f32),
            pltpu.VMEM((tps, tile, width), f32),
            pltpu.VMEM((tile, width), f32),
            pltpu.VMEM((4, tile, width), bf16),
            pltpu.VMEM((2, tile, width), bf16),
            pltpu.VMEM((tps, tile, local), bf16),
            pltpu.VMEM((tps, tile, local), bf16),
            dma((tps,)), dma((tps,)),
            dma((PARTS + 1, cps)), dma((PARTS + 1, cps, reps)), dma((PARTS + 1, shards)),
            dma((-(-BACK // tile),)), dma((-(-BACK // tile),)),
            dma((tps,)), dma((tps,)), dma((tps,)), dma((tps,)),
            dma((tps,)), dma((tps,)), dma((tps,)), dma((tps,)),
        ],
        compiler_params=pltpu.CompilerParams(
            collective_id=0, has_side_effects=True, vmem_limit_bytes=58 * 1024 * 1024
        ),
        cost_estimate=pl.CostEstimate(flops=flops, bytes_accessed=2 * width * 5120, transcendentals=0),
    )(
        tokens[0].T, qkv_weight.transpose(1, 0, 2), out_weight.T, gate_up_weight, down_weight.T, vectors
    )
    return out.T[None]


def body(*arrays):
    depth, tile = arrays[1].shape[0], arrays[0].shape[1] // lax.axis_size("tp")
    aligned = lax.axis_size("tp") == 4 and lax.axis_size("cp") == 4 and lax.axis_size("rep") == 2 and depth % 16 == 0 and tile % 64 == 0 and arrays[3].shape[2] % (128 * PARTS) == 0
    return fused_body(*arrays) if aligned else plain_body(*arrays)


def solution(mesh):
    in_specs = (
        P("rep", "cp", "tp"),
        P(("rep", "cp"), None, "tp"),
        P("tp", ("rep", "cp")),
        P(("rep", "cp"), None, "tp"),
        P("tp", ("rep", "cp")),
        P("tp"),
        P(),
        P(),
        P("tp"),
        P("tp"),
        P("rep", None),
    )
    out_specs = P("rep", "cp", "tp")
    return jax.shard_map(body, mesh=mesh, in_specs=in_specs, out_specs=out_specs, check_vma=False)
```

```python
import functools
import math

import jax
import jax.numpy as jnp
from jax import lax
from jax.experimental import pallas as pl
from jax.experimental.pallas import tpu as pltpu
from jax.sharding import PartitionSpec as P

D = 1280
HD = 64


EPS = 1e-06


def shifted(block, axis, distance):
    devices = range(lax.axis_size(axis))
    route = [(i - distance, i) for i in devices if i - distance in devices]
    return lax.ppermute(block, axis, route)


def unit_rows(array):
    return array * lax.rsqrt(jnp.sum(array * array, axis=-1, keepdims=True) + EPS)


def share_unit(array):
    totals = lax.psum(jnp.sum(array * array, axis=-1), "tp")
    return array * lax.rsqrt(totals + EPS)[:, None]


def rotate(array, position):
    half_dim = array.shape[-1] // 2
    frequency = jnp.exp(
        -math.log(10000.0) * jnp.arange(half_dim, dtype=jnp.float32) * 2.0 / array.shape[-1]
    )
    angles = position.astype(jnp.float32)[:, None] * frequency[None, :]
    cosine = jnp.cos(angles)[:, None, :]
    sine_part = jnp.sin(angles)[:, None, :]
    first_half = array[..., :half_dim]
    second_half = array[..., half_dim:]
    return jnp.concatenate(
        [
            first_half * cosine - second_half * sine_part,
            first_half * sine_part + second_half * cosine,
        ],
        axis=-1,
    )


def stream_positions(segment):
    order_index = jnp.arange(segment.shape[0], dtype=jnp.int32)
    earlier = jnp.concatenate([segment[:1], segment[:-1]])
    boundary = jnp.where(segment != earlier, order_index, jnp.zeros_like(order_index))
    return order_index - lax.cummax(boundary)


def fold_rows(left, piece):
    return jnp.dot(left, piece.reshape(piece.shape[0], -1), preferred_element_type=jnp.float32)


def right_product(left, piece):
    return jnp.dot(left, piece, preferred_element_type=jnp.float32)


def plain_body(
    tokens,
    qkv_weight,
    out_weight,
    gate_up_weight,
    down_weight,
    qk_scale,
    attn_rate,
    mlp_rate,
    up_scale,
    gate_scale,
    segment_ids,
):
    rows = tokens.shape[1]
    local = tokens.shape[2]
    heads = local // HD
    hidden_local = gate_up_weight.shape[2]
    tp_index = lax.axis_index("tp")
    cp_index = lax.axis_index("cp")
    whole_tokens = lax.all_gather(tokens, "tp", axis=2, tiled=True)[0]
    state = unit_rows(whole_tokens.astype(jnp.float32))
    state_in = state.astype(jnp.bfloat16)
    sums = lax.psum(
        (
            jnp.sum(qkv_weight * qkv_weight, axis=0),
            jnp.sum(out_weight * out_weight, axis=1),
            jnp.sum(gate_up_weight * gate_up_weight, axis=0),
            jnp.sum(down_weight * down_weight, axis=1),
        ),
        ("rep", "cp"),
    )
    qkv_norm = (qkv_weight * lax.rsqrt(sums[0] + EPS)[None]).astype(jnp.bfloat16)
    out_norm = (out_weight * lax.rsqrt(sums[1] + EPS)[:, None]).astype(jnp.bfloat16)
    gate_up_norm = (gate_up_weight * lax.rsqrt(sums[2] + EPS)[None]).astype(jnp.bfloat16)
    down_norm = (down_weight * lax.rsqrt(sums[3] + EPS)[:, None]).astype(jnp.bfloat16)
    projected = fold_rows(state_in, lax.all_gather(qkv_norm, ("rep", "cp"), axis=0, tiled=True))
    projected = projected.reshape(rows, 3, heads, HD)
    scale_table = qk_scale.reshape(heads, HD)
    query = (scale_table * unit_rows(projected[:, 0])).astype(jnp.bfloat16)
    keys = (scale_table * unit_rows(projected[:, 1])).astype(jnp.bfloat16)
    values = projected[:, 2].astype(jnp.bfloat16)
    prev_keys, prev_values = shifted((keys, values), "cp", 1)
    segment = segment_ids[0]
    position = stream_positions(segment)
    own_start = cp_index * rows
    prev_start = jnp.maximum(own_start - rows, 0)
    own_pos = lax.dynamic_slice_in_dim(position, own_start, rows)
    prev_pos = lax.dynamic_slice_in_dim(position, prev_start, rows)
    own_seg = lax.dynamic_slice_in_dim(segment, own_start, rows)
    prev_seg = lax.dynamic_slice_in_dim(segment, prev_start, rows)
    query_rot = rotate(query.astype(jnp.float32), own_pos).astype(jnp.bfloat16)
    keys_rot = jnp.concatenate(
        [
            rotate(prev_keys.astype(jnp.float32), prev_pos),
            rotate(keys.astype(jnp.float32), own_pos),
        ],
        axis=0,
    ).astype(jnp.bfloat16)
    key_values = jnp.concatenate([prev_values, values], axis=0)
    key_seg = jnp.concatenate([prev_seg, own_seg])
    key_order = jnp.arange(2 * rows, dtype=jnp.int32)
    query_order = jnp.arange(rows, dtype=jnp.int32) + rows
    allowed = (
        (own_seg[:, None] == key_seg[None, :])
        & (query_order[:, None] >= key_order[None, :])
        & ((key_order[None, :] >= rows) | (cp_index > 0))
    )
    scores = jnp.einsum(
        "qhd,khd->hqk", query_rot, keys_rot, preferred_element_type=jnp.float32
    ) * math.sqrt(HD)
    scores = jnp.where(allowed[None], scores, -1e30)
    exponent = jnp.exp(scores - jnp.max(scores, axis=-1, keepdims=True))
    probs = (exponent / jnp.sum(exponent, axis=-1, keepdims=True)).astype(jnp.bfloat16)
    attended = (
        jnp.einsum("hqk,khd->qhd", probs, key_values, preferred_element_type=jnp.float32)
        .astype(jnp.bfloat16)
        .reshape(rows, local)
    )
    attn_part = right_product(attended, lax.all_gather(out_norm, ("rep", "cp"), axis=1, tiled=True))
    attn_block = lax.psum_scatter(attn_part, "tp", scatter_dimension=1, tiled=True)
    state_block = lax.dynamic_slice_in_dim(state, tp_index * local, local, 1)
    rate_block = lax.dynamic_slice_in_dim(attn_rate, tp_index * local, local, 0)
    mixed = share_unit(state_block + rate_block * (share_unit(attn_block) - state_block))
    mixed_in = lax.all_gather(mixed.astype(jnp.bfloat16), "tp", axis=1, tiled=True)
    gate_up = fold_rows(mixed_in, lax.all_gather(gate_up_norm, ("rep", "cp"), axis=0, tiled=True))
    up_branch = gate_up[:, :hidden_local] * up_scale
    gate_branch = gate_up[:, hidden_local:] * gate_scale * math.sqrt(D)
    inner = (up_branch * jax.nn.silu(gate_branch)).astype(jnp.bfloat16)
    mlp_part = right_product(inner, lax.all_gather(down_norm, ("rep", "cp"), axis=1, tiled=True))
    mlp_block = lax.psum_scatter(mlp_part, "tp", scatter_dimension=1, tiled=True)
    mlp_rate_block = lax.dynamic_slice_in_dim(mlp_rate, tp_index * local, local, 0)
    result = math.sqrt(D) * share_unit(mixed + mlp_rate_block * (share_unit(mlp_block) - mixed))
    return result.astype(jnp.bfloat16)[None]

MESH = pl.DeviceIdType.MESH
PARTS = 5
SWAPPED = (2, 4)
BACK = 512
NT = (((1,), (1,)), ((), ()))


def column_scale(block_ref, shards):
    def add(i, total):
        piece = block_ref[i].astype(jnp.float32)
        return total + jnp.sum(piece * piece, axis=0, keepdims=True)

    zero = jnp.zeros((1, block_ref.shape[-1]), jnp.float32)
    return lax.rsqrt(lax.fori_loop(0, shards, add, zero) + EPS)


def fused_kernel(
    reps, tps, cps,
    tok_all, qkv_all, outs_all, gu_all, down_all, vec_ref,
    out_ref,
    tok_raw, qkv_raw, outs_raw, gu_raw, down_raw, load, table_ref, tok, xt, wa, wb, wo, csa, q_s, kv, near, far, xm, mix, macc, kept_part, near2, far2, obuf, fin,
    tok_send, tok_recv, w_send_z, w_send_y, w_recv, kv_send, kv_recv,
    a_send, a_recv, m_send, m_recv, b_send, b_recv, o_send, o_recv,
):
    r, t, c = lax.axis_index("rep"), lax.axis_index("tp"), lax.axis_index("cp")
    shards = reps * cps
    tile = xt.shape[1]
    width = xt.shape[2]
    local = tok.shape[2]
    heads = local // HD
    depth = wa.shape[1]
    hid = wb.shape[3] // 3
    mine = r * cps + c
    hidden = PARTS * hid
    tok_ref = tok.at[t]
    beside = t + 1 - 2 * lax.rem(t, 2)
    across = lax.rem(t + 2, tps)
    diagonal = lax.rem(beside + 2, tps)

    def tp_peer(d):
        return lax.rem(t + d, tps)

    def cp_peer(d):
        return lax.rem(c + d, cps)

    def rep_peer(d):
        return lax.rem(r + d, reps)

    loads = [
        pltpu.make_async_copy(source, place, load.at[i])
        for i, (source, place) in enumerate(
            [(qkv_all, qkv_raw), (outs_all, outs_raw), (tok_all, tok_raw), (gu_all, gu_raw), (down_all, down_raw)]
        )
    ]
    for copy in loads:
        copy.start()
    barrier = pltpu.get_barrier_semaphore()
    for d in range(1, tps):
        pl.semaphore_signal(barrier, inc=1, device_id=(r, tp_peer(d), c), device_id_type=MESH)
    for d in range(1, cps):
        pl.semaphore_signal(barrier, inc=1, device_id=(r, t, cp_peer(d)), device_id_type=MESH)
    for d in range(1, reps):
        pl.semaphore_signal(barrier, inc=1, device_id=(rep_peer(d), t, c), device_id_type=MESH)
    pl.semaphore_wait(barrier, tps + cps + reps - 3)

    def remote(src, dst, send, recv, device):
        return pltpu.make_async_remote_copy(
            src_ref=src, dst_ref=dst, send_sem=send, recv_sem=recv, device_id=device, device_id_type=MESH
        )

    def slot(j, s):
        return wa.at[s] if j is None else wb.at[j, s]

    def near_cp(k):
        if k == 1:
            return c + 1 - 2 * lax.rem(c, 2)
        return jnp.where(c < 2, k, 3 - k)

    inner_cp = (c == 1) | (c == 2)

    def row(j):
        return 0 if j is None else j + 1

    def z_copy(j, k):
        part = slot(j, mine)
        return remote(part, part, w_send_z.at[row(j), k], w_recv.at[row(j), mine], (r, t, near_cp(k)))

    def z_relay(j):
        s = r * cps + near_cp(3)
        part = slot(j, s)
        return remote(part, part, w_send_z.at[row(j), 0], w_recv.at[row(j), s], (r, t, near_cp(1)))

    def y_copy(j, k, d):
        s = mine if k == 0 else r * cps + near_cp(k)
        part = slot(j, s)
        return remote(part, part, w_send_y.at[row(j), k, d], w_recv.at[row(j), s], (rep_peer(d), t, c))

    def arrive(j, s):
        part = slot(j, s)
        remote(part, part, w_send_z.at[row(j), 0], w_recv.at[row(j), s], (r, t, near_cp(1))).wait_recv()

    def swap_copy(j):
        s = rep_peer(1) * cps + c
        part = slot(j, s)
        return remote(part, part, w_send_y.at[row(j), 1, 0], w_recv.at[row(j), s], (r, t, near_cp(1)))

    def send_y(j):
        for d in range(1, reps):
            y_copy(j, 0, d).start()

    def send_z(j):
        z_copy(j, 1).start()
        z_copy(j, 2).start()
        if j in SWAPPED:
            z_copy(j, 3).start()
        else:

            @pl.when(inner_cp)
            def _():
                z_copy(j, 3).start()

    def comm_part(j):
        if j in SWAPPED:
            arrive(j, rep_peer(1) * cps + c)
            swap_copy(j).start()
        for k in range(1, cps):
            arrive(j, r * cps + near_cp(k))
            if k == 3 and j not in SWAPPED:

                @pl.when(inner_cp)
                def _():
                    z_relay(j).start()

            if k > 1 or j not in SWAPPED:
                for d in range(1, reps):
                    y_copy(j, k, d).start()

    def finish_part(j):
        for d in range(1, reps):
            for k in range(1, cps):
                arrive(j, rep_peer(d) * cps + cp_peer(k))

            if j is None:
                arrive(j, rep_peer(d) * cps + c)
            else:

                @pl.when(functools.reduce(lambda a, b: a & b, [j != q for q in SWAPPED]))
                def _():
                    arrive(j, rep_peer(d) * cps + c)

    def drain(j):
        z_copy(j, 1).wait_send()
        z_copy(j, 2).wait_send()

        if j in SWAPPED:
            z_copy(j, 3).wait_send()
        else:

            @pl.when(inner_cp)
            def _():
                z_copy(j, 3).wait_send()
                z_relay(j).wait_send()

        for d in range(1, reps):
            for k in range(cps):
                if k == 1 and j in SWAPPED:
                    swap_copy(j).wait_send()
                else:
                    y_copy(j, k, d).wait_send()

    def tok_copy(d):
        return remote(tok_ref, tok.at[t], tok_send.at[d], tok_recv.at[t], (r, tp_peer(d), c))

    loads[0].wait()
    loads[1].wait()
    for kind in range(3):
        wa[mine, :, kind * local : (kind + 1) * local] = qkv_raw[kind].astype(jnp.bfloat16)
    wa[mine, :, 3 * local :] = outs_raw[...].astype(jnp.bfloat16)
    send_y(None)
    send_z(None)
    loads[2].wait()
    tok[t] = tok_raw[...].astype(jnp.float32).T.astype(jnp.bfloat16)
    for d in range(1, tps):
        tok_copy(d).start()
    loads[3].wait()
    loads[4].wait()
    for j in range(PARTS):
        wb[j, mine, :, :hid] = gu_raw[:, 0, j * hid : (j + 1) * hid].astype(jnp.bfloat16)
        wb[j, mine, :, hid : 2 * hid] = gu_raw[:, 1, j * hid : (j + 1) * hid].astype(jnp.bfloat16)
        wb[j, mine, :, 2 * hid :] = down_raw[:, j * hid : (j + 1) * hid].astype(jnp.bfloat16)

    segments_at = 2 * width + 2 * hidden
    rates_at = segments_at + kv.shape[0]
    qks_at = rates_at + 2 * HD
    window = BACK + tile
    for i in range(tps):
        begin = segments_at + i * tile
        key_ids = vec_ref[:, begin : begin + window]
        square = (tile, tile)
        diagonal_only = lax.broadcasted_iota(jnp.int32, square, 0) == lax.broadcasted_iota(jnp.int32, square, 1)
        own_ids = jnp.sum(jnp.where(diagonal_only, key_ids[:, BACK:], 0.0), axis=1, keepdims=True)
        column = lax.broadcasted_iota(jnp.int32, (tile, window), 1)
        line = lax.broadcasted_iota(jnp.int32, (tile, window), 0) + BACK
        earlier = (key_ids == own_ids) & (column < line)
        position = jnp.sum(jnp.where(earlier, 1.0, 0.0), axis=1, keepdims=True)
        angles = position * vec_ref[:, rates_at : rates_at + HD]
        left = lax.broadcasted_iota(jnp.int32, (tile, HD), 1) < HD // 2
        sine = jnp.sin(angles)
        begins = lax.broadcasted_iota(jnp.int32, (tile, 2 * HD), 0).astype(jnp.float32) + BACK - position
        table_ref[i] = jnp.concatenate([jnp.cos(angles), jnp.where(left, -sine, sine), begins], axis=1)

    comm_part(None)
    send_z(0)
    for j in range(3):
        send_y(j)
    for d in range(1, tps):
        s = tp_peer(d)
        remote(tok_ref, tok.at[s], tok_send.at[d], tok_recv.at[s], (r, s, c)).wait_recv()
    finish_part(None)
    csa[...] = column_scale(wa, shards)
    wo[...] = wa[:, :, 3 * local :].reshape(width, local)
    comm_part(0)

    rows_all = kv.shape[0]

    kv_pieces = -(-BACK // tile)

    def kv_copy(piece):
        count = min(tile, BACK - piece * tile)
        taken = piece * tile + count
        return remote(
            kv.at[pl.ds(rows_all - taken, count)],
            kv.at[pl.ds(BACK - taken, count)],
            kv_send.at[piece],
            kv_recv.at[piece],
            (r, t, cp_peer(1)),
        )

    def project(step, carry):
        i = tps - 1 - step
        rows = pl.ds(pl.multiple_of(i * tile, 64), tile)
        x = jnp.concatenate([tok[s, rows, :] for s in range(tps)], axis=1)
        xt[i] = x
        xf = x.astype(jnp.float32)
        inv = lax.rsqrt(jnp.sum(xf * xf, axis=1, keepdims=True) + EPS)
        weights = wa[:, :, : 3 * local].reshape(width, 3 * local)
        pr = jnp.dot(x, weights, preferred_element_type=jnp.float32) * inv * csa[:, : 3 * local]
        cosine, sine = table_ref[i, :, :HD], table_ref[i, :, HD : 2 * HD]

        def rope(base, factor):
            pieces = []
            for h in range(heads):
                v = pr[:, base + HD * h : base + HD * (h + 1)]
                v = v * lax.rsqrt(jnp.sum(v * v, axis=1, keepdims=True) + EPS)
                v = v * (vec_ref[:, qks_at + HD * h : qks_at + HD * (h + 1)] * factor)
                swapped = jnp.concatenate([v[:, HD // 2 :], v[:, : HD // 2]], axis=1)
                pieces.append(v * cosine + swapped * sine)
            return jnp.concatenate(pieces, axis=1)

        q_s[i] = rope(0, math.sqrt(HD)).astype(jnp.bfloat16)
        kv[pl.ds(pl.multiple_of(BACK + i * tile, 64), tile), :] = jnp.concatenate(
            [rope(local, 1.0), pr[:, 2 * local :]], axis=1
        ).astype(jnp.bfloat16)

        for piece in range(kv_pieces):

            @pl.when((step == piece) & (c < cps - 1))
            def _():
                kv_copy(piece).start()

        @pl.when(step == kv_pieces - 1)
        def _():
            send_z(1)
            send_y(3)
            send_y(4)

        return carry

    @pl.when(c == 0)
    def _():
        kv[pl.ds(0, BACK), :] = jnp.zeros((BACK, kv.shape[1]), kv.dtype)

    lax.fori_loop(0, tps, project, 0)

    @pl.when(c > 0)
    def _():
        for piece in range(kv_pieces):
            kv_copy(piece).wait_recv()

    send_z(2)

    def near_copy(buf, k, send, recv):
        return remote(buf.at[k], buf.at[2 + k], send.at[k], recv.at[k], (r, beside, c))

    def far_copy(buf, send, recv):
        return remote(buf.at[0], buf.at[1], send.at[2], recv.at[2], (r, across, c))

    def scatter_step(step, part, kept, buf_near, buf_far, send, recv):
        @pl.when(step == 0)
        def _():
            buf_near[0] = part.astype(jnp.bfloat16)
            near_copy(buf_near, 0, send, recv).start()

        @pl.when(step == 1)
        def _():
            near_copy(buf_near, 0, send, recv).wait_recv()
            buf_far[0] = (part + buf_near[2].astype(jnp.float32)).astype(jnp.bfloat16)
            far_copy(buf_far, send, recv).start()

        @pl.when(step == 2)
        def _():
            buf_near[1] = part.astype(jnp.bfloat16)
            near_copy(buf_near, 1, send, recv).start()

        @pl.when(step == 3)
        def _():
            kept[...] = part

    def scatter_total(kept, buf_near, buf_far, send, recv):
        near_copy(buf_near, 1, send, recv).wait_recv()
        far_copy(buf_far, send, recv).wait_recv()
        return kept[...] + buf_near[3].astype(jnp.float32) + buf_far[1].astype(jnp.float32)

    def scatter_drain(buf_near, buf_far, send, recv):
        near_copy(buf_near, 0, send, recv).wait_send()
        near_copy(buf_near, 1, send, recv).wait_send()
        far_copy(buf_far, send, recv).wait_send()

    def target(step):
        late = jnp.where(step == 2, beside, t)
        return jnp.where(step == 0, diagonal, jnp.where(step == 1, across, late))

    def attend(step, carry):
        i = target(step)
        first = pl.ds(pl.multiple_of(i * tile, 64), window)
        column = lax.broadcasted_iota(jnp.int32, (tile, window), 1)
        line = lax.broadcasted_iota(jnp.int32, (tile, window), 0) + BACK
        allowed = (column <= line) & (column >= table_ref[i, :, 2 * HD : 2 * HD + 1].astype(jnp.int32))
        qt = q_s[i]
        outs = []
        for h in range(heads):
            keys = kv[first, HD * h : HD * (h + 1)]
            values = kv[first, local + HD * h : local + HD * (h + 1)]
            scores = lax.dot_general(
                qt[:, HD * h : HD * (h + 1)], keys, NT, preferred_element_type=jnp.float32
            )
            scores = jnp.where(allowed, scores, -1e30)
            exponent = jnp.exp(scores - jnp.max(scores, axis=1, keepdims=True))
            total = jnp.sum(exponent, axis=1, keepdims=True)
            got = jnp.dot(exponent.astype(jnp.bfloat16), values, preferred_element_type=jnp.float32)
            outs.append(got / total)
        att = (jnp.concatenate(outs, axis=1) * csa[:, 3 * local :]).astype(jnp.bfloat16)
        part = lax.dot_general(att, wo[...], NT, preferred_element_type=jnp.float32)
        scatter_step(step, part, mix, near, far, a_send, a_recv)

        @pl.when(step == 0)
        def _():
            send_z(3)

        @pl.when(step == 1)
        def _():
            send_z(4)

        @pl.when(step == 2)
        def _():
            comm_part(1)

        return carry

    lax.fori_loop(0, tps, attend, 0)
    comm_part(2)

    def unit(v):
        return v * lax.rsqrt(jnp.sum(v * v, axis=1, keepdims=True) + EPS)

    attn = unit(scatter_total(mix, near, far, a_send, a_recv))
    state = unit(xt[t].astype(jnp.float32))
    mixed = unit(state + vec_ref[:, :width] * (attn - state))
    mix[...] = mixed
    xm[t] = mixed.astype(jnp.bfloat16)

    def mix_copy(k, s, device):
        return remote(xm.at[s], xm.at[s], m_send.at[k], m_recv.at[s], (r, device, c))

    mix_copy(0, t, across).start()
    mix_copy(1, t, beside).start()
    macc[...] = jnp.zeros_like(macc)
    mix_copy(0, across, across).wait_recv()
    mix_copy(2, across, beside).start()
    comm_part(3)
    mix_copy(1, beside, beside).wait_recv()
    mix_copy(2, diagonal, beside).wait_recv()

    def scales(j):
        cs = column_scale(wb.at[j], shards)
        mine_up = pl.ds(pl.multiple_of(2 * width + j * hid, 128), hid)
        mine_gate = pl.ds(pl.multiple_of(2 * width + hidden + j * hid, 128), hid)
        up_by = cs[:, :hid] * vec_ref[:, mine_up]
        gate_by = cs[:, hid : 2 * hid] * vec_ref[:, mine_gate] * math.sqrt(width)
        return up_by, gate_by, cs[:, 2 * hid :]

    def feed(x, j, by):
        gu = jnp.dot(x, wb[j, :, :, : 2 * hid].reshape(width, 2 * hid), preferred_element_type=jnp.float32)
        up = gu[:, :hid] * by[0]
        gate = gu[:, hid:] * by[1]
        inner = (up * (gate / (1.0 + jnp.exp(-gate))) * by[2]).astype(jnp.bfloat16)
        return lax.dot_general(
            inner, wb[j, :, :, 2 * hid :].reshape(width, hid), NT, preferred_element_type=jnp.float32
        )

    def feed_part(j, carry):
        finish_part(j)
        by = scales(j)

        def pair(i, inner_carry):
            both = pl.ds(2 * i, 2)
            part = feed(xm[both].reshape(2 * tile, width), j, by)
            macc[both] = macc[both] + part.reshape(2, tile, width)
            return inner_carry

        lax.fori_loop(0, tps // 2, pair, 0)

        @pl.when(j == 0)
        def _():
            comm_part(4)

        return carry

    lax.fori_loop(0, PARTS - 1, feed_part, 0)
    finish_part(PARTS - 1)
    last_by = scales(PARTS - 1)

    def feed_last(step, carry):
        p = target(step)
        part = macc[p] + feed(xm[p], PARTS - 1, last_by)
        scatter_step(step, part, kept_part, near2, far2, b_send, b_recv)
        return carry

    lax.fori_loop(0, tps, feed_last, 0)
    mlp = unit(scatter_total(kept_part, near2, far2, b_send, b_recv))
    kept = mix[...]
    final = (math.sqrt(width) * unit(kept + vec_ref[:, width : 2 * width] * (mlp - kept))).astype(jnp.bfloat16)
    for p in range(tps):
        obuf[p] = final[:, local * p : local * (p + 1)]

    def out_copy(p):
        return remote(obuf.at[p], fin.at[t], o_send.at[p], o_recv.at[t], (r, p, c))

    for d in range(1, tps):
        out_copy(tp_peer(d)).start()
    fin[t] = obuf[t]
    for d in range(1, tps):
        s = tp_peer(d)
        remote(obuf.at[t], fin.at[s], o_send.at[t], o_recv.at[s], (r, s, c)).wait_recv()
    whole = jnp.concatenate([fin[s] for s in range(tps)], axis=0)
    out_ref[...] = whole.astype(jnp.float32).T.astype(jnp.bfloat16)

    drain(None)

    for j in range(PARTS):
        drain(j)

    for d in range(1, tps):
        p = tp_peer(d)
        tok_copy(d).wait_send()
        out_copy(p).wait_send()

    scatter_drain(near, far, a_send, a_recv)
    scatter_drain(near2, far2, b_send, b_recv)
    mix_copy(0, t, across).wait_send()
    mix_copy(1, t, beside).wait_send()
    mix_copy(2, across, beside).wait_send()

    @pl.when(c < cps - 1)
    def _():
        for piece in range(kv_pieces):
            kv_copy(piece).wait_send()


def fused_body(
    tokens, qkv_weight, out_weight, gate_up_weight, down_weight, qk_scale,
    attn_rate, mlp_rate, up_scale, gate_scale, segment_ids,
):
    reps, tps, cps = lax.axis_size("rep"), lax.axis_size("tp"), lax.axis_size("cp")
    rows, local = tokens.shape[1], tokens.shape[2]
    depth = qkv_weight.shape[0]
    hidden = gate_up_weight.shape[2]
    hid = hidden // PARTS
    shards = reps * cps
    width = depth * shards
    tile = rows // tps
    bf16 = jnp.bfloat16
    cp = lax.axis_index("cp")
    padded = jnp.concatenate([jnp.full((BACK,), -1.0, jnp.float32), segment_ids[0].astype(jnp.float32)])
    window = lax.dynamic_slice_in_dim(padded, cp * rows, BACK + rows)
    half = HD // 2
    frequency = jnp.exp(-math.log(10000.0) * jnp.arange(half, dtype=jnp.float32) * 2.0 / HD)
    vectors = jnp.concatenate(
        [attn_rate, mlp_rate, up_scale, gate_scale, window, frequency, frequency, frequency, frequency, qk_scale]
    )[None]
    vmem = pl.BlockSpec(memory_space=pltpu.VMEM)
    hbm = pl.BlockSpec(memory_space=pl.ANY)
    dma = pltpu.SemaphoreType.DMA
    f32 = jnp.float32
    flops = 2 * rows * width * (4 * local + 3 * hidden) + 4 * rows * (BACK + tile) * local
    out = pl.pallas_call(
        lambda *refs: fused_kernel(reps, tps, cps, *refs),
        out_shape=jax.ShapeDtypeStruct((local, rows), bf16),
        in_specs=[hbm] * 5 + [vmem],
        out_specs=vmem,
        scratch_shapes=[
            pltpu.VMEM((local, rows), bf16),
            pltpu.VMEM((3, depth, local), f32),
            pltpu.VMEM((depth, local), f32),
            pltpu.VMEM((depth, 2, hidden), f32),
            pltpu.VMEM((depth, hidden), f32),
            dma((5,)),
            pltpu.VMEM((tps, tile, 4 * HD), f32),
            pltpu.VMEM((tps, rows, local), bf16),
            pltpu.VMEM((tps, tile, width), bf16),
            pltpu.VMEM((shards, depth, 4 * local), bf16),
            pltpu.VMEM((PARTS, shards, depth, 3 * hid), bf16),
            pltpu.VMEM((width, local), bf16),
            pltpu.VMEM((1, 4 * local), f32),
            pltpu.VMEM((tps, tile, local), bf16),
            pltpu.VMEM((BACK + rows, 2 * local), bf16),
            pltpu.VMEM((4, tile, width), bf16),
            pltpu.VMEM((2, tile, width), bf16),
            pltpu.VMEM((tps, tile, width), bf16),
            pltpu.VMEM((tile, width), f32),
            pltpu.VMEM((tps, tile, width), f32),
            pltpu.VMEM((tile, width), f32),
            pltpu.VMEM((4, tile, width), bf16),
            pltpu.VMEM((2, tile, width), bf16),
            pltpu.VMEM((tps, tile, local), bf16),
            pltpu.VMEM((tps, tile, local), bf16),
            dma((tps,)), dma((tps,)),
            dma((PARTS + 1, cps)), dma((PARTS + 1, cps, reps)), dma((PARTS + 1, shards)),
            dma((-(-BACK // tile),)), dma((-(-BACK // tile),)),
            dma((tps,)), dma((tps,)), dma((tps,)), dma((tps,)),
            dma((tps,)), dma((tps,)), dma((tps,)), dma((tps,)),
        ],
        compiler_params=pltpu.CompilerParams(
            collective_id=0, has_side_effects=True, vmem_limit_bytes=58 * 1024 * 1024
        ),
        cost_estimate=pl.CostEstimate(flops=flops, bytes_accessed=2 * width * 5120, transcendentals=0),
    )(
        tokens[0].T, qkv_weight.transpose(1, 0, 2), out_weight.T, gate_up_weight, down_weight.T, vectors
    )
    return out.T[None]


def body(*arrays):
    depth, tile = arrays[1].shape[0], arrays[0].shape[1] // lax.axis_size("tp")
    aligned = lax.axis_size("tp") == 4 and lax.axis_size("cp") == 4 and lax.axis_size("rep") == 2 and depth % 16 == 0 and tile % 64 == 0 and arrays[3].shape[2] % (128 * PARTS) == 0
    return fused_body(*arrays) if aligned else plain_body(*arrays)


def solution(mesh):
    in_specs = (
        P("rep", "cp", "tp"),
        P(("rep", "cp"), None, "tp"),
        P("tp", ("rep", "cp")),
        P(("rep", "cp"), None, "tp"),
        P("tp", ("rep", "cp")),
        P("tp"),
        P(),
        P(),
        P("tp"),
        P("tp"),
        P("rep", None),
    )
    out_specs = P("rep", "cp", "tp")
    return jax.shard_map(body, mesh=mesh, in_specs=in_specs, out_specs=out_specs, check_vma=False)
```
